512 devices in a mesh: lat: 32 (over z, core), lon: 16 (over x, y).
Axes of the slice: x: 4, y: 4, z: 16, core: 2. Of those that a mesh axis runs over, the one named last changes fastest.
Arguments:
- state: float32 [6, 1, 512, 5760], P(None, None, 'lat', 'lon'), may hold values from -6 to 6
- zonal_wind: float32 [1, 512, 5760], P(None, 'lat', 'lon'), may hold values from -6 to 6
- meridional_wind: float32 [1, 512, 5760], P(None, 'lat', 'lon'), may hold values from -6 to 6
- filter_flag: int32 [512], replicated, may hold values from 0 to 1, as said below
- mode_count: int32 [512], replicated, may hold values from 0 to 360, as said below
Outputs:
- advanced: float32 [6, 1, 512, 5760], P(None, None, 'lat', 'lon')
The draws below stay inside these ranges and needn't reach their ends.
Inputs may be any that keep to these rules, and one draw needn't show every extreme that they name: `filter_flag`: 0 outside the 128 latitudes nearest each pole; 1 at the latitude nearest each pole. `mode_count`: 0 outside the 128 latitudes nearest each pole, 1 or more inside them, 360 at the latitude nearest each pole.
All inputs are finite; a program needn't handle non-finite values.
Results may differ from the reference program's by a relative error of at most 0.00005.
Values sent between devices are 32-bit elements; how exact they have to be, the bound alone decides.
No kernel may reach another device: no remote copies, remote signals or barrier semaphores. Data moves between devices by JAX's collectives and lax.ppermute only.
A program may use at most 64 MiB of HBM per device.

```python
import math
import jax
import jax.numpy as jnp
from jax import lax

F = 6
LEV = 1
NLAT = 512
NLON = 5760
KMAX = 360
POLAR = 128


def draw_filter_flag(key, part):
    key = jax.random.fold_in(key, 3)
    latitudes = jnp.arange(NLAT, dtype=jnp.int32)
    pole_gap = jnp.minimum(latitudes, NLAT - 1 - latitudes)
    coin = jax.random.randint(key, (NLAT,), 0, 4)
    chosen = (pole_gap < POLAR) & ((coin > 0) | (pole_gap == 0))
    return jnp.where(chosen, 1, 0).astype(jnp.int32)


def draw_mode_count(key, part):
    key = jax.random.fold_in(key, 11)
    latitudes = jnp.arange(NLAT, dtype=jnp.int32)
    pole_gap = jnp.minimum(latitudes, NLAT - 1 - latitudes)
    counts = jax.random.randint(key, (NLAT,), 1, KMAX + 1)
    counts = jnp.where(pole_gap == 0, KMAX, counts)
    return jnp.where(pole_gap < POLAR, counts, 0).astype(jnp.int32)


def block_levels(own_key, dims, shards, smallest, largest):
    loudness = 1.0
    for dim, shards_of in shards:
        steps = jax.random.uniform(jax.random.fold_in(jax.random.fold_in(own_key, 6), dim), (shards_of,), jnp.float32, smallest / len(shards), largest / len(shards))
        loudness = loudness * jnp.repeat(jnp.exp(steps), dims[dim] // shards_of).reshape((-1,) + (1,) * (len(dims) - 1 - dim))
    return loudness


def scatter_about(rng, shape, scale, bound, shards=(), held_as=jnp.bfloat16):
    result = jax.random.normal(rng, shape, jnp.float32) * scale
    if len(shards) > 0:
        result = block_levels(rng, shape, shards, -0.22, 0.18) * result
    return jnp.clip(result, min=-bound, max=bound).astype(held_as)


def setup_inputs(seed: int = 0) -> dict:
    splits = jax.random.split(jax.random.key(seed), 6)
    state = scatter_about(splits[0], (F, LEV, NLAT, NLON), 1.0, 6.0, ((2, 32), (3, 16)), jnp.float32)
    zonal_wind = scatter_about(splits[1], (LEV, NLAT, NLON), 1.0, 6.0, ((1, 32), (2, 16)), jnp.float32)
    meridional_wind = scatter_about(splits[2], (LEV, NLAT, NLON), 1.0, 6.0, ((1, 32), (2, 16)), jnp.float32)
    filter_flag = draw_filter_flag(jax.random.fold_in(splits[5], 71), 0)
    mode_count = draw_mode_count(jax.random.fold_in(splits[5], 71), 0)
    return {"state": state, "zonal_wind": zonal_wind, "meridional_wind": meridional_wind, "filter_flag": filter_flag, "mode_count": mode_count}


meridional_scale = 0.25


def reference(state, zonal_wind, meridional_wind, filter_flag, mode_count):
    center_angle = (jnp.arange(NLAT, dtype=jnp.float32) + 0.5) * (math.pi / NLAT) - math.pi / 2
    center_metric = jnp.cos(center_angle)
    face_metric = jnp.sin((jnp.arange(NLAT, dtype=jnp.float32) + 1.0) * (math.pi / NLAT))
    zonal_scale = math.sin(math.pi / (2 * NLAT))
    half_length = NLON // 2
    wavenumbers = jnp.arange(half_length + 1, dtype=jnp.int32)
    ranks = wavenumbers - (half_length - KMAX)
    inside = (ranks >= 0) & (ranks < KMAX)
    raised = jnp.maximum(ranks[None, :] - KMAX + mode_count[:, None] + 1, 0)
    damping = raised.astype(jnp.float32) / jnp.maximum(mode_count[:, None].astype(jnp.float32), 1.0)
    damping = jnp.where(inside[None, :], damping, 0.0) * filter_flag[:, None].astype(jnp.float32)
    keep_factor = 1.0 - damping

    def one_field(field):
        east = jnp.roll(field, -1, axis=2)
        flux_east = zonal_wind * (0.5 * (field + east))
        zonal_diff = flux_east - jnp.roll(flux_east, 1, axis=2)
        zero_row = jnp.zeros_like(field[:, :1, :])
        north = jnp.concatenate([field[:, 1:, :], zero_row], axis=1)
        flux_north = (meridional_wind * face_metric[:, None]) * (0.5 * (field + north))
        flux_south = jnp.concatenate([zero_row, flux_north[:, :-1, :]], axis=1)
        merid_diff = flux_north - flux_south
        increment = -(zonal_scale / center_metric)[:, None] * zonal_diff - (meridional_scale / center_metric)[:, None] * merid_diff
        spectrum = jnp.fft.rfft(increment, axis=-1)
        filtered = jnp.fft.irfft(spectrum * keep_factor[None, :, :], n=NLON, axis=-1).astype(field.dtype)
        return field + filtered

    return lax.map(one_field, state)
```

```python
import math

import jax
import jax.numpy as jnp
import ml_dtypes
import numpy as np
from jax import lax
from jax.experimental import pallas as pl
from jax.experimental.pallas import tpu as pltpu
from jax.sharding import PartitionSpec as P

meridional_scale = 0.25
SLABS = 3
SLAB = 120
POINTS = 48
ROWS = 8 * SLABS
GROUPS = 3


def mode_layout(circle, kmax):
    table = np.zeros((GROUPS, 256, 256), np.float64)
    reduced = np.full((GROUPS, 256), 1 << 20, np.int32)
    scale = np.zeros((GROUPS, 256), np.float64)
    b = np.arange(SLAB)
    sign = np.where(b % 2 == 0, 1.0, -1.0)
    for residue in range(POINTS // 2):
        group, place = divmod(residue, 8)
        if residue == 0:
            waves = [(48 * n, 0) for n in range(1, 8)] + [(24 + 48 * n, 128) for n in range(8)]
            factor = 2.0 / circle
        else:
            waves = [(residue + 48 * n, None) for n in range(-8, 8) if abs(residue + 48 * n) <= kmax]
            factor = 1.0 / circle
        for t, (k, row) in enumerate(waves):
            angle = 2.0 * np.pi * ((k * b) % circle) / circle
            cosine, sine = sign * np.cos(angle), sign * np.sin(angle)
            re, im = 32 * place + t, 32 * place + 16 + t
            if row is None:
                table[group, :SLAB, re], table[group, 128 : 128 + SLAB, re] = cosine, sine
                table[group, :SLAB, im], table[group, 128 : 128 + SLAB, im] = -sine, cosine
            else:
                table[group, row : row + SLAB, re] = cosine
                table[group, row : row + SLAB, im] = -sine
            reduced[group, [re, im]] = abs(k)
            scale[group, [re, im]] = factor
    high = table.astype(np.float32).astype(ml_dtypes.bfloat16)
    low = (table - high.astype(np.float64)).astype(np.float32).astype(ml_dtypes.bfloat16)
    return high, low, reduced, scale.astype(np.float32)


def c_add(x, y):
    return (x[0] + y[0], y[1] if x[1] is None else x[1] if y[1] is None else x[1] + y[1])


def c_sub(x, y):
    if y[1] is None:
        return (x[0] - y[0], x[1])
    return (x[0] - y[0], -y[1] if x[1] is None else x[1] - y[1])


def c_conj(x):
    return (x[0], None if x[1] is None else -x[1])


def c_turn(x, numer, denom):
    numer %= denom
    eighth = 8 * numer
    if numer == 0:
        return x
    if 2 * numer == denom:
        return (-x[0], None if x[1] is None else -x[1])
    if 4 * numer == denom:
        return (jnp.zeros_like(x[0]) if x[1] is None else -x[1], x[0])
    if 4 * numer == 3 * denom:
        return (jnp.zeros_like(x[0]) if x[1] is None else x[1], -x[0])
    angle = 2.0 * math.pi * numer / denom
    c, s = math.cos(angle), math.sin(angle)
    if x[1] is None:
        return (x[0] * c, x[0] * s)
    if eighth in (denom, 3 * denom, 5 * denom, 7 * denom):
        h = math.sqrt(0.5)
        a, b = (x[0] - x[1]) * h, (x[0] + x[1]) * h
        return {1: (a, b), 3: (-b, a), 5: (-a, -b), 7: (b, -a)}[eighth // denom]
    return (x[0] * c - x[1] * s, x[0] * s + x[1] * c)


def rfft(x):
    count = len(x)
    if count == 1:
        return [(x[0], None)]
    if count == 2:
        return [(x[0] + x[1], None), (x[0] - x[1], None)]
    even, odd = rfft(x[0::2]), rfft(x[1::2])
    result = [None] * (count // 2 + 1)
    for k in range(count // 4 + 1):
        turned = c_turn(odd[k], -k, count)
        result[k] = c_add(even[k], turned)
        if k != count // 4 or count == 2:
            result[count // 2 - k] = c_conj(c_sub(even[k], turned))
    return result


def irfft(z):
    count = 2 * (len(z) - 1)
    if count == 2:
        return [z[0][0] + z[1][0], z[0][0] - z[1][0]]
    even, odd = [], []
    for k in range(count // 4 + 1):
        mirror = c_conj(z[count // 2 - k])
        even.append(c_add(z[k], mirror))
        odd.append(c_turn(c_sub(z[k], mirror), k, count))
    result = [None] * count
    result[0::2], result[1::2] = irfft(even), irfft(odd)
    return result


def circle_forward(x):
    parts = [rfft(x[a::3]) for a in range(3)]
    result = [None] * 25
    half, root = 0.5, math.sqrt(3.0) / 2.0
    for k in range(9):
        t0 = parts[0][k]
        t1, t2 = c_turn(parts[1][k], -k, 48), c_turn(parts[2][k], -2 * k, 48)
        total, gap = c_add(t1, t2), c_sub(t1, t2)
        result[k] = c_add(t0, total)
        mid = (t0[0] - half * total[0], None if t0[1] is None and total[1] is None else
               (t0[1] if total[1] is None else (0.0 if t0[1] is None else t0[1]) - half * total[1]))
        turn = (None if gap[1] is None else root * gap[1], -root * gap[0])
        plus_re = mid[0] if turn[0] is None else mid[0] + turn[0]
        plus_im = turn[1] if mid[1] is None else mid[1] + turn[1]
        minus_re = mid[0] if turn[0] is None else mid[0] - turn[0]
        minus_im = -turn[1] if mid[1] is None else mid[1] - turn[1]
        if k + 16 <= 24:
            result[k + 16] = (plus_re, plus_im)
        if k > 0 and 16 - k != k + 16 and result[16 - k] is None:
            result[16 - k] = (minus_re, -minus_im)
    return result


def circle_backward(z):
    half, root = 0.5, math.sqrt(3.0) / 2.0
    spectra = [[], [], []]
    for k in range(9):
        t0 = z[k]
        t1 = z[k + 16] if k + 16 <= 24 else c_conj(z[32 - k])
        t2 = c_conj(z[16 - k])
        total, gap = c_add(t1, t2), c_sub(t1, t2)
        if k == 0:
            total, gap = (2.0 * t1[0], None), (None, 2.0 * t1[1])
        spectra[0].append(c_add(t0, total))
        mid = (t0[0] - half * total[0],
               t0[1] if total[1] is None else (-half * total[1] if t0[1] is None else t0[1] - half * total[1]))
        turn = (-root * gap[1], None if gap[0] is None else root * gap[0])
        plus = c_add(mid, turn)
        minus = c_sub(mid, turn)
        spectra[1].append(c_turn(plus, k, 48))
        spectra[2].append(c_turn(minus, 2 * k, 48))
    result = [None] * 48
    for a in range(3):
        result[a::3] = irfft(spectra[a])
    return result


def increment_kernel(state, zonal, merid, south, north, metric, chunks, pad):
    fields, rows, cells = state.shape
    wide = 128 * SLABS
    for f in range(fields + 2):
        pad[f, :, wide - 128 :] = jnp.zeros((rows, 128), jnp.float32)
    for f in range(fields):
        pad[f, :, :cells] = state[f]
    pad[fields, :, :cells] = zonal[...]
    pad[fields + 1, :, :cells] = merid[...]
    lane = lax.broadcasted_iota(jnp.int32, (rows, wide), 1)
    row = lax.broadcasted_iota(jnp.int32, (rows, wide), 0)
    short = lane[:, :128]

    def spread(index):
        part = metric[index]
        return jnp.concatenate([part] * SLABS, axis=1)

    zonal_factor, merid_factor, face, face_before = (spread(i) for i in range(4))
    east_wind = pad[fields]
    last_wind = pltpu.roll(east_wind, 3, 1)
    inner_wind = jnp.where(lane < cells - 1, east_wind, 0.0)
    north_wind = pad[fields + 1] * face
    south_wind = south[fields : fields + 1, :] * face_before[0:1, :]
    for f in range(fields):
        q = pad[f]
        flux_east = inner_wind * (0.5 * (q + pltpu.roll(q, wide - 1, 1)))
        zonal_diff = flux_east - pltpu.roll(flux_east, 1, 1)
        q_north = jnp.where(row == rows - 1, north[f : f + 1, :], pltpu.roll(q, rows - 1, 0))
        flux_north = north_wind * (0.5 * (q + q_north))
        flux_first = south_wind * (0.5 * (south[f : f + 1, :] + q[0:1, :]))
        merid_diff = flux_north - jnp.where(row == 0, flux_first, pltpu.roll(flux_north, 1, 0))
        part = -zonal_factor * zonal_diff - merid_factor * merid_diff
        part = jnp.where(lane == cells, pltpu.roll(q, cells, 1), part)
        part = jnp.where(lane == cells + 1, pltpu.roll(q, 2, 1), part)
        part = jnp.where(lane == cells + 2, last_wind, part)
        v0, v1, v2 = part[:, :128], part[:, 128:256], part[:, 256:]
        slabs = (
            v0,
            jnp.where(short < 8, pltpu.roll(v0, 8, 1), pltpu.roll(v1, 8, 1)),
            jnp.where(short < 16, pltpu.roll(v1, 16, 1), pltpu.roll(v2, 16, 1)),
        )
        for a in range(SLABS):
            chunks[pl.ds(8 * a + f, rows, stride=ROWS), :] = slabs[a]
    for f in range(fields, 8):
        for a in range(SLABS):
            chunks[pl.ds(8 * a + f, rows, stride=ROWS), :] = jnp.zeros((rows, 128), jnp.float32)


def split(x):
    high = x.astype(jnp.bfloat16)
    return high, (x - high.astype(jnp.float32)).astype(jnp.bfloat16)


def product(x, high, low, dims):
    def dot(p, q):
        return lax.dot_general(p, q, (dims, ((), ())), preferred_element_type=jnp.float32)

    x_high, x_low = split(x)
    return dot(x_high, high) + (dot(x_low, high) + dot(x_high, low))


def filter_kernel(chunks, own, damping, high, low, result):
    sectors = chunks.shape[0]
    lane = lax.broadcasted_iota(jnp.int32, (8, 128), 1)
    zonal_factor = own[...]
    points = [chunks[p // 3, 8 * (p % 3) : 8 * (p % 3) + 8, :] for p in range(POINTS)]
    lasts = [points[3 * s + 2] for s in range(sectors)]
    for s in range(sectors):
        after = (s + 1) % sectors
        flux = pltpu.roll(lasts[s], 125, 1) * (
            0.5 * (pltpu.roll(lasts[s], 126, 1) + pltpu.roll(lasts[after], 127, 1))
        )
        edge = jnp.where(lane == SLAB - 1, zonal_factor * flux, 0.0)
        points[3 * s + 2] = points[3 * s + 2] - edge
        points[3 * after] = points[3 * after] + pltpu.roll(edge, 128 - (SLAB - 1), 1)
    for p in range(POINTS):
        result[p // 3, 8 * (p % 3) : 8 * (p % 3) + 8, :] = points[p]
    spectrum = circle_forward(points)
    spectrum[0] = (spectrum[0][0], spectrum[24][0])
    block = lax.broadcasted_iota(jnp.int32, (64, 256), 0) // 8
    column = lax.broadcasted_iota(jnp.int32, (64, 256), 1) // 32
    back = [None] * 25
    for g in range(GROUPS):
        rows = jnp.concatenate(
            [jnp.concatenate(spectrum[8 * g + i], axis=1) for i in range(8)], axis=0
        )
        modes = product(rows, high[g], low[g], ((1,), (0,)))
        modes = jnp.where(block == column, modes * damping[g : g + 1, :], 0.0)
        rows = product(modes, high[g], low[g], ((1,), (1,)))
        for i in range(8):
            part = rows[8 * i : 8 * i + 8, :]
            back[8 * g + i] = (part[:, :128], part[:, 128:])
    back[24] = (back[0][1], None)
    back[0] = (back[0][0], None)
    correction = circle_backward(back)
    for p in range(POINTS):
        place = (p // 3, slice(8 * (p % 3), 8 * (p % 3) + 8), slice(None))
        result[place] = result[place] - correction[p]


def final_kernel(chunks, state, advanced):
    fields, rows, cells = state.shape
    lane = lax.broadcasted_iota(jnp.int32, (rows, 128), 1)
    for f in range(fields):
        s0, s1, s2 = (chunks[pl.ds(8 * a + f, rows, stride=ROWS), :] for a in range(SLABS))
        s1, s2 = pltpu.roll(s1, 120, 1), pltpu.roll(s2, 112, 1)
        advanced[f, :, :128] = state[f, :, :128] + jnp.where(lane < 120, s0, s1)
        advanced[f, :, 128:256] = state[f, :, 128:256] + jnp.where(lane < 112, s1, s2)
        advanced[f, :, 256:] = state[f, :, 256:] + s2[:, : cells - 256]


def in_vmem(count):
    return [pl.BlockSpec(memory_space=pltpu.VMEM)] * count


def body(state, zonal_wind, meridional_wind, filter_flag, mode_count):
    field_count, level_count, lat_cells, lon_cells = state.shape
    item_count = field_count * level_count
    band_total, sectors = lax.axis_size("lat"), lax.axis_size("lon")
    nlat, circle = lat_cells * band_total, lon_cells * sectors
    band_index = lax.axis_index("lat")
    wide = 128 * SLABS
    fields = state.reshape(item_count, lat_cells, lon_cells)
    zonal, merid = (w.reshape(lat_cells, lon_cells) for w in (zonal_wind, meridional_wind))

    forward = [(i, i + 1) for i in range(band_total - 1)]
    backward = [(target, source) for source, target in forward]
    top = jnp.concatenate([fields[:, -1], merid[-1:]], axis=0)
    top = jnp.pad(top, ((0, 8 - item_count - 1), (0, wide - lon_cells)))
    bottom = jnp.pad(fields[:, 0], ((0, 8 - item_count), (0, wide - lon_cells)))
    south = lax.ppermute(top, "lat", forward)
    north = lax.ppermute(bottom, "lat", backward)

    zonal_scale = math.sin(math.pi / (2 * nlat))

    def center_metric(ids):
        return jnp.cos((ids.astype(jnp.float32) + 0.5) * (math.pi / nlat) - math.pi / 2)

    def face_metric(ids):
        return jnp.sin((ids.astype(jnp.float32) + 1.0) * (math.pi / nlat))

    ids = band_index * lat_cells + jnp.arange(lat_cells, dtype=jnp.int32)
    center = center_metric(ids)
    metric = jnp.stack(
        [zonal_scale / center, meridional_scale / center, face_metric(ids), face_metric(ids - 1)]
    )
    metric = jnp.broadcast_to(metric[:, :, None], (4, lat_cells, 128))

    high, low, reduced, scale = mode_layout(circle, circle // 16)
    own_row = band_index * lat_cells + lax.axis_index("lon")
    chosen = jnp.arange(nlat, dtype=jnp.int32) == own_row
    flag = jnp.sum(jnp.where(chosen, filter_flag, 0))
    count = jnp.sum(jnp.where(chosen, mode_count, 0))
    raised = jnp.maximum(count + 1 - jnp.asarray(reduced), 0).astype(jnp.float32)
    damping = raised / jnp.maximum(count.astype(jnp.float32), 1.0) * flag.astype(jnp.float32)
    damping = damping * jnp.asarray(scale)
    own = jnp.broadcast_to(zonal_scale / center_metric(own_row), (8, 128))

    chunks = pl.pallas_call(
        increment_kernel,
        out_shape=jax.ShapeDtypeStruct((sectors * ROWS, 128), jnp.float32),
        in_specs=in_vmem(6),
        out_specs=pl.BlockSpec(memory_space=pltpu.VMEM),
        scratch_shapes=[pltpu.VMEM((8, lat_cells, wide), jnp.float32)],
        name="increments",
    )(fields, zonal, merid, south, north, metric)
    chunks = lax.all_to_all(chunks.reshape(sectors, ROWS, 128), "lon", 0, 0, tiled=True)
    chunks = pl.pallas_call(
        filter_kernel,
        out_shape=jax.ShapeDtypeStruct((sectors, ROWS, 128), jnp.float32),
        in_specs=in_vmem(5),
        out_specs=pl.BlockSpec(memory_space=pltpu.VMEM),
        name="filter_rows",
    )(chunks, own, damping, jnp.asarray(high), jnp.asarray(low))
    chunks = lax.all_to_all(chunks, "lon", 0, 0, tiled=True)
    advanced = pl.pallas_call(
        final_kernel,
        out_shape=jax.ShapeDtypeStruct((item_count, lat_cells, lon_cells), jnp.float32),
        in_specs=in_vmem(2),
        out_specs=pl.BlockSpec(memory_space=pltpu.VMEM),
        name="advance",
    )(chunks.reshape(sectors * ROWS, 128), fields)
    return advanced.reshape(state.shape)


def solution(mesh):
    placed = (P(None, None, "lat", "lon"), P(None, "lat", "lon"), P(None, "lat", "lon"), P(), P())
    return jax.shard_map(
        body, mesh=mesh, in_specs=placed, out_specs=P(None, None, "lat", "lon"), check_vma=False
    )
```

```python
import math

import jax
import jax.numpy as jnp
import ml_dtypes
import numpy as np
from jax import lax
from jax.experimental import pallas as pl
from jax.experimental.pallas import tpu as pltpu
from jax.sharding import PartitionSpec as P

meridional_scale = 0.25
SLABS = 3
SLAB = 120
POINTS = 48
ROWS = 8 * SLABS
GROUPS = 3


def mode_layout(circle, kmax):
    table = np.zeros((GROUPS, 256, 256), np.float64)
    reduced = np.full((GROUPS, 256), 1 << 20, np.int32)
    scale = np.zeros((GROUPS, 256), np.float64)
    b = np.arange(SLAB)
    sign = np.where(b % 2 == 0, 1.0, -1.0)
    for residue in range(POINTS // 2):
        group, place = divmod(residue, 8)
        if residue == 0:
            waves = [(48 * n, 0) for n in range(1, 8)] + [(24 + 48 * n, 128) for n in range(8)]
            factor = 2.0 / circle
        else:
            waves = [(residue + 48 * n, None) for n in range(-8, 8) if abs(residue + 48 * n) <= kmax]
            factor = 1.0 / circle
        for t, (k, row) in enumerate(waves):
            angle = 2.0 * np.pi * ((k * b) % circle) / circle
            cosine, sine = sign * np.cos(angle), sign * np.sin(angle)
            re, im = 32 * place + t, 32 * place + 16 + t
            if row is None:
                table[group, :SLAB, re], table[group, 128 : 128 + SLAB, re] = cosine, sine
                table[group, :SLAB, im], table[group, 128 : 128 + SLAB, im] = -sine, cosine
            else:
                table[group, row : row + SLAB, re] = cosine
                table[group, row : row + SLAB, im] = -sine
            reduced[group, [re, im]] = abs(k)
            scale[group, [re, im]] = factor
    high = table.astype(np.float32).astype(ml_dtypes.bfloat16)
    low = (table - high.astype(np.float64)).astype(np.float32).astype(ml_dtypes.bfloat16)
    return high, low, reduced, scale.astype(np.float32)


def c_add(x, y):
    return (x[0] + y[0], y[1] if x[1] is None else x[1] if y[1] is None else x[1] + y[1])


def c_sub(x, y):
    if y[1] is None:
        return (x[0] - y[0], x[1])
    return (x[0] - y[0], -y[1] if x[1] is None else x[1] - y[1])


def c_conj(x):
    return (x[0], None if x[1] is None else -x[1])


def c_turn(x, numer, denom):
    numer %= denom
    eighth = 8 * numer
    if numer == 0:
        return x
    if 2 * numer == denom:
        return (-x[0], None if x[1] is None else -x[1])
    if 4 * numer == denom:
        return (jnp.zeros_like(x[0]) if x[1] is None else -x[1], x[0])
    if 4 * numer == 3 * denom:
        return (jnp.zeros_like(x[0]) if x[1] is None else x[1], -x[0])
    angle = 2.0 * math.pi * numer / denom
    c, s = math.cos(angle), math.sin(angle)
    if x[1] is None:
        return (x[0] * c, x[0] * s)
    if eighth in (denom, 3 * denom, 5 * denom, 7 * denom):
        h = math.sqrt(0.5)
        a, b = (x[0] - x[1]) * h, (x[0] + x[1]) * h
        return {1: (a, b), 3: (-b, a), 5: (-a, -b), 7: (b, -a)}[eighth // denom]
    return (x[0] * c - x[1] * s, x[0] * s + x[1] * c)


def rfft(x):
    count = len(x)
    if count == 1:
        return [(x[0], None)]
    if count == 2:
        return [(x[0] + x[1], None), (x[0] - x[1], None)]
    even, odd = rfft(x[0::2]), rfft(x[1::2])
    result = [None] * (count // 2 + 1)
    for k in range(count // 4 + 1):
        turned = c_turn(odd[k], -k, count)
        result[k] = c_add(even[k], turned)
        if k != count // 4 or count == 2:
            result[count // 2 - k] = c_conj(c_sub(even[k], turned))
    return result


def irfft(z):
    count = 2 * (len(z) - 1)
    if count == 2:
        return [z[0][0] + z[1][0], z[0][0] - z[1][0]]
    even, odd = [], []
    for k in range(count // 4 + 1):
        mirror = c_conj(z[count // 2 - k])
        even.append(c_add(z[k], mirror))
        odd.append(c_turn(c_sub(z[k], mirror), k, count))
    result = [None] * count
    result[0::2], result[1::2] = irfft(even), irfft(odd)
    return result


def circle_forward(x):
    parts = [rfft(x[a::3]) for a in range(3)]
    result = [None] * 25
    half, root = 0.5, math.sqrt(3.0) / 2.0
    for k in range(9):
        t0 = parts[0][k]
        t1, t2 = c_turn(parts[1][k], -k, 48), c_turn(parts[2][k], -2 * k, 48)
        total, gap = c_add(t1, t2), c_sub(t1, t2)
        result[k] = c_add(t0, total)
        mid = (t0[0] - half * total[0], None if t0[1] is None and total[1] is None else
               (t0[1] if total[1] is None else (0.0 if t0[1] is None else t0[1]) - half * total[1]))
        turn = (None if gap[1] is None else root * gap[1], -root * gap[0])
        plus_re = mid[0] if turn[0] is None else mid[0] + turn[0]
        plus_im = turn[1] if mid[1] is None else mid[1] + turn[1]
        minus_re = mid[0] if turn[0] is None else mid[0] - turn[0]
        minus_im = -turn[1] if mid[1] is None else mid[1] - turn[1]
        if k + 16 <= 24:
            result[k + 16] = (plus_re, plus_im)
        if k > 0 and 16 - k != k + 16 and result[16 - k] is None:
            result[16 - k] = (minus_re, -minus_im)
    return result


def circle_backward(z):
    half, root = 0.5, math.sqrt(3.0) / 2.0
    spectra = [[], [], []]
    for k in range(9):
        t0 = z[k]
        t1 = z[k + 16] if k + 16 <= 24 else c_conj(z[32 - k])
        t2 = c_conj(z[16 - k])
        total, gap = c_add(t1, t2), c_sub(t1, t2)
        if k == 0:
            total, gap = (2.0 * t1[0], None), (None, 2.0 * t1[1])
        spectra[0].append(c_add(t0, total))
        mid = (t0[0] - half * total[0],
               t0[1] if total[1] is None else (-half * total[1] if t0[1] is None else t0[1] - half * total[1]))
        turn = (-root * gap[1], None if gap[0] is None else root * gap[0])
        plus = c_add(mid, turn)
        minus = c_sub(mid, turn)
        spectra[1].append(c_turn(plus, k, 48))
        spectra[2].append(c_turn(minus, 2 * k, 48))
    result = [None] * 48
    for a in range(3):
        result[a::3] = irfft(spectra[a])
    return result


def slabs_of(part):
    lane = lax.broadcasted_iota(jnp.int32, (part.shape[0], 128), 1)
    v0, v1, v2 = part[:, :128], part[:, 128:256], part[:, 256:]
    return (
        v0,
        jnp.where(lane < 8, pltpu.roll(v0, 8, 1), pltpu.roll(v1, 8, 1)),
        jnp.where(lane < 16, pltpu.roll(v1, 16, 1), pltpu.roll(v2, 16, 1)),
    )


def border_kernel(state, merid, top, bottom, pad):
    fields, rows, cells = state.shape
    pad[:, :, 128 * (SLABS - 1) :] = jnp.zeros((2, 8, 128), jnp.float32)
    pad[1, fields:, :] = jnp.zeros((8 - fields, 128 * SLABS), jnp.float32)
    pad[0, fields:, :] = jnp.zeros((8 - fields, 128 * SLABS), jnp.float32)
    for f in range(fields):
        pad[0, f : f + 1, :cells] = state[f, rows - 1 :, :]
        pad[1, f : f + 1, :cells] = state[f, :1, :]
    pad[0, fields : fields + 1, :cells] = merid[rows - 1 :, :]
    for place, border in ((0, top), (1, bottom)):
        for a, slab in enumerate(slabs_of(pad[place])):
            border[8 * a : 8 * a + 8, :] = slab


def increment_kernel(state, zonal, merid, metric, chunks, pad):
    fields, rows, cells = state.shape
    wide = 128 * SLABS
    for f in range(fields + 2):
        pad[f, :, wide - 128 :] = jnp.zeros((rows, 128), jnp.float32)
    for f in range(fields):
        pad[f, :, :cells] = state[f]
    pad[fields, :, :cells] = zonal[...]
    pad[fields + 1, :, :cells] = merid[...]
    lane = lax.broadcasted_iota(jnp.int32, (rows, wide), 1)
    row = lax.broadcasted_iota(jnp.int32, (rows, wide), 0)

    def spread(index):
        part = metric[index]
        return jnp.concatenate([part] * SLABS, axis=1)

    zonal_factor, merid_factor, face = (spread(i) for i in range(3))
    east_wind = pad[fields]
    last_wind = pltpu.roll(east_wind, 3, 1)
    inner_wind = jnp.where(lane < cells - 1, east_wind, 0.0)
    north_wind = jnp.where(row < rows - 1, pad[fields + 1] * face, 0.0)
    for f in range(fields):
        q = pad[f]
        flux_east = inner_wind * (0.5 * (q + pltpu.roll(q, wide - 1, 1)))
        zonal_diff = flux_east - pltpu.roll(flux_east, 1, 1)
        flux_north = north_wind * (0.5 * (q + pltpu.roll(q, rows - 1, 0)))
        merid_diff = flux_north - pltpu.roll(flux_north, 1, 0)
        part = -zonal_factor * zonal_diff - merid_factor * merid_diff
        part = jnp.where(lane == cells, pltpu.roll(q, cells, 1), part)
        part = jnp.where(lane == cells + 1, pltpu.roll(q, 2, 1), part)
        part = jnp.where(lane == cells + 2, last_wind, part)
        for a, slab in enumerate(slabs_of(part)):
            chunks[pl.ds(8 * a + f, rows, stride=ROWS), :] = slab
    for f in range(fields, 8):
        for a in range(SLABS):
            chunks[pl.ds(8 * a + f, rows, stride=ROWS), :] = jnp.zeros((rows, 128), jnp.float32)


def border_fluxes_kernel(part, top, bottom, south, north, metric, chunks):
    fields, last = 6, part.shape[0] - ROWS
    rows = metric.shape[1]
    inside = lax.broadcasted_iota(jnp.int32, (8, 128), 1) < SLAB
    first_factor, last_factor = metric[1, 0:1, :], metric[1, rows - 1 :, :]
    first_face, last_face = metric[3, 0:1, :], metric[2, rows - 1 :, :]
    has_north = metric[4, 0:1, :]
    chunks[...] = part[...]
    for a in range(SLABS):
        here = slice(8 * a, 8 * a + 8)
        wind = slice(8 * a + fields, 8 * a + fields + 1)
        flux = (south[wind, :] * first_face) * (0.5 * (south[here, :] + bottom[here, :]))
        chunks[here, :] = part[here, :] + jnp.where(inside, first_factor * flux, 0.0)
        flux = (top[wind, :] * last_face) * (0.5 * (top[here, :] + has_north * north[here, :]))
        there = slice(last + 8 * a, last + 8 * a + 8)
        chunks[there, :] = part[there, :] - jnp.where(inside, last_factor * flux, 0.0)


def split(x):
    high = x.astype(jnp.bfloat16)
    return high, (x - high.astype(jnp.float32)).astype(jnp.bfloat16)


def product(x, high, low, dims):
    def dot(p, q):
        return lax.dot_general(p, q, (dims, ((), ())), preferred_element_type=jnp.float32)

    x_high, x_low = split(x)
    return dot(x_high, high) + (dot(x_low, high) + dot(x_high, low))


def filter_kernel(chunks, own, damping, high, low, result):
    sectors = chunks.shape[0]
    lane = lax.broadcasted_iota(jnp.int32, (8, 128), 1)
    zonal_factor = own[...]
    points = [chunks[p // 3, 8 * (p % 3) : 8 * (p % 3) + 8, :] for p in range(POINTS)]
    lasts = [points[3 * s + 2] for s in range(sectors)]
    for s in range(sectors):
        after = (s + 1) % sectors
        flux = pltpu.roll(lasts[s], 125, 1) * (
            0.5 * (pltpu.roll(lasts[s], 126, 1) + pltpu.roll(lasts[after], 127, 1))
        )
        edge = jnp.where(lane == SLAB - 1, zonal_factor * flux, 0.0)
        points[3 * s + 2] = points[3 * s + 2] - edge
        points[3 * after] = points[3 * after] + pltpu.roll(edge, 128 - (SLAB - 1), 1)
    for p in range(POINTS):
        result[p // 3, 8 * (p % 3) : 8 * (p % 3) + 8, :] = points[p]
    spectrum = circle_forward(points)
    spectrum[0] = (spectrum[0][0], spectrum[24][0])
    block = lax.broadcasted_iota(jnp.int32, (64, 256), 0) // 8
    column = lax.broadcasted_iota(jnp.int32, (64, 256), 1) // 32
    back = [None] * 25
    for g in range(GROUPS):
        rows = jnp.concatenate(
            [jnp.concatenate(spectrum[8 * g + i], axis=1) for i in range(8)], axis=0
        )
        modes = product(rows, high[g], low[g], ((1,), (0,)))
        modes = jnp.where(block == column, modes * damping[g : g + 1, :], 0.0)
        rows = product(modes, high[g], low[g], ((1,), (1,)))
        for i in range(8):
            part = rows[8 * i : 8 * i + 8, :]
            back[8 * g + i] = (part[:, :128], part[:, 128:])
    back[24] = (back[0][1], None)
    back[0] = (back[0][0], None)
    correction = circle_backward(back)
    for p in range(POINTS):
        place = (p // 3, slice(8 * (p % 3), 8 * (p % 3) + 8), slice(None))
        result[place] = result[place] - correction[p]


def final_kernel(chunks, state, advanced):
    fields, rows, cells = state.shape
    lane = lax.broadcasted_iota(jnp.int32, (rows, 128), 1)
    for f in range(fields):
        s0, s1, s2 = (chunks[pl.ds(8 * a + f, rows, stride=ROWS), :] for a in range(SLABS))
        s1, s2 = pltpu.roll(s1, 120, 1), pltpu.roll(s2, 112, 1)
        advanced[f, :, :128] = state[f, :, :128] + jnp.where(lane < 120, s0, s1)
        advanced[f, :, 128:256] = state[f, :, 128:256] + jnp.where(lane < 112, s1, s2)
        advanced[f, :, 256:] = state[f, :, 256:] + s2[:, : cells - 256]


def call(kernel, name, outs, mebibytes, args, scratch=()):
    vmem = pl.BlockSpec(memory_space=pltpu.VMEM)
    return pl.pallas_call(
        kernel,
        out_shape=[jax.ShapeDtypeStruct(shape, jnp.float32) for shape in outs],
        in_specs=[vmem] * len(args),
        out_specs=[vmem] * len(outs),
        scratch_shapes=[pltpu.VMEM(shape, jnp.float32) for shape in scratch],
        compiler_params=pltpu.CompilerParams(vmem_limit_bytes=mebibytes << 20),
        name=name,
    )(*args)


def body(state, zonal_wind, meridional_wind, filter_flag, mode_count):
    field_count, level_count, lat_cells, lon_cells = state.shape
    item_count = field_count * level_count
    band_total, sectors = lax.axis_size("lat"), lax.axis_size("lon")
    nlat, circle = lat_cells * band_total, lon_cells * sectors
    band_index = lax.axis_index("lat")
    wide = 128 * SLABS
    fields = state.reshape(item_count, lat_cells, lon_cells)
    zonal, merid = (w.reshape(lat_cells, lon_cells) for w in (zonal_wind, meridional_wind))

    forward = [(i, (i + 1) % band_total) for i in range(band_total)]
    backward = [(target, source) for source, target in forward]
    top, bottom = call(
        border_kernel, "borders", [(ROWS, 128)] * 2, 2, (fields, merid), [(2, 8, wide)]
    )
    south = lax.ppermute(top, "lat", forward)
    north = lax.ppermute(bottom, "lat", backward)

    zonal_scale = math.sin(math.pi / (2 * nlat))

    def center_metric(ids):
        return jnp.cos((ids.astype(jnp.float32) + 0.5) * (math.pi / nlat) - math.pi / 2)

    def face_metric(ids):
        return jnp.sin((ids.astype(jnp.float32) + 1.0) * (math.pi / nlat))

    ids = band_index * lat_cells + jnp.arange(lat_cells, dtype=jnp.int32)
    center = center_metric(ids)
    has_north = jnp.where(band_index < band_total - 1, jnp.ones_like(center), 0.0)
    metric = jnp.stack(
        [zonal_scale / center, meridional_scale / center, face_metric(ids), face_metric(ids - 1), has_north]
    )
    metric = jnp.broadcast_to(metric[:, :, None], (5, lat_cells, 128))

    high, low, reduced, scale = mode_layout(circle, circle // 16)
    own_row = band_index * lat_cells + lax.axis_index("lon")
    chosen = jnp.arange(nlat, dtype=jnp.int32) == own_row
    flag = jnp.sum(jnp.where(chosen, filter_flag, 0))
    count = jnp.sum(jnp.where(chosen, mode_count, 0))
    raised = jnp.maximum(count + 1 - jnp.asarray(reduced), 0).astype(jnp.float32)
    damping = raised / jnp.maximum(count.astype(jnp.float32), 1.0) * flag.astype(jnp.float32)
    damping = damping * jnp.asarray(scale)
    own = jnp.broadcast_to(zonal_scale / center_metric(own_row), (8, 128))

    packed = (sectors * ROWS, 128)
    (part,) = call(
        increment_kernel, "increments", [packed], 4, (fields, zonal, merid, metric), [(8, lat_cells, wide)]
    )
    (chunks,) = call(
        border_fluxes_kernel, "border_fluxes", [packed], 2, (part, top, bottom, south, north, metric)
    )
    chunks = lax.all_to_all(chunks.reshape(sectors, ROWS, 128), "lon", 0, 0, tiled=True)
    (chunks,) = call(
        filter_kernel,
        "filter_rows",
        [(sectors, ROWS, 128)],
        8,
        (chunks, own, damping, jnp.asarray(high), jnp.asarray(low)),
    )
    chunks = lax.all_to_all(chunks, "lon", 0, 0, tiled=True)
    (advanced,) = call(final_kernel, "advance", [fields.shape], 4, (chunks.reshape(packed), fields))
    return advanced.reshape(state.shape)


def solution(mesh):
    placed = (P(None, None, "lat", "lon"), P(None, "lat", "lon"), P(None, "lat", "lon"), P(), P())
    return jax.shard_map(
        body, mesh=mesh, in_specs=placed, out_specs=P(None, None, "lat", "lon"), check_vma=False
    )
```

```python
import math

import jax
import jax.numpy as jnp
import ml_dtypes
import numpy as np
from jax import lax
from jax.experimental import pallas as pl
from jax.experimental.pallas import tpu as pltpu
from jax.sharding import PartitionSpec as P

meridional_scale = 0.25
SLABS = 3
SLAB = 120
POINTS = 48
ROWS = 8 * SLABS
GROUPS = 3


def mode_layout(circle, kmax):
    table = np.zeros((GROUPS, 256, 256), np.float64)
    reduced = np.full((GROUPS, 256), 1 << 20, np.int32)
    scale = np.zeros((GROUPS, 256), np.float64)
    b = np.arange(SLAB)
    sign = np.where(b % 2 == 0, 1.0, -1.0)
    for residue in range(POINTS // 2):
        group, place = divmod(residue, 8)
        if residue == 0:
            waves = [(48 * n, 0) for n in range(1, 8)] + [(24 + 48 * n, 128) for n in range(8)]
            factor = 2.0 / circle
        else:
            waves = [(residue + 48 * n, None) for n in range(-8, 8) if abs(residue + 48 * n) <= kmax]
            factor = 1.0 / circle
        for t, (k, row) in enumerate(waves):
            angle = 2.0 * np.pi * ((k * b) % circle) / circle
            cosine, sine = sign * np.cos(angle), sign * np.sin(angle)
            re, im = 32 * place + t, 32 * place + 16 + t
            if row is None:
                table[group, :SLAB, re], table[group, 128 : 128 + SLAB, re] = cosine, sine
                table[group, :SLAB, im], table[group, 128 : 128 + SLAB, im] = -sine, cosine
            else:
                table[group, row : row + SLAB, re] = cosine
                table[group, row : row + SLAB, im] = -sine
            reduced[group, [re, im]] = abs(k)
            scale[group, [re, im]] = factor
    high = table.astype(np.float32).astype(ml_dtypes.bfloat16)
    low = (table - high.astype(np.float64)).astype(np.float32).astype(ml_dtypes.bfloat16)
    return high, low, reduced, scale.astype(np.float32)


def row_metrics(nlat, bands):
    ids = np.arange(nlat, dtype=np.float32)
    step = np.float32(math.pi / nlat)
    center = (ids + np.float32(0.5)) * step - np.float32(math.pi / 2)
    center = np.cos(center.astype(np.float64)).astype(np.float32)
    result = np.zeros((nlat, 128), np.float32)
    result[:, 0] = np.float32(math.sin(math.pi / (2 * nlat))) / center
    result[:, 1] = np.float32(meridional_scale) / center
    result[:, 2] = np.sin(((ids + np.float32(1.0)) * step).astype(np.float64))
    result[:, 3] = np.sin((ids * step).astype(np.float64))
    result[:, 4] = np.arange(nlat) // (nlat // bands) < bands - 1
    return result.reshape(bands, nlat // bands, 128)


def c_add(x, y):
    return (x[0] + y[0], y[1] if x[1] is None else x[1] if y[1] is None else x[1] + y[1])


def c_sub(x, y):
    if y[1] is None:
        return (x[0] - y[0], x[1])
    return (x[0] - y[0], -y[1] if x[1] is None else x[1] - y[1])


def c_conj(x):
    return (x[0], None if x[1] is None else -x[1])


def c_turn(x, numer, denom):
    numer %= denom
    eighth = 8 * numer
    if numer == 0:
        return x
    if 2 * numer == denom:
        return (-x[0], None if x[1] is None else -x[1])
    if 4 * numer == denom:
        return (jnp.zeros_like(x[0]) if x[1] is None else -x[1], x[0])
    if 4 * numer == 3 * denom:
        return (jnp.zeros_like(x[0]) if x[1] is None else x[1], -x[0])
    angle = 2.0 * math.pi * numer / denom
    c, s = math.cos(angle), math.sin(angle)
    if x[1] is None:
        return (x[0] * c, x[0] * s)
    if eighth in (denom, 3 * denom, 5 * denom, 7 * denom):
        h = math.sqrt(0.5)
        a, b = (x[0] - x[1]) * h, (x[0] + x[1]) * h
        return {1: (a, b), 3: (-b, a), 5: (-a, -b), 7: (b, -a)}[eighth // denom]
    return (x[0] * c - x[1] * s, x[0] * s + x[1] * c)


def rfft(x):
    count = len(x)
    if count == 1:
        return [(x[0], None)]
    if count == 2:
        return [(x[0] + x[1], None), (x[0] - x[1], None)]
    even, odd = rfft(x[0::2]), rfft(x[1::2])
    result = [None] * (count // 2 + 1)
    for k in range(count // 4 + 1):
        turned = c_turn(odd[k], -k, count)
        result[k] = c_add(even[k], turned)
        if k != count // 4 or count == 2:
            result[count // 2 - k] = c_conj(c_sub(even[k], turned))
    return result


def irfft(z):
    count = 2 * (len(z) - 1)
    if count == 2:
        return [z[0][0] + z[1][0], z[0][0] - z[1][0]]
    even, odd = [], []
    for k in range(count // 4 + 1):
        mirror = c_conj(z[count // 2 - k])
        even.append(c_add(z[k], mirror))
        odd.append(c_turn(c_sub(z[k], mirror), k, count))
    result = [None] * count
    result[0::2], result[1::2] = irfft(even), irfft(odd)
    return result


def circle_forward(x):
    parts = [rfft(x[a::3]) for a in range(3)]
    result = [None] * 25
    half, root = 0.5, math.sqrt(3.0) / 2.0
    for k in range(9):
        t0 = parts[0][k]
        t1, t2 = c_turn(parts[1][k], -k, 48), c_turn(parts[2][k], -2 * k, 48)
        total, gap = c_add(t1, t2), c_sub(t1, t2)
        result[k] = c_add(t0, total)
        mid = (t0[0] - half * total[0], None if t0[1] is None and total[1] is None else
               (t0[1] if total[1] is None else (0.0 if t0[1] is None else t0[1]) - half * total[1]))
        turn = (None if gap[1] is None else root * gap[1], -root * gap[0])
        plus_re = mid[0] if turn[0] is None else mid[0] + turn[0]
        plus_im = turn[1] if mid[1] is None else mid[1] + turn[1]
        minus_re = mid[0] if turn[0] is None else mid[0] - turn[0]
        minus_im = -turn[1] if mid[1] is None else mid[1] - turn[1]
        if k + 16 <= 24:
            result[k + 16] = (plus_re, plus_im)
        if k > 0 and 16 - k != k + 16 and result[16 - k] is None:
            result[16 - k] = (minus_re, -minus_im)
    return result


def circle_backward(z):
    half, root = 0.5, math.sqrt(3.0) / 2.0
    spectra = [[], [], []]
    for k in range(9):
        t0 = z[k]
        t1 = z[k + 16] if k + 16 <= 24 else c_conj(z[32 - k])
        t2 = c_conj(z[16 - k])
        total, gap = c_add(t1, t2), c_sub(t1, t2)
        if k == 0:
            total, gap = (2.0 * t1[0], None), (None, 2.0 * t1[1])
        spectra[0].append(c_add(t0, total))
        mid = (t0[0] - half * total[0],
               t0[1] if total[1] is None else (-half * total[1] if t0[1] is None else t0[1] - half * total[1]))
        turn = (-root * gap[1], None if gap[0] is None else root * gap[0])
        plus = c_add(mid, turn)
        minus = c_sub(mid, turn)
        spectra[1].append(c_turn(plus, k, 48))
        spectra[2].append(c_turn(minus, 2 * k, 48))
    result = [None] * 48
    for a in range(3):
        result[a::3] = irfft(spectra[a])
    return result


def slabs_of(part):
    lane = lax.broadcasted_iota(jnp.int32, (part.shape[0], 128), 1)
    v0, v1, v2 = part[:, :128], part[:, 128:256], part[:, 256:]
    return (
        v0,
        jnp.where(lane < 8, pltpu.roll(v0, 8, 1), pltpu.roll(v1, 8, 1)),
        jnp.where(lane < 16, pltpu.roll(v1, 16, 1), pltpu.roll(v2, 16, 1)),
    )


def border_kernel(state_in, zonal_in, merid_in, top, bottom, state, zonal, merid, pad, sems):
    fields, rows, cells = state.shape
    copies = [
        pltpu.make_async_copy(source, target, sems.at[i])
        for i, (source, target) in enumerate(((state_in, state), (merid_in, merid), (zonal_in, zonal)))
    ]
    for copy in copies:
        copy.start()
    pad[...] = jnp.zeros(pad.shape, jnp.float32)
    for copy in copies:
        copy.wait()
    for f in range(fields):
        pad[0, f : f + 1, :cells] = state[f, rows - 1 :, :]
        pad[1, f : f + 1, :cells] = state[f, :1, :]
    pad[0, fields : fields + 1, :cells] = merid[rows - 1 :, :]
    for place, border in ((0, top), (1, bottom)):
        for a, slab in enumerate(slabs_of(pad[place])):
            border[8 * a : 8 * a + 8, :] = slab


def increment_kernel(
    state, zonal, merid, reduced, scale, table, flags, counts,
    chunks, metric, own, pad, flags_here, counts_here, sems,
):
    fields, rows, cells = state.shape
    wide = 128 * SLABS
    band, sector = lax.axis_index("lat"), lax.axis_index("lon")
    copies = [
        pltpu.make_async_copy(table.at[band], metric, sems.at[0]),
        pltpu.make_async_copy(flags, flags_here, sems.at[1]),
        pltpu.make_async_copy(counts, counts_here, sems.at[2]),
    ]
    for copy in copies:
        copy.start()
    for f in range(fields + 2):
        pad[f, :, wide - 128 :] = jnp.zeros((rows, 128), jnp.float32)
    for f in range(fields):
        pad[f, :, :cells] = state[f]
    pad[fields, :, :cells] = zonal[...]
    pad[fields + 1, :, :cells] = merid[...]
    lane = lax.broadcasted_iota(jnp.int32, (rows, wide), 1)
    row = lax.broadcasted_iota(jnp.int32, (rows, wide), 0)
    for copy in copies:
        copy.wait()

    def spread(index):
        return jnp.broadcast_to(metric[:, index : index + 1], (rows, wide))

    zonal_factor, merid_factor, face = (spread(i) for i in range(3))
    east_wind = pad[fields]
    last_wind = pltpu.roll(east_wind, 3, 1)
    inner_wind = jnp.where(lane < cells - 1, east_wind, 0.0)
    north_wind = jnp.where(row < rows - 1, pad[fields + 1] * face, 0.0)
    for f in range(fields):
        q = pad[f]
        flux_east = inner_wind * (0.5 * (q + pltpu.roll(q, wide - 1, 1)))
        zonal_diff = flux_east - pltpu.roll(flux_east, 1, 1)
        flux_north = north_wind * (0.5 * (q + pltpu.roll(q, rows - 1, 0)))
        merid_diff = flux_north - pltpu.roll(flux_north, 1, 0)
        part = -zonal_factor * zonal_diff - merid_factor * merid_diff
        part = jnp.where(lane == cells, pltpu.roll(q, cells, 1), part)
        part = jnp.where(lane == cells + 1, pltpu.roll(q, 2, 1), part)
        part = jnp.where(lane == cells + 2, last_wind, part)
        for a, slab in enumerate(slabs_of(part)):
            chunks[pl.ds(8 * a + f, rows, stride=ROWS), :] = slab
    for f in range(fields, 8):
        for a in range(SLABS):
            chunks[pl.ds(8 * a + f, rows, stride=ROWS), :] = jnp.zeros((rows, 128), jnp.float32)
    flag = flags_here[band * rows + sector].astype(jnp.float32)
    count = counts_here[band * rows + sector].astype(jnp.float32)
    raised = jnp.maximum(count + 1.0 - reduced[...], 0.0)
    own[:8, :] = raised / jnp.maximum(count, 1.0) * flag * scale[...]
    mine = jnp.where(row == sector, zonal_factor, 0.0)[:, :256]
    own[8:, :] = jnp.broadcast_to(jnp.sum(mine, axis=0, keepdims=True), (8, 256))


def border_fluxes_kernel(part, top, bottom, south, north, metric, chunks):
    fields, last, rows = 6, part.shape[0] - ROWS, metric.shape[0]
    inside = lax.broadcasted_iota(jnp.int32, (8, 128), 1) < SLAB

    def spread(row, index):
        return jnp.broadcast_to(metric[row : row + 1, index : index + 1], (8, 128))

    first_factor, last_factor = spread(0, 1), spread(rows - 1, 1)
    first_face, last_face = spread(0, 3), spread(rows - 1, 2)
    has_north = spread(0, 4)
    chunks[...] = part[...]
    for a in range(SLABS):
        here = slice(8 * a, 8 * a + 8)
        wind = slice(8 * a + fields, 8 * a + fields + 1)
        flux = (south[wind, :] * first_face) * (0.5 * (south[here, :] + bottom[here, :]))
        chunks[here, :] = part[here, :] + jnp.where(inside, first_factor * flux, 0.0)
        flux = (top[wind, :] * last_face) * (0.5 * (top[here, :] + has_north * north[here, :]))
        there = slice(last + 8 * a, last + 8 * a + 8)
        chunks[there, :] = part[there, :] - jnp.where(inside, last_factor * flux, 0.0)


def split(x):
    high = x.astype(jnp.bfloat16)
    return high, (x - high.astype(jnp.float32)).astype(jnp.bfloat16)


def product(x, high, low, dims):
    def dot(p, q):
        return lax.dot_general(p, q, (dims, ((), ())), preferred_element_type=jnp.float32)

    x_high, x_low = split(x)
    return dot(x_high, high) + (dot(x_low, high) + dot(x_high, low))


def filter_kernel(chunks, own, high, low, result):
    sectors = chunks.shape[0]
    lane = lax.broadcasted_iota(jnp.int32, (8, 128), 1)
    zonal_factor = own[8:, :128]
    points = [chunks[p // 3, 8 * (p % 3) : 8 * (p % 3) + 8, :] for p in range(POINTS)]
    lasts = [points[3 * s + 2] for s in range(sectors)]
    for s in range(sectors):
        after = (s + 1) % sectors
        flux = pltpu.roll(lasts[s], 125, 1) * (
            0.5 * (pltpu.roll(lasts[s], 126, 1) + pltpu.roll(lasts[after], 127, 1))
        )
        edge = jnp.where(lane == SLAB - 1, zonal_factor * flux, 0.0)
        points[3 * s + 2] = points[3 * s + 2] - edge
        points[3 * after] = points[3 * after] + pltpu.roll(edge, 128 - (SLAB - 1), 1)
    for p in range(POINTS):
        result[p // 3, 8 * (p % 3) : 8 * (p % 3) + 8, :] = points[p]
    spectrum = circle_forward(points)
    spectrum[0] = (spectrum[0][0], spectrum[24][0])
    block = lax.broadcasted_iota(jnp.int32, (64, 256), 0) // 8
    column = lax.broadcasted_iota(jnp.int32, (64, 256), 1) // 32
    back = [None] * 25
    for g in range(GROUPS):
        rows = jnp.concatenate(
            [jnp.concatenate(spectrum[8 * g + i], axis=1) for i in range(8)], axis=0
        )
        modes = product(rows, high[g], low[g], ((1,), (0,)))
        modes = jnp.where(block == column, modes * own[g : g + 1, :], 0.0)
        rows = product(modes, high[g], low[g], ((1,), (1,)))
        for i in range(8):
            part = rows[8 * i : 8 * i + 8, :]
            back[8 * g + i] = (part[:, :128], part[:, 128:])
    back[24] = (back[0][1], None)
    back[0] = (back[0][0], None)
    correction = circle_backward(back)
    for p in range(POINTS):
        place = (p // 3, slice(8 * (p % 3), 8 * (p % 3) + 8), slice(None))
        result[place] = result[place] - correction[p]


def final_kernel(chunks, state, advanced):
    fields, rows, cells = state.shape
    lane = lax.broadcasted_iota(jnp.int32, (rows, 128), 1)
    for f in range(fields):
        s0, s1, s2 = (chunks[pl.ds(8 * a + f, rows, stride=ROWS), :] for a in range(SLABS))
        s1, s2 = pltpu.roll(s1, 120, 1), pltpu.roll(s2, 112, 1)
        advanced[f, :, :128] = state[f, :, :128] + jnp.where(lane < 120, s0, s1)
        advanced[f, :, 128:256] = state[f, :, 128:256] + jnp.where(lane < 112, s1, s2)
        advanced[f, :, 256:] = state[f, :, 256:] + s2[:, : cells - 256]


def call(kernel, name, outs, mebibytes, args, elsewhere=0, scratch=()):
    vmem = pl.BlockSpec(memory_space=pltpu.VMEM)
    stay = pl.BlockSpec(memory_space=pltpu.HBM)
    fixed = len(args) - elsewhere
    args = args[:fixed] + tuple(
        pltpu.with_memory_space_constraint(arg, pltpu.HBM) for arg in args[fixed:]
    )
    return pl.pallas_call(
        kernel,
        out_shape=[jax.ShapeDtypeStruct(shape, jnp.float32) for shape in outs],
        in_specs=[vmem] * fixed + [stay] * elsewhere,
        out_specs=[vmem] * len(outs),
        scratch_shapes=list(scratch),
        compiler_params=pltpu.CompilerParams(vmem_limit_bytes=mebibytes << 20),
        name=name,
    )(*args)


def body(state, zonal_wind, meridional_wind, filter_flag, mode_count):
    field_count, level_count, lat_cells, lon_cells = state.shape
    item_count = field_count * level_count
    band_total, sectors = lax.axis_size("lat"), lax.axis_size("lon")
    nlat, circle = lat_cells * band_total, lon_cells * sectors
    wide = 128 * SLABS
    fields = state.reshape(item_count, lat_cells, lon_cells)
    zonal, merid = (w.reshape(lat_cells, lon_cells) for w in (zonal_wind, meridional_wind))
    high, low, reduced, scale = mode_layout(circle, circle // 16)

    def eight(rows):
        return jnp.asarray(np.pad(rows.astype(np.float32), ((0, 8 - rows.shape[0]), (0, 0))))

    top, bottom, fields, zonal, merid = call(
        border_kernel,
        "borders",
        [(ROWS, 128)] * 2 + [fields.shape, zonal.shape, merid.shape],
        3,
        (fields, zonal, merid),
        3,
        [pltpu.VMEM((2, 8, wide), jnp.float32), pltpu.SemaphoreType.DMA((3,))],
    )
    forward = [(i, i + 1) for i in range(band_total - 1)]
    backward = [(target, source) for source, target in forward]
    south = lax.ppermute(top, "lat", forward)
    north = lax.ppermute(bottom, "lat", backward)

    packed = (sectors * ROWS, 128)
    part, metric, own = call(
        increment_kernel,
        "increments",
        [packed, (lat_cells, 128), (16, 256)],
        4,
        (fields, zonal, merid, eight(reduced), eight(scale))
        + (jnp.asarray(row_metrics(nlat, band_total)), filter_flag, mode_count),
        3,
        [
            pltpu.VMEM((8, lat_cells, wide), jnp.float32),
            pltpu.SMEM(filter_flag.shape, jnp.int32),
            pltpu.SMEM(mode_count.shape, jnp.int32),
            pltpu.SemaphoreType.DMA((3,)),
        ],
    )
    (chunks,) = call(
        border_fluxes_kernel, "border_fluxes", [packed], 2, (part, top, bottom, south, north, metric)
    )
    chunks = lax.all_to_all(chunks.reshape(sectors, ROWS, 128), "lon", 0, 0, tiled=True)
    (chunks,) = call(
        filter_kernel,
        "filter_rows",
        [(sectors, ROWS, 128)],
        8,
        (chunks, own, jnp.asarray(high), jnp.asarray(low)),
    )
    chunks = lax.all_to_all(chunks, "lon", 0, 0, tiled=True)
    (advanced,) = call(final_kernel, "advance", [fields.shape], 4, (chunks.reshape(packed), fields))
    return advanced.reshape(state.shape)


def solution(mesh):
    placed = (P(None, None, "lat", "lon"), P(None, "lat", "lon"), P(None, "lat", "lon"), P(), P())
    return jax.shard_map(
        body, mesh=mesh, in_specs=placed, out_specs=P(None, None, "lat", "lon"), check_vma=False
    )
```

```python
import math

import jax
import jax.numpy as jnp
import ml_dtypes
import numpy as np
from jax import lax
from jax.experimental import pallas as pl
from jax.experimental.pallas import tpu as pltpu
from jax.sharding import PartitionSpec as P

meridional_scale = 0.25
SLABS = 3
SLAB = 120
POINTS = 48
ROWS = 8 * SLABS
GROUPS = 3


def mode_layout(circle, kmax):
    table = np.zeros((GROUPS, 256, 256), np.float64)
    reduced = np.full((GROUPS, 256), 1 << 20, np.int32)
    scale = np.zeros((GROUPS, 256), np.float64)
    b = np.arange(SLAB)
    sign = np.where(b % 2 == 0, 1.0, -1.0)
    for residue in range(POINTS // 2):
        group, place = divmod(residue, 8)
        if residue == 0:
            waves = [(48 * n, 0) for n in range(1, 8)] + [(24 + 48 * n, 128) for n in range(8)]
            factor = 2.0 / circle
        else:
            waves = [(residue + 48 * n, None) for n in range(-8, 8) if abs(residue + 48 * n) <= kmax]
            factor = 1.0 / circle
        for t, (k, row) in enumerate(waves):
            angle = 2.0 * np.pi * ((k * b) % circle) / circle
            cosine, sine = sign * np.cos(angle), sign * np.sin(angle)
            re, im = 32 * place + t, 32 * place + 16 + t
            if row is None:
                table[group, :SLAB, re], table[group, 128 : 128 + SLAB, re] = cosine, sine
                table[group, :SLAB, im], table[group, 128 : 128 + SLAB, im] = -sine, cosine
            else:
                table[group, row : row + SLAB, re] = cosine
                table[group, row : row + SLAB, im] = -sine
            reduced[group, [re, im]] = abs(k)
            scale[group, [re, im]] = factor
    high = table.astype(np.float32).astype(ml_dtypes.bfloat16)
    low = (table - high.astype(np.float64)).astype(np.float32).astype(ml_dtypes.bfloat16)
    return high, low, reduced, scale.astype(np.float32)


def row_metrics(nlat, bands):
    ids = np.arange(nlat, dtype=np.float32)
    step = np.float32(math.pi / nlat)
    center = (ids + np.float32(0.5)) * step - np.float32(math.pi / 2)
    center = np.cos(center.astype(np.float64)).astype(np.float32)
    result = np.zeros((nlat, 128), np.float32)
    result[:, 0] = np.float32(math.sin(math.pi / (2 * nlat))) / center
    result[:, 1] = np.float32(meridional_scale) / center
    result[:, 2] = np.sin(((ids + np.float32(1.0)) * step).astype(np.float64))
    result[:, 3] = np.sin((ids * step).astype(np.float64))
    result[:, 4] = np.arange(nlat) // (nlat // bands) % 2
    return result.reshape(bands, nlat // bands, 128)


def c_add(x, y):
    return (x[0] + y[0], y[1] if x[1] is None else x[1] if y[1] is None else x[1] + y[1])


def c_sub(x, y):
    if y[1] is None:
        return (x[0] - y[0], x[1])
    return (x[0] - y[0], -y[1] if x[1] is None else x[1] - y[1])


def c_conj(x):
    return (x[0], None if x[1] is None else -x[1])


def c_turn(x, numer, denom):
    numer %= denom
    eighth = 8 * numer
    if numer == 0:
        return x
    if 2 * numer == denom:
        return (-x[0], None if x[1] is None else -x[1])
    if 4 * numer == denom:
        return (jnp.zeros_like(x[0]) if x[1] is None else -x[1], x[0])
    if 4 * numer == 3 * denom:
        return (jnp.zeros_like(x[0]) if x[1] is None else x[1], -x[0])
    angle = 2.0 * math.pi * numer / denom
    c, s = math.cos(angle), math.sin(angle)
    if x[1] is None:
        return (x[0] * c, x[0] * s)
    if eighth in (denom, 3 * denom, 5 * denom, 7 * denom):
        h = math.sqrt(0.5)
        a, b = (x[0] - x[1]) * h, (x[0] + x[1]) * h
        return {1: (a, b), 3: (-b, a), 5: (-a, -b), 7: (b, -a)}[eighth // denom]
    return (x[0] * c - x[1] * s, x[0] * s + x[1] * c)


def rfft(x):
    count = len(x)
    if count == 1:
        return [(x[0], None)]
    if count == 2:
        return [(x[0] + x[1], None), (x[0] - x[1], None)]
    even, odd = rfft(x[0::2]), rfft(x[1::2])
    result = [None] * (count // 2 + 1)
    for k in range(count // 4 + 1):
        turned = c_turn(odd[k], -k, count)
        result[k] = c_add(even[k], turned)
        if k != count // 4 or count == 2:
            result[count // 2 - k] = c_conj(c_sub(even[k], turned))
    return result


def irfft(z):
    count = 2 * (len(z) - 1)
    if count == 2:
        return [z[0][0] + z[1][0], z[0][0] - z[1][0]]
    even, odd = [], []
    for k in range(count // 4 + 1):
        mirror = c_conj(z[count // 2 - k])
        even.append(c_add(z[k], mirror))
        odd.append(c_turn(c_sub(z[k], mirror), k, count))
    result = [None] * count
    result[0::2], result[1::2] = irfft(even), irfft(odd)
    return result


def circle_forward(x):
    parts = [rfft(x[a::3]) for a in range(3)]
    result = [None] * 25
    half, root = 0.5, math.sqrt(3.0) / 2.0
    for k in range(9):
        t0 = parts[0][k]
        t1, t2 = c_turn(parts[1][k], -k, 48), c_turn(parts[2][k], -2 * k, 48)
        total, gap = c_add(t1, t2), c_sub(t1, t2)
        result[k] = c_add(t0, total)
        mid = (t0[0] - half * total[0], None if t0[1] is None and total[1] is None else
               (t0[1] if total[1] is None else (0.0 if t0[1] is None else t0[1]) - half * total[1]))
        turn = (None if gap[1] is None else root * gap[1], -root * gap[0])
        plus_re = mid[0] if turn[0] is None else mid[0] + turn[0]
        plus_im = turn[1] if mid[1] is None else mid[1] + turn[1]
        minus_re = mid[0] if turn[0] is None else mid[0] - turn[0]
        minus_im = -turn[1] if mid[1] is None else mid[1] - turn[1]
        if k + 16 <= 24:
            result[k + 16] = (plus_re, plus_im)
        if k > 0 and 16 - k != k + 16 and result[16 - k] is None:
            result[16 - k] = (minus_re, -minus_im)
    return result


def circle_backward(z):
    half, root = 0.5, math.sqrt(3.0) / 2.0
    spectra = [[], [], []]
    for k in range(9):
        t0 = z[k]
        t1 = z[k + 16] if k + 16 <= 24 else c_conj(z[32 - k])
        t2 = c_conj(z[16 - k])
        total, gap = c_add(t1, t2), c_sub(t1, t2)
        if k == 0:
            total, gap = (2.0 * t1[0], None), (None, 2.0 * t1[1])
        spectra[0].append(c_add(t0, total))
        mid = (t0[0] - half * total[0],
               t0[1] if total[1] is None else (-half * total[1] if t0[1] is None else t0[1] - half * total[1]))
        turn = (-root * gap[1], None if gap[0] is None else root * gap[0])
        plus = c_add(mid, turn)
        minus = c_sub(mid, turn)
        spectra[1].append(c_turn(plus, k, 48))
        spectra[2].append(c_turn(minus, 2 * k, 48))
    result = [None] * 48
    for a in range(3):
        result[a::3] = irfft(spectra[a])
    return result


def slabs_of(part):
    lane = lax.broadcasted_iota(jnp.int32, (part.shape[0], 128), 1)
    v0, v1, v2 = part[:, :128], part[:, 128:256], part[:, 256:]
    return (
        v0,
        jnp.where(lane < 8, pltpu.roll(v0, 8, 1), pltpu.roll(v1, 8, 1)),
        jnp.where(lane < 16, pltpu.roll(v1, 16, 1), pltpu.roll(v2, 16, 1)),
    )


def border_kernel(state_in, zonal_in, merid_in, near, far, state, zonal, merid, pad, sems):
    fields, rows, cells = state.shape
    copies = [
        pltpu.make_async_copy(source, target, sems.at[i])
        for i, (source, target) in enumerate(((state_in, state), (merid_in, merid), (zonal_in, zonal)))
    ]
    for copy in copies:
        copy.start()
    pad[...] = jnp.zeros(pad.shape, jnp.float32)
    for copy in copies:
        copy.wait()
    for f in range(fields):
        pad[0, f : f + 1, :cells] = state[f, rows - 1 :, :]
        pad[1, f : f + 1, :cells] = state[f, :1, :]
    pad[0, fields : fields + 1, :cells] = merid[rows - 1 :, :]
    odd = lax.axis_index("lat") % 2 == 1
    for a, (top, bottom) in enumerate(zip(slabs_of(pad[0]), slabs_of(pad[1]))):
        near[8 * a : 8 * a + 8, :] = jnp.where(odd, bottom, top)
        far[8 * a : 8 * a + 8, :] = jnp.where(odd, top, bottom)


def increment_kernel(
    state, zonal, merid, reduced, scale, table, flags, counts,
    chunks, metric, own, pad, flags_here, counts_here, sems,
):
    fields, rows, cells = state.shape
    wide = 128 * SLABS
    band, sector = lax.axis_index("lat"), lax.axis_index("lon")
    copies = [
        pltpu.make_async_copy(table.at[band], metric, sems.at[0]),
        pltpu.make_async_copy(flags, flags_here, sems.at[1]),
        pltpu.make_async_copy(counts, counts_here, sems.at[2]),
    ]
    for copy in copies:
        copy.start()
    for f in range(fields + 2):
        pad[f, :, wide - 128 :] = jnp.zeros((rows, 128), jnp.float32)
    for f in range(fields):
        pad[f, :, :cells] = state[f]
    pad[fields, :, :cells] = zonal[...]
    pad[fields + 1, :, :cells] = merid[...]
    lane = lax.broadcasted_iota(jnp.int32, (rows, wide), 1)
    row = lax.broadcasted_iota(jnp.int32, (rows, wide), 0)
    for copy in copies:
        copy.wait()

    def spread(index):
        return jnp.broadcast_to(metric[:, index : index + 1], (rows, wide))

    zonal_factor, merid_factor, face = (spread(i) for i in range(3))
    east_wind = pad[fields]
    last_wind = pltpu.roll(east_wind, 3, 1)
    inner_wind = jnp.where(lane < cells - 1, east_wind, 0.0)
    north_wind = jnp.where(row < rows - 1, pad[fields + 1] * face, 0.0)
    for f in range(fields):
        q = pad[f]
        flux_east = inner_wind * (0.5 * (q + pltpu.roll(q, wide - 1, 1)))
        zonal_diff = flux_east - pltpu.roll(flux_east, 1, 1)
        flux_north = north_wind * (0.5 * (q + pltpu.roll(q, rows - 1, 0)))
        merid_diff = flux_north - pltpu.roll(flux_north, 1, 0)
        part = -zonal_factor * zonal_diff - merid_factor * merid_diff
        part = jnp.where(lane == cells, pltpu.roll(q, cells, 1), part)
        part = jnp.where(lane == cells + 1, pltpu.roll(q, 2, 1), part)
        part = jnp.where(lane == cells + 2, last_wind, part)
        for a, slab in enumerate(slabs_of(part)):
            chunks[pl.ds(8 * a + f, rows, stride=ROWS), :] = slab
    for f in range(fields, 8):
        for a in range(SLABS):
            chunks[pl.ds(8 * a + f, rows, stride=ROWS), :] = jnp.zeros((rows, 128), jnp.float32)
    flag = flags_here[band * rows + sector].astype(jnp.float32)
    count = counts_here[band * rows + sector].astype(jnp.float32)
    raised = jnp.maximum(count + 1.0 - reduced[...], 0.0)
    own[:8, :] = raised / jnp.maximum(count, 1.0) * flag * scale[...]
    mine = jnp.where(row == sector, zonal_factor, 0.0)[:, :256]
    own[8:, :] = jnp.broadcast_to(jnp.sum(mine, axis=0, keepdims=True), (8, 256))


def border_fluxes_kernel(part, near, far, from_near, from_far, metric, chunks):
    fields, last, rows = 6, part.shape[0] - ROWS, metric.shape[0]
    inside = lax.broadcasted_iota(jnp.int32, (8, 128), 1) < SLAB

    def spread(row, index):
        return jnp.broadcast_to(metric[row : row + 1, index : index + 1], (8, 128))

    first_factor, last_factor = spread(0, 1), spread(rows - 1, 1)
    first_face, last_face = spread(0, 3), spread(rows - 1, 2)
    odd = spread(0, 4) > 0.5
    chunks[...] = part[...]
    for a in range(SLABS):
        here = slice(8 * a, 8 * a + 8)
        mine, next_chip = near[here, :], far[here, :]
        top, bottom = jnp.where(odd, next_chip, mine), jnp.where(odd, mine, next_chip)
        mine, next_chip = from_near[here, :], from_far[here, :]
        north, south = jnp.where(odd, next_chip, mine), jnp.where(odd, mine, next_chip)
        flux = (south[fields : fields + 1, :] * first_face) * (0.5 * (south + bottom))
        chunks[here, :] = part[here, :] + jnp.where(inside, first_factor * flux, 0.0)
        flux = (top[fields : fields + 1, :] * last_face) * (0.5 * (top + north))
        there = slice(last + 8 * a, last + 8 * a + 8)
        chunks[there, :] = part[there, :] - jnp.where(inside, last_factor * flux, 0.0)


def split(x):
    high = x.astype(jnp.bfloat16)
    return high, (x - high.astype(jnp.float32)).astype(jnp.bfloat16)


def product(x, high, low, dims):
    def dot(p, q):
        return lax.dot_general(p, q, (dims, ((), ())), preferred_element_type=jnp.float32)

    x_high, x_low = split(x)
    return dot(x_high, high) + (dot(x_low, high) + dot(x_high, low))


def filter_kernel(chunks, own, high, low, result):
    sectors = chunks.shape[0]
    lane = lax.broadcasted_iota(jnp.int32, (8, 128), 1)
    zonal_factor = own[8:, :128]
    points = [chunks[p // 3, 8 * (p % 3) : 8 * (p % 3) + 8, :] for p in range(POINTS)]
    lasts = [points[3 * s + 2] for s in range(sectors)]
    for s in range(sectors):
        after = (s + 1) % sectors
        flux = pltpu.roll(lasts[s], 125, 1) * (
            0.5 * (pltpu.roll(lasts[s], 126, 1) + pltpu.roll(lasts[after], 127, 1))
        )
        edge = jnp.where(lane == SLAB - 1, zonal_factor * flux, 0.0)
        points[3 * s + 2] = points[3 * s + 2] - edge
        points[3 * after] = points[3 * after] + pltpu.roll(edge, 128 - (SLAB - 1), 1)
    for p in range(POINTS):
        result[p // 3, 8 * (p % 3) : 8 * (p % 3) + 8, :] = points[p]
    spectrum = circle_forward(points)
    spectrum[0] = (spectrum[0][0], spectrum[24][0])
    block = lax.broadcasted_iota(jnp.int32, (64, 256), 0) // 8
    column = lax.broadcasted_iota(jnp.int32, (64, 256), 1) // 32
    back = [None] * 25
    for g in range(GROUPS):
        rows = jnp.concatenate(
            [jnp.concatenate(spectrum[8 * g + i], axis=1) for i in range(8)], axis=0
        )
        modes = product(rows, high[g], low[g], ((1,), (0,)))
        modes = jnp.where(block == column, modes * own[g : g + 1, :], 0.0)
        rows = product(modes, high[g], low[g], ((1,), (1,)))
        for i in range(8):
            part = rows[8 * i : 8 * i + 8, :]
            back[8 * g + i] = (part[:, :128], part[:, 128:])
    back[24] = (back[0][1], None)
    back[0] = (back[0][0], None)
    correction = circle_backward(back)
    for p in range(POINTS):
        place = (p // 3, slice(8 * (p % 3), 8 * (p % 3) + 8), slice(None))
        result[place] = result[place] - correction[p]


def final_kernel(chunks, state, advanced):
    fields, rows, cells = state.shape
    lane = lax.broadcasted_iota(jnp.int32, (rows, 128), 1)
    for f in range(fields):
        s0, s1, s2 = (chunks[pl.ds(8 * a + f, rows, stride=ROWS), :] for a in range(SLABS))
        s1, s2 = pltpu.roll(s1, 120, 1), pltpu.roll(s2, 112, 1)
        advanced[f, :, :128] = state[f, :, :128] + jnp.where(lane < 120, s0, s1)
        advanced[f, :, 128:256] = state[f, :, 128:256] + jnp.where(lane < 112, s1, s2)
        advanced[f, :, 256:] = state[f, :, 256:] + s2[:, : cells - 256]


def call(kernel, name, outs, mebibytes, args, elsewhere=0, scratch=()):
    vmem = pl.BlockSpec(memory_space=pltpu.VMEM)
    stay = pl.BlockSpec(memory_space=pltpu.HBM)
    fixed = len(args) - elsewhere
    args = args[:fixed] + tuple(
        pltpu.with_memory_space_constraint(arg, pltpu.HBM) for arg in args[fixed:]
    )
    return pl.pallas_call(
        kernel,
        out_shape=[jax.ShapeDtypeStruct(shape, jnp.float32) for shape in outs],
        in_specs=[vmem] * fixed + [stay] * elsewhere,
        out_specs=[vmem] * len(outs),
        scratch_shapes=list(scratch),
        compiler_params=pltpu.CompilerParams(vmem_limit_bytes=mebibytes << 20),
        name=name,
    )(*args)


def body(state, zonal_wind, meridional_wind, filter_flag, mode_count):
    field_count, level_count, lat_cells, lon_cells = state.shape
    item_count = field_count * level_count
    band_total, sectors = lax.axis_size("lat"), lax.axis_size("lon")
    nlat, circle = lat_cells * band_total, lon_cells * sectors
    wide = 128 * SLABS
    fields = state.reshape(item_count, lat_cells, lon_cells)
    zonal, merid = (w.reshape(lat_cells, lon_cells) for w in (zonal_wind, meridional_wind))
    high, low, reduced, scale = mode_layout(circle, circle // 16)

    def eight(rows):
        return jnp.asarray(np.pad(rows.astype(np.float32), ((0, 8 - rows.shape[0]), (0, 0))))

    near, far, fields, zonal, merid = call(
        border_kernel,
        "borders",
        [(ROWS, 128)] * 2 + [fields.shape, zonal.shape, merid.shape],
        3,
        (fields, zonal, merid),
        3,
        [pltpu.VMEM((2, 8, wide), jnp.float32), pltpu.SemaphoreType.DMA((3,))],
    )
    from_near = lax.ppermute(near, "lat", [(i, i ^ 1) for i in range(band_total)])
    pairs = [(i, i + 1) for i in range(1, band_total - 1, 2)]
    from_far = lax.ppermute(far, "lat", pairs + [(target, source) for source, target in pairs])

    packed = (sectors * ROWS, 128)
    part, metric, own = call(
        increment_kernel,
        "increments",
        [packed, (lat_cells, 128), (16, 256)],
        4,
        (fields, zonal, merid, eight(reduced), eight(scale))
        + (jnp.asarray(row_metrics(nlat, band_total)), filter_flag, mode_count),
        3,
        [
            pltpu.VMEM((8, lat_cells, wide), jnp.float32),
            pltpu.SMEM(filter_flag.shape, jnp.int32),
            pltpu.SMEM(mode_count.shape, jnp.int32),
            pltpu.SemaphoreType.DMA((3,)),
        ],
    )
    (chunks,) = call(
        border_fluxes_kernel, "border_fluxes", [packed], 2, (part, near, far, from_near, from_far, metric)
    )
    chunks = lax.all_to_all(chunks.reshape(sectors, ROWS, 128), "lon", 0, 0, tiled=True)
    (chunks,) = call(
        filter_kernel,
        "filter_rows",
        [(sectors, ROWS, 128)],
        8,
        (chunks, own, jnp.asarray(high), jnp.asarray(low)),
    )
    chunks = lax.all_to_all(chunks, "lon", 0, 0, tiled=True)
    (advanced,) = call(final_kernel, "advance", [fields.shape], 4, (chunks.reshape(packed), fields))
    return advanced.reshape(state.shape)


def solution(mesh):
    placed = (P(None, None, "lat", "lon"), P(None, "lat", "lon"), P(None, "lat", "lon"), P(), P())
    return jax.shard_map(
        body, mesh=mesh, in_specs=placed, out_specs=P(None, None, "lat", "lon"), check_vma=False
    )
```

```python
import math

import jax
import jax.numpy as jnp
import ml_dtypes
import numpy as np
from jax import lax
from jax.experimental import pallas as pl
from jax.experimental.pallas import tpu as pltpu
from jax.sharding import PartitionSpec as P

meridional_scale = 0.25
SLABS = 3
SLAB = 120
POINTS = 48
ROWS = 8 * SLABS
GROUPS = 3


def mode_layout(circle, kmax):
    table = np.zeros((GROUPS, 256, 256), np.float64)
    reduced = np.full((GROUPS, 256), 1 << 20, np.int32)
    scale = np.zeros((GROUPS, 256), np.float64)
    b = np.arange(SLAB)
    sign = np.where(b % 2 == 0, 1.0, -1.0)
    for residue in range(POINTS // 2):
        group, place = divmod(residue, 8)
        if residue == 0:
            waves = [(48 * n, 0) for n in range(1, 8)] + [(24 + 48 * n, 128) for n in range(8)]
            factor = 2.0 / circle
        else:
            waves = [(residue + 48 * n, None) for n in range(-8, 8) if abs(residue + 48 * n) <= kmax]
            factor = 1.0 / circle
        for t, (k, row) in enumerate(waves):
            angle = 2.0 * np.pi * ((k * b) % circle) / circle
            cosine, sine = sign * np.cos(angle), sign * np.sin(angle)
            re, im = 32 * place + t, 32 * place + 16 + t
            if row is None:
                table[group, :SLAB, re], table[group, 128 : 128 + SLAB, re] = cosine, sine
                table[group, :SLAB, im], table[group, 128 : 128 + SLAB, im] = -sine, cosine
            else:
                table[group, row : row + SLAB, re] = cosine
                table[group, row : row + SLAB, im] = -sine
            reduced[group, [re, im]] = abs(k)
            scale[group, [re, im]] = factor
    high = table.astype(np.float32).astype(ml_dtypes.bfloat16)
    low = (table - high.astype(np.float64)).astype(np.float32).astype(ml_dtypes.bfloat16)
    return high, low, reduced, scale.astype(np.float32)


def row_metrics(nlat, bands):
    ids = np.arange(nlat, dtype=np.float32)
    step = np.float32(math.pi / nlat)
    center = (ids + np.float32(0.5)) * step - np.float32(math.pi / 2)
    center = np.cos(center.astype(np.float64)).astype(np.float32)
    result = np.zeros((nlat, 128), np.float32)
    result[:, 0] = np.float32(math.sin(math.pi / (2 * nlat))) / center
    result[:, 1] = np.float32(meridional_scale) / center
    result[:, 2] = np.sin(((ids + np.float32(1.0)) * step).astype(np.float64))
    result[:, 3] = np.sin((ids * step).astype(np.float64))
    result[:, 4] = np.arange(nlat) // (nlat // bands) % 2
    return result.reshape(bands, nlat // bands, 128)


def c_add(x, y):
    return (x[0] + y[0], y[1] if x[1] is None else x[1] if y[1] is None else x[1] + y[1])


def c_sub(x, y):
    if y[1] is None:
        return (x[0] - y[0], x[1])
    return (x[0] - y[0], -y[1] if x[1] is None else x[1] - y[1])


def c_conj(x):
    return (x[0], None if x[1] is None else -x[1])


def c_turn(x, numer, denom):
    numer %= denom
    eighth = 8 * numer
    if numer == 0:
        return x
    if 2 * numer == denom:
        return (-x[0], None if x[1] is None else -x[1])
    if 4 * numer == denom:
        return (jnp.zeros_like(x[0]) if x[1] is None else -x[1], x[0])
    if 4 * numer == 3 * denom:
        return (jnp.zeros_like(x[0]) if x[1] is None else x[1], -x[0])
    angle = 2.0 * math.pi * numer / denom
    c, s = math.cos(angle), math.sin(angle)
    if x[1] is None:
        return (x[0] * c, x[0] * s)
    if eighth in (denom, 3 * denom, 5 * denom, 7 * denom):
        h = math.sqrt(0.5)
        a, b = (x[0] - x[1]) * h, (x[0] + x[1]) * h
        return {1: (a, b), 3: (-b, a), 5: (-a, -b), 7: (b, -a)}[eighth // denom]
    return (x[0] * c - x[1] * s, x[0] * s + x[1] * c)


def rfft(x):
    count = len(x)
    if count == 1:
        return [(x[0], None)]
    if count == 2:
        return [(x[0] + x[1], None), (x[0] - x[1], None)]
    even, odd = rfft(x[0::2]), rfft(x[1::2])
    result = [None] * (count // 2 + 1)
    for k in range(count // 4 + 1):
        turned = c_turn(odd[k], -k, count)
        result[k] = c_add(even[k], turned)
        if k != count // 4 or count == 2:
            result[count // 2 - k] = c_conj(c_sub(even[k], turned))
    return result


def irfft(z):
    count = 2 * (len(z) - 1)
    if count == 2:
        return [z[0][0] + z[1][0], z[0][0] - z[1][0]]
    even, odd = [], []
    for k in range(count // 4 + 1):
        mirror = c_conj(z[count // 2 - k])
        even.append(c_add(z[k], mirror))
        odd.append(c_turn(c_sub(z[k], mirror), k, count))
    result = [None] * count
    result[0::2], result[1::2] = irfft(even), irfft(odd)
    return result


def circle_forward(x):
    parts = [rfft(x[a::3]) for a in range(3)]
    result = [None] * 25
    half, root = 0.5, math.sqrt(3.0) / 2.0
    for k in range(9):
        t0 = parts[0][k]
        t1, t2 = c_turn(parts[1][k], -k, 48), c_turn(parts[2][k], -2 * k, 48)
        total, gap = c_add(t1, t2), c_sub(t1, t2)
        result[k] = c_add(t0, total)
        mid = (t0[0] - half * total[0], None if t0[1] is None and total[1] is None else
               (t0[1] if total[1] is None else (0.0 if t0[1] is None else t0[1]) - half * total[1]))
        turn = (None if gap[1] is None else root * gap[1], -root * gap[0])
        plus_re = mid[0] if turn[0] is None else mid[0] + turn[0]
        plus_im = turn[1] if mid[1] is None else mid[1] + turn[1]
        minus_re = mid[0] if turn[0] is None else mid[0] - turn[0]
        minus_im = -turn[1] if mid[1] is None else mid[1] - turn[1]
        if k + 16 <= 24:
            result[k + 16] = (plus_re, plus_im)
        if k > 0 and 16 - k != k + 16 and result[16 - k] is None:
            result[16 - k] = (minus_re, -minus_im)
    return result


def circle_backward(z):
    half, root = 0.5, math.sqrt(3.0) / 2.0
    spectra = [[], [], []]
    for k in range(9):
        t0 = z[k]
        t1 = z[k + 16] if k + 16 <= 24 else c_conj(z[32 - k])
        t2 = c_conj(z[16 - k])
        total, gap = c_add(t1, t2), c_sub(t1, t2)
        if k == 0:
            total, gap = (2.0 * t1[0], None), (None, 2.0 * t1[1])
        spectra[0].append(c_add(t0, total))
        mid = (t0[0] - half * total[0],
               t0[1] if total[1] is None else (-half * total[1] if t0[1] is None else t0[1] - half * total[1]))
        turn = (-root * gap[1], None if gap[0] is None else root * gap[0])
        plus = c_add(mid, turn)
        minus = c_sub(mid, turn)
        spectra[1].append(c_turn(plus, k, 48))
        spectra[2].append(c_turn(minus, 2 * k, 48))
    result = [None] * 48
    for a in range(3):
        result[a::3] = irfft(spectra[a])
    return result


def slabs_of(part):
    lane = lax.broadcasted_iota(jnp.int32, (part.shape[0], 128), 1)
    v0, v1, v2 = part[:, :128], part[:, 128:256], part[:, 256:]
    return (
        v0,
        jnp.where(lane < 8, pltpu.roll(v0, 8, 1), pltpu.roll(v1, 8, 1)),
        jnp.where(lane < 16, pltpu.roll(v1, 16, 1), pltpu.roll(v2, 16, 1)),
    )


def border_kernel(
    state_in, zonal_in, merid_in, table, flags_in, counts_in,
    far, near, top, bottom, state, zonal, merid, metric, flags, counts, pad, sems,
):
    fields, rows, cells = state.shape
    band = lax.axis_index("lat")
    sources = (state_in, merid_in, zonal_in, table.at[band], flags_in, counts_in)
    targets = (state, merid, zonal, metric, flags, counts)
    copies = [
        pltpu.make_async_copy(source, target, sems.at[i])
        for i, (source, target) in enumerate(zip(sources, targets))
    ]
    for copy in copies:
        copy.start()
    pad[...] = jnp.zeros(pad.shape, jnp.float32)
    for copy in copies:
        copy.wait()
    for f in range(fields):
        pad[0, f : f + 1, :cells] = state[f, rows - 1 :, :]
        pad[1, f : f + 1, :cells] = state[f, :1, :]
    pad[0, fields : fields + 1, :cells] = merid[rows - 1 :, :]
    odd = band % 2 == 1
    for a, (last, first) in enumerate(zip(slabs_of(pad[0]), slabs_of(pad[1]))):
        here = slice(8 * a, 8 * a + 8)
        top[here, :], bottom[here, :] = last, first
        far[here, :] = jnp.where(odd, last, first)
        near[here, :] = jnp.where(odd, first, last)


def increment_kernel(
    state, zonal, merid, metric, flags, counts, reduced, scale, chunks, own, pad
):
    fields, rows, cells = state.shape
    wide = 128 * SLABS
    band, sector = lax.axis_index("lat"), lax.axis_index("lon")
    for f in range(fields + 2):
        pad[f, :, wide - 128 :] = jnp.zeros((rows, 128), jnp.float32)
    for f in range(fields):
        pad[f, :, :cells] = state[f]
    pad[fields, :, :cells] = zonal[...]
    pad[fields + 1, :, :cells] = merid[...]
    lane = lax.broadcasted_iota(jnp.int32, (rows, wide), 1)
    row = lax.broadcasted_iota(jnp.int32, (rows, wide), 0)

    def spread(index):
        return jnp.broadcast_to(metric[:, index : index + 1], (rows, wide))

    zonal_factor, merid_factor, face = (spread(i) for i in range(3))
    east_wind = pad[fields]
    last_wind = pltpu.roll(east_wind, 3, 1)
    inner_wind = jnp.where(lane < cells - 1, east_wind, 0.0)
    north_wind = jnp.where(row < rows - 1, pad[fields + 1] * face, 0.0)
    for f in range(fields):
        q = pad[f]
        flux_east = inner_wind * (0.5 * (q + pltpu.roll(q, wide - 1, 1)))
        zonal_diff = flux_east - pltpu.roll(flux_east, 1, 1)
        flux_north = north_wind * (0.5 * (q + pltpu.roll(q, rows - 1, 0)))
        merid_diff = flux_north - pltpu.roll(flux_north, 1, 0)
        part = -zonal_factor * zonal_diff - merid_factor * merid_diff
        part = jnp.where(lane == cells, pltpu.roll(q, cells, 1), part)
        part = jnp.where(lane == cells + 1, pltpu.roll(q, 2, 1), part)
        part = jnp.where(lane == cells + 2, last_wind, part)
        for a, slab in enumerate(slabs_of(part)):
            chunks[pl.ds(8 * a + f, rows, stride=ROWS), :] = slab
    for f in range(fields, 8):
        for a in range(SLABS):
            chunks[pl.ds(8 * a + f, rows, stride=ROWS), :] = jnp.zeros((rows, 128), jnp.float32)
    place = lax.broadcasted_iota(jnp.int32, flags.shape, 0) * 128 + lax.broadcasted_iota(jnp.int32, flags.shape, 1)
    chosen = place == band * rows + sector

    def pick(values):
        picked = jnp.where(chosen, values[...].astype(jnp.float32), 0.0)
        return jnp.sum(jnp.sum(picked, axis=1, keepdims=True), axis=0, keepdims=True)

    flag, count = pick(flags), pick(counts)
    raised = jnp.maximum(count + 1.0 - reduced[...], 0.0)
    own[:8, :] = raised / jnp.maximum(count, 1.0) * flag * scale[...]
    mine = jnp.where(row == sector, zonal_factor, 0.0)[:, :256]
    own[8:, :] = jnp.broadcast_to(jnp.sum(mine, axis=0, keepdims=True), (8, 256))


def border_fluxes_kernel(part, top_in, bottom_in, both, from_far, metric, chunks):
    fields, last, rows = 6, part.shape[0] - ROWS, metric.shape[0]
    inside = lax.broadcasted_iota(jnp.int32, (8, 128), 1) < SLAB

    def spread(row, index):
        return jnp.broadcast_to(metric[row : row + 1, index : index + 1], (8, 128))

    first_factor, last_factor = spread(0, 1), spread(rows - 1, 1)
    first_face, last_face = spread(0, 3), spread(rows - 1, 2)
    odd = spread(0, 4) > 0.5
    chunks[...] = part[...]
    for a in range(SLABS):
        here = slice(8 * a, 8 * a + 8)
        top, bottom = top_in[here, :], bottom_in[here, :]
        mine, next_chip = jnp.where(odd, both[here, :], both[ROWS + 8 * a : ROWS + 8 * a + 8, :]), from_far[here, :]
        north, south = jnp.where(odd, next_chip, mine), jnp.where(odd, mine, next_chip)
        flux = (south[fields : fields + 1, :] * first_face) * (0.5 * (south + bottom))
        chunks[here, :] = part[here, :] + jnp.where(inside, first_factor * flux, 0.0)
        flux = (top[fields : fields + 1, :] * last_face) * (0.5 * (top + north))
        there = slice(last + 8 * a, last + 8 * a + 8)
        chunks[there, :] = part[there, :] - jnp.where(inside, last_factor * flux, 0.0)


def split(x):
    high = x.astype(jnp.bfloat16)
    return high, (x - high.astype(jnp.float32)).astype(jnp.bfloat16)


def product(x, high, low, dims):
    def dot(p, q):
        return lax.dot_general(p, q, (dims, ((), ())), preferred_element_type=jnp.float32)

    x_high, x_low = split(x)
    return dot(x_high, high) + (dot(x_low, high) + dot(x_high, low))


def filter_kernel(chunks, own, high, low, result):
    sectors = chunks.shape[0]
    lane = lax.broadcasted_iota(jnp.int32, (8, 128), 1)
    zonal_factor = own[8:, :128]
    points = [chunks[p // 3, 8 * (p % 3) : 8 * (p % 3) + 8, :] for p in range(POINTS)]
    lasts = [points[3 * s + 2] for s in range(sectors)]
    for s in range(sectors):
        after = (s + 1) % sectors
        flux = pltpu.roll(lasts[s], 125, 1) * (
            0.5 * (pltpu.roll(lasts[s], 126, 1) + pltpu.roll(lasts[after], 127, 1))
        )
        edge = jnp.where(lane == SLAB - 1, zonal_factor * flux, 0.0)
        points[3 * s + 2] = points[3 * s + 2] - edge
        points[3 * after] = points[3 * after] + pltpu.roll(edge, 128 - (SLAB - 1), 1)
    for p in range(POINTS):
        result[p // 3, 8 * (p % 3) : 8 * (p % 3) + 8, :] = points[p]
    spectrum = circle_forward(points)
    spectrum[0] = (spectrum[0][0], spectrum[24][0])
    block = lax.broadcasted_iota(jnp.int32, (64, 256), 0) // 8
    column = lax.broadcasted_iota(jnp.int32, (64, 256), 1) // 32
    back = [None] * 25
    for g in range(GROUPS):
        rows = jnp.concatenate(
            [jnp.concatenate(spectrum[8 * g + i], axis=1) for i in range(8)], axis=0
        )
        modes = product(rows, high[g], low[g], ((1,), (0,)))
        modes = jnp.where(block == column, modes * own[g : g + 1, :], 0.0)
        rows = product(modes, high[g], low[g], ((1,), (1,)))
        for i in range(8):
            part = rows[8 * i : 8 * i + 8, :]
            back[8 * g + i] = (part[:, :128], part[:, 128:])
    back[24] = (back[0][1], None)
    back[0] = (back[0][0], None)
    correction = circle_backward(back)
    for p in range(POINTS):
        place = (p // 3, slice(8 * (p % 3), 8 * (p % 3) + 8), slice(None))
        result[place] = result[place] - correction[p]


def final_kernel(chunks, state, advanced):
    fields, rows, cells = state.shape
    lane = lax.broadcasted_iota(jnp.int32, (rows, 128), 1)
    for f in range(fields):
        s0, s1, s2 = (chunks[pl.ds(8 * a + f, rows, stride=ROWS), :] for a in range(SLABS))
        s1, s2 = pltpu.roll(s1, 120, 1), pltpu.roll(s2, 112, 1)
        advanced[f, :, :128] = state[f, :, :128] + jnp.where(lane < 120, s0, s1)
        advanced[f, :, 128:256] = state[f, :, 128:256] + jnp.where(lane < 112, s1, s2)
        advanced[f, :, 256:] = state[f, :, 256:] + s2[:, : cells - 256]


def floats(*shape):
    return jax.ShapeDtypeStruct(shape, jnp.float32)


def call(kernel, name, outs, mebibytes, args, elsewhere=0, scratch=()):
    vmem = pl.BlockSpec(memory_space=pltpu.VMEM)
    stay = pl.BlockSpec(memory_space=pltpu.HBM)
    fixed = len(args) - elsewhere
    args = args[:fixed] + tuple(
        pltpu.with_memory_space_constraint(arg, pltpu.HBM) for arg in args[fixed:]
    )
    return pl.pallas_call(
        kernel,
        out_shape=[jax.ShapeDtypeStruct(out.shape, out.dtype) for out in outs],
        in_specs=[vmem] * fixed + [stay] * elsewhere,
        out_specs=[vmem] * len(outs),
        scratch_shapes=list(scratch),
        compiler_params=pltpu.CompilerParams(vmem_limit_bytes=mebibytes << 20),
        name=name,
    )(*args)


def body(state, zonal_wind, meridional_wind, filter_flag, mode_count):
    field_count, level_count, lat_cells, lon_cells = state.shape
    item_count = field_count * level_count
    band_total, sectors = lax.axis_size("lat"), lax.axis_size("lon")
    nlat, circle = lat_cells * band_total, lon_cells * sectors
    wide = 128 * SLABS
    fields = state.reshape(item_count, lat_cells, lon_cells)
    zonal, merid = (w.reshape(lat_cells, lon_cells) for w in (zonal_wind, meridional_wind))
    high, low, reduced, scale = mode_layout(circle, circle // 16)

    def eight(rows):
        return jnp.asarray(np.pad(rows.astype(np.float32), ((0, 8 - rows.shape[0]), (0, 0))))

    flags, counts = filter_flag.reshape(-1, 128), mode_count.reshape(-1, 128)
    border = floats(ROWS, 128)
    far, near, top, bottom, fields, zonal, merid, metric, flags, counts = call(
        border_kernel,
        "borders",
        [border, border, border, border, fields, zonal, merid, floats(lat_cells, 128), flags, counts],
        3,
        (fields, zonal, merid, jnp.asarray(row_metrics(nlat, band_total)), flags, counts),
        6,
        [pltpu.VMEM((2, 8, wide), jnp.float32), pltpu.SemaphoreType.DMA((6,))],
    )
    pairs = [(i, i + 1) for i in range(1, band_total - 1, 2)]
    from_far = lax.ppermute(far, "lat", pairs + [(target, source) for source, target in pairs])
    chips = [[i, i + 1] for i in range(0, band_total, 2)]
    both = lax.all_gather(near, "lat", axis=0, tiled=True, axis_index_groups=chips)

    packed = (sectors * ROWS, 128)
    part, own = call(
        increment_kernel,
        "increments",
        [floats(*packed), floats(16, 256)],
        4,
        (fields, zonal, merid, metric, flags, counts, eight(reduced), eight(scale)),
        0,
        [pltpu.VMEM((8, lat_cells, wide), jnp.float32)],
    )
    (chunks,) = call(
        border_fluxes_kernel,
        "border_fluxes",
        [floats(*packed)],
        2,
        (part, top, bottom, both, from_far, metric),
    )
    chunks = lax.all_to_all(chunks.reshape(sectors, ROWS, 128), "lon", 0, 0, tiled=True)
    (chunks,) = call(
        filter_kernel,
        "filter_rows",
        [floats(sectors, ROWS, 128)],
        8,
        (chunks, own, jnp.asarray(high), jnp.asarray(low)),
    )
    chunks = lax.all_to_all(chunks, "lon", 0, 0, tiled=True)
    (advanced,) = call(final_kernel, "advance", [fields], 4, (chunks.reshape(packed), fields))
    return advanced.reshape(state.shape)


def solution(mesh):
    placed = (P(None, None, "lat", "lon"), P(None, "lat", "lon"), P(None, "lat", "lon"), P(), P())
    return jax.shard_map(
        body, mesh=mesh, in_specs=placed, out_specs=P(None, None, "lat", "lon"), check_vma=False
    )
```

```python
import math

import jax
import jax.numpy as jnp
import ml_dtypes
import numpy as np
from jax import lax
from jax.experimental import pallas as pl
from jax.experimental.pallas import tpu as pltpu
from jax.sharding import PartitionSpec as P

meridional_scale = 0.25
SLABS = 3
SLAB = 120
POINTS = 48
ROWS = 8 * SLABS
CHUNK = 6 * SLABS
GROUPS = 3


def mode_layout(circle, kmax):
    table = np.zeros((GROUPS, 256, 256), np.float64)
    reduced = np.full((GROUPS, 256), 1 << 20, np.int32)
    scale = np.zeros((GROUPS, 256), np.float64)
    b = np.arange(SLAB)
    sign = np.where(b % 2 == 0, 1.0, -1.0)
    for residue in range(POINTS // 2):
        group, place = divmod(residue, 8)
        if residue == 0:
            waves = [(48 * n, 0) for n in range(1, 8)] + [(24 + 48 * n, 128) for n in range(8)]
            factor = 2.0 / circle
        else:
            waves = [(residue + 48 * n, None) for n in range(-8, 8) if abs(residue + 48 * n) <= kmax]
            factor = 1.0 / circle
        for t, (k, row) in enumerate(waves):
            angle = 2.0 * np.pi * ((k * b) % circle) / circle
            cosine, sine = sign * np.cos(angle), sign * np.sin(angle)
            re, im = 32 * place + t, 32 * place + 16 + t
            if row is None:
                table[group, :SLAB, re], table[group, 128 : 128 + SLAB, re] = cosine, sine
                table[group, :SLAB, im], table[group, 128 : 128 + SLAB, im] = -sine, cosine
            else:
                table[group, row : row + SLAB, re] = cosine
                table[group, row : row + SLAB, im] = -sine
            reduced[group, [re, im]] = abs(k)
            scale[group, [re, im]] = factor
    high = table.astype(np.float32).astype(ml_dtypes.bfloat16)
    low = (table - high.astype(np.float64)).astype(np.float32).astype(ml_dtypes.bfloat16)
    return high, low, reduced, scale.astype(np.float32)


def row_metrics(nlat, bands):
    ids = np.arange(nlat, dtype=np.float32)
    step = np.float32(math.pi / nlat)
    center = (ids + np.float32(0.5)) * step - np.float32(math.pi / 2)
    center = np.cos(center.astype(np.float64)).astype(np.float32)
    result = np.zeros((nlat, 128), np.float32)
    result[:, 0] = np.float32(math.sin(math.pi / (2 * nlat))) / center
    result[:, 1] = np.float32(meridional_scale) / center
    result[:, 2] = np.sin(((ids + np.float32(1.0)) * step).astype(np.float64))
    result[:, 3] = np.sin((ids * step).astype(np.float64))
    result[:, 4] = np.arange(nlat) // (nlat // bands) % 2
    return result.reshape(bands, nlat // bands, 128)


def c_add(x, y):
    return (x[0] + y[0], y[1] if x[1] is None else x[1] if y[1] is None else x[1] + y[1])


def c_sub(x, y):
    if y[1] is None:
        return (x[0] - y[0], x[1])
    return (x[0] - y[0], -y[1] if x[1] is None else x[1] - y[1])


def c_conj(x):
    return (x[0], None if x[1] is None else -x[1])


def c_turn(x, numer, denom):
    numer %= denom
    eighth = 8 * numer
    if numer == 0:
        return x
    if 2 * numer == denom:
        return (-x[0], None if x[1] is None else -x[1])
    if 4 * numer == denom:
        return (jnp.zeros_like(x[0]) if x[1] is None else -x[1], x[0])
    if 4 * numer == 3 * denom:
        return (jnp.zeros_like(x[0]) if x[1] is None else x[1], -x[0])
    angle = 2.0 * math.pi * numer / denom
    c, s = math.cos(angle), math.sin(angle)
    if x[1] is None:
        return (x[0] * c, x[0] * s)
    if eighth in (denom, 3 * denom, 5 * denom, 7 * denom):
        h = math.sqrt(0.5)
        a, b = (x[0] - x[1]) * h, (x[0] + x[1]) * h
        return {1: (a, b), 3: (-b, a), 5: (-a, -b), 7: (b, -a)}[eighth // denom]
    return (x[0] * c - x[1] * s, x[0] * s + x[1] * c)


def rfft(x):
    count = len(x)
    if count == 1:
        return [(x[0], None)]
    if count == 2:
        return [(x[0] + x[1], None), (x[0] - x[1], None)]
    even, odd = rfft(x[0::2]), rfft(x[1::2])
    result = [None] * (count // 2 + 1)
    for k in range(count // 4 + 1):
        turned = c_turn(odd[k], -k, count)
        result[k] = c_add(even[k], turned)
        if k != count // 4 or count == 2:
            result[count // 2 - k] = c_conj(c_sub(even[k], turned))
    return result


def irfft(z):
    count = 2 * (len(z) - 1)
    if count == 2:
        return [z[0][0] + z[1][0], z[0][0] - z[1][0]]
    even, odd = [], []
    for k in range(count // 4 + 1):
        mirror = c_conj(z[count // 2 - k])
        even.append(c_add(z[k], mirror))
        odd.append(c_turn(c_sub(z[k], mirror), k, count))
    result = [None] * count
    result[0::2], result[1::2] = irfft(even), irfft(odd)
    return result


def circle_forward(x):
    parts = [rfft(x[a::3]) for a in range(3)]
    result = [None] * 25
    half, root = 0.5, math.sqrt(3.0) / 2.0
    for k in range(9):
        t0 = parts[0][k]
        t1, t2 = c_turn(parts[1][k], -k, 48), c_turn(parts[2][k], -2 * k, 48)
        total, gap = c_add(t1, t2), c_sub(t1, t2)
        result[k] = c_add(t0, total)
        mid = (t0[0] - half * total[0], None if t0[1] is None and total[1] is None else
               (t0[1] if total[1] is None else (0.0 if t0[1] is None else t0[1]) - half * total[1]))
        turn = (None if gap[1] is None else root * gap[1], -root * gap[0])
        plus_re = mid[0] if turn[0] is None else mid[0] + turn[0]
        plus_im = turn[1] if mid[1] is None else mid[1] + turn[1]
        minus_re = mid[0] if turn[0] is None else mid[0] - turn[0]
        minus_im = -turn[1] if mid[1] is None else mid[1] - turn[1]
        if k + 16 <= 24:
            result[k + 16] = (plus_re, plus_im)
        if k > 0 and 16 - k != k + 16 and result[16 - k] is None:
            result[16 - k] = (minus_re, -minus_im)
    return result


def circle_backward(z):
    half, root = 0.5, math.sqrt(3.0) / 2.0
    spectra = [[], [], []]
    for k in range(9):
        t0 = z[k]
        t1 = z[k + 16] if k + 16 <= 24 else c_conj(z[32 - k])
        t2 = c_conj(z[16 - k])
        total, gap = c_add(t1, t2), c_sub(t1, t2)
        if k == 0:
            total, gap = (2.0 * t1[0], None), (None, 2.0 * t1[1])
        spectra[0].append(c_add(t0, total))
        mid = (t0[0] - half * total[0],
               t0[1] if total[1] is None else (-half * total[1] if t0[1] is None else t0[1] - half * total[1]))
        turn = (-root * gap[1], None if gap[0] is None else root * gap[0])
        plus = c_add(mid, turn)
        minus = c_sub(mid, turn)
        spectra[1].append(c_turn(plus, k, 48))
        spectra[2].append(c_turn(minus, 2 * k, 48))
    result = [None] * 48
    for a in range(3):
        result[a::3] = irfft(spectra[a])
    return result


def slabs_of(part):
    lane = lax.broadcasted_iota(jnp.int32, (part.shape[0], 128), 1)
    v0, v1, v2 = part[:, :128], part[:, 128:256], part[:, 256:]
    return (
        v0,
        jnp.where(lane < 8, pltpu.roll(v0, 8, 1), pltpu.roll(v1, 8, 1)),
        jnp.where(lane < 16, pltpu.roll(v1, 16, 1), pltpu.roll(v2, 16, 1)),
    )


def border_kernel(
    state_in, zonal_in, merid_in, table, flags_in, counts_in, modes_in,
    far, near, top, bottom, state, zonal, merid, metric, flags, counts, modes, chunks, own, pad, sems,
):
    fields, rows, cells = state.shape
    band = lax.axis_index("lat")
    sources = (state_in, merid_in, zonal_in, table.at[band], flags_in, counts_in, modes_in)
    targets = (state, merid, zonal, metric, flags, counts, modes)
    copies = [
        pltpu.make_async_copy(source, target, sems.at[i])
        for i, (source, target) in enumerate(zip(sources, targets))
    ]
    for copy in copies:
        copy.start()
    pad[...] = jnp.zeros(pad.shape, jnp.float32)
    for copy in copies:
        copy.wait()
    for f in range(fields):
        pad[0, f : f + 1, :cells] = state[f, rows - 1 :, :]
        pad[1, f : f + 1, :cells] = state[f, :1, :]
    pad[0, fields : fields + 1, :cells] = merid[rows - 1 :, :]
    odd = band % 2 == 1
    for a, (last, first) in enumerate(zip(slabs_of(pad[0, :8, :]), slabs_of(pad[1, :8, :]))):
        here = slice(8 * a, 8 * a + 8)
        top[here, :], bottom[here, :] = last, first
        far[here, :] = jnp.where(odd, last, first)
        near[here, :] = jnp.where(odd, first, last)
    pl.when(odd)(lambda: increments(state, zonal, merid, metric, flags, counts, modes, chunks, own, pad))


def even_kernel(*refs):
    even = lax.axis_index("lat") % 2 == 0
    pl.when(even)(lambda: increments(*refs))


def increments(state, zonal, merid, metric, flags, counts, modes, chunks_out, own, pad):
    fields, rows, cells = state.shape
    wide = 128 * SLABS
    band, sector = lax.axis_index("lat"), lax.axis_index("lon")
    chunks = chunks_out.reshape(rows * CHUNK, 128)
    for f in range(fields + 2):
        pad[f, :, wide - 128 :] = jnp.zeros((rows, 128), jnp.float32)
    for f in range(fields):
        pad[f, :, :cells] = state[f]
    pad[fields, :, :cells] = zonal[...]
    pad[fields + 1, :, :cells] = merid[...]
    lane = lax.broadcasted_iota(jnp.int32, (rows, wide), 1)
    row = lax.broadcasted_iota(jnp.int32, (rows, wide), 0)

    def spread(index):
        return jnp.broadcast_to(metric[:, index : index + 1], (rows, wide))

    zonal_factor, merid_factor, face = (spread(i) for i in range(3))
    east_wind = pad[fields]
    last_wind = pltpu.roll(east_wind, 3, 1)
    inner_wind = jnp.where(lane < cells - 1, east_wind, 0.0)
    north_wind = jnp.where(row < rows - 1, pad[fields + 1] * face, 0.0)
    for f in range(fields):
        q = pad[f]
        flux_east = inner_wind * (0.5 * (q + pltpu.roll(q, wide - 1, 1)))
        zonal_diff = flux_east - pltpu.roll(flux_east, 1, 1)
        flux_north = north_wind * (0.5 * (q + pltpu.roll(q, rows - 1, 0)))
        merid_diff = flux_north - pltpu.roll(flux_north, 1, 0)
        part = -zonal_factor * zonal_diff - merid_factor * merid_diff
        part = jnp.where(lane == cells, pltpu.roll(q, cells, 1), part)
        part = jnp.where(lane == cells + 1, pltpu.roll(q, 2, 1), part)
        part = jnp.where(lane == cells + 2, last_wind, part)
        for a, slab in enumerate(slabs_of(part)):
            chunks[pl.ds(fields * a + f, rows, stride=CHUNK), :] = slab
    place = lax.broadcasted_iota(jnp.int32, flags.shape, 0) * 128 + lax.broadcasted_iota(jnp.int32, flags.shape, 1)
    chosen = place == band * rows + sector

    def pick(values):
        picked = jnp.where(chosen, values[...].astype(jnp.float32), 0.0)
        return jnp.sum(jnp.sum(picked, axis=1, keepdims=True), axis=0, keepdims=True)

    flag, count = pick(flags), pick(counts)
    raised = jnp.maximum(count + 1.0 - modes[:8, :], 0.0)
    own[:8, :] = raised / jnp.maximum(count, 1.0) * flag * modes[8:, :]
    mine = jnp.where(row == sector, zonal_factor, 0.0)[:, :256]
    own[8:, :] = jnp.broadcast_to(jnp.sum(mine, axis=0, keepdims=True), (8, 256))


def border_fluxes_kernel(
    odd_part, even_part, odd_own, even_own, top_in, bottom_in, both, from_far, metric, chunks_out, own
):
    fields, rows = 6, metric.shape[0]
    inside = lax.broadcasted_iota(jnp.int32, (8, 128), 1) < SLAB

    def spread(row, index):
        return jnp.broadcast_to(metric[row : row + 1, index : index + 1], (8, 128))

    first_factor, last_factor = spread(0, 1), spread(rows - 1, 1)
    first_face, last_face = spread(0, 3), spread(rows - 1, 2)
    odd = spread(0, 4) > 0.5
    chunks = chunks_out.reshape(rows * CHUNK, 128)
    is_odd = lax.axis_index("lat") % 2 == 1

    @pl.when(is_odd)
    def _():
        chunks_out[...] = odd_part[...]
        own[...] = odd_own[...]

    @pl.when(jnp.logical_not(is_odd))
    def _():
        chunks_out[...] = even_part[...]
        own[...] = even_own[...]

    for a in range(SLABS):
        here = slice(8 * a, 8 * a + 8)
        top, bottom = top_in[here, :], bottom_in[here, :]
        other = jnp.where(odd, both[here, :], both[ROWS + 8 * a : ROWS + 8 * a + 8, :])
        next_chip = from_far[here, :]
        north, south = jnp.where(odd, next_chip, other), jnp.where(odd, other, next_chip)
        flux = (south[fields : fields + 1, :] * first_face) * (0.5 * (south + bottom))
        flux = jnp.where(inside, first_factor * flux, 0.0)
        there = slice(fields * a, fields * (a + 1))
        chunks[there, :] = chunks[there, :] + flux[:fields]
        flux = (top[fields : fields + 1, :] * last_face) * (0.5 * (top + north))
        flux = jnp.where(inside, last_factor * flux, 0.0)
        there = slice((rows - 1) * CHUNK + fields * a, (rows - 1) * CHUNK + fields * (a + 1))
        chunks[there, :] = chunks[there, :] - flux[:fields]


def split(x):
    high = x.astype(jnp.bfloat16)
    return high, (x - high.astype(jnp.float32)).astype(jnp.bfloat16)


def product(x, high, low, dims):
    def dot(p, q):
        return lax.dot_general(p, q, (dims, ((), ())), preferred_element_type=jnp.float32)

    x_high, x_low = split(x)
    both = dot(jnp.concatenate([x_high, x_low], axis=0), high)
    return both[: x.shape[0]] + (both[x.shape[0] :] + dot(x_high, low))


def filter_kernel(chunks_in, own, high, low, result_out):
    sectors, fields = chunks_in.shape[0], 6
    chunks = chunks_in.reshape(sectors * CHUNK, 128)
    result = result_out.reshape(sectors * CHUNK, 128)
    lane = lax.broadcasted_iota(jnp.int32, (8, 128), 1)
    zonal_factor = own[8:, :128]
    points = [chunks[fields * p : fields * p + 8, :] for p in range(POINTS - 1)]
    points.append(pltpu.roll(chunks[sectors * CHUNK - 8 :, :], 6, 0))
    lasts = [points[3 * s + 2] for s in range(sectors)]
    for s in range(sectors):
        after = (s + 1) % sectors
        flux = pltpu.roll(lasts[s], 125, 1) * (
            0.5 * (pltpu.roll(lasts[s], 126, 1) + pltpu.roll(lasts[after], 127, 1))
        )
        edge = jnp.where(lane == SLAB - 1, zonal_factor * flux, 0.0)
        points[3 * s + 2] = points[3 * s + 2] - edge
        points[3 * after] = points[3 * after] + pltpu.roll(edge, 128 - (SLAB - 1), 1)
    for p in range(POINTS):
        result[fields * p : fields * (p + 1), :] = points[p][:fields]
    spectrum = circle_forward(points)
    spectrum[0] = (spectrum[0][0], spectrum[24][0])
    block = lax.broadcasted_iota(jnp.int32, (64, 256), 0) // 8
    column = lax.broadcasted_iota(jnp.int32, (64, 256), 1) // 32
    back = [None] * 25
    for g in range(GROUPS):
        rows = jnp.concatenate(
            [jnp.concatenate(spectrum[8 * g + i], axis=1) for i in range(8)], axis=0
        )
        modes = product(rows, high[g], low[g], ((1,), (0,)))
        modes = jnp.where(block == column, modes * own[g : g + 1, :], 0.0)
        rows = product(modes, high[g], low[g], ((1,), (1,)))
        for i in range(8):
            part = rows[8 * i : 8 * i + 8, :]
            back[8 * g + i] = (part[:, :128], part[:, 128:])
    back[24] = (back[0][1], None)
    back[0] = (back[0][0], None)
    correction = circle_backward(back)
    for p in range(POINTS):
        place = slice(fields * p, fields * (p + 1))
        result[place, :] = result[place, :] - correction[p][:fields]


def final_kernel(chunks_in, state, advanced):
    fields, rows, cells = state.shape
    chunks = chunks_in.reshape(rows * CHUNK, 128)
    lane = lax.broadcasted_iota(jnp.int32, (rows, 128), 1)
    for f in range(fields):
        s0, s1, s2 = (chunks[pl.ds(fields * a + f, rows, stride=CHUNK), :] for a in range(SLABS))
        s1, s2 = pltpu.roll(s1, 120, 1), pltpu.roll(s2, 112, 1)
        advanced[f, :, :128] = state[f, :, :128] + jnp.where(lane < 120, s0, s1)
        advanced[f, :, 128:256] = state[f, :, 128:256] + jnp.where(lane < 112, s1, s2)
        advanced[f, :, 256:] = state[f, :, 256:] + s2[:, : cells - 256]


def floats(*shape):
    return jax.ShapeDtypeStruct(shape, jnp.float32)


def call(kernel, name, outs, mebibytes, args, elsewhere=0, scratch=()):
    vmem = pl.BlockSpec(memory_space=pltpu.VMEM)
    stay = pl.BlockSpec(memory_space=pltpu.HBM)
    fixed = len(args) - elsewhere
    args = args[:fixed] + tuple(
        pltpu.with_memory_space_constraint(arg, pltpu.HBM) for arg in args[fixed:]
    )
    return pl.pallas_call(
        kernel,
        out_shape=[jax.ShapeDtypeStruct(out.shape, out.dtype) for out in outs],
        in_specs=[vmem] * fixed + [stay] * elsewhere,
        out_specs=[vmem] * len(outs),
        scratch_shapes=list(scratch),
        compiler_params=pltpu.CompilerParams(vmem_limit_bytes=mebibytes << 20),
        name=name,
    )(*args)


def body(state, zonal_wind, meridional_wind, filter_flag, mode_count):
    field_count, level_count, lat_cells, lon_cells = state.shape
    item_count = field_count * level_count
    band_total, sectors = lax.axis_size("lat"), lax.axis_size("lon")
    nlat, circle = lat_cells * band_total, lon_cells * sectors
    wide = 128 * SLABS
    fields = state.reshape(item_count, lat_cells, lon_cells)
    zonal, merid = (w.reshape(lat_cells, lon_cells) for w in (zonal_wind, meridional_wind))
    high, low, reduced, scale = mode_layout(circle, circle // 16)

    modes = np.concatenate([np.pad(rows, ((0, 8 - GROUPS), (0, 0))) for rows in (reduced, scale)])
    modes = jnp.asarray(modes.astype(np.float32))
    flags, counts = filter_flag.reshape(-1, 128), mode_count.reshape(-1, 128)
    border = floats(ROWS, 128)
    metric, own = floats(lat_cells, 128), floats(16, 256)
    packed = floats(sectors, CHUNK // 2, 2, 128)
    pad = pltpu.VMEM((8, lat_cells, wide), jnp.float32)
    here = (fields, zonal, merid, jnp.asarray(row_metrics(nlat, band_total)), flags, counts, modes)
    far, near, top, bottom, *here, odd_part, odd_own = call(
        border_kernel,
        "borders",
        [border] * 4 + [fields, zonal, merid, metric, flags, counts, modes, packed, own],
        4,
        here,
        7,
        [pad, pltpu.SemaphoreType.DMA((7,))],
    )
    fields, zonal, merid, metric = here[:4]
    pairs = [(i, i + 1) for i in range(1, band_total - 1, 2)]
    from_far = lax.ppermute(far, "lat", pairs + [(target, source) for source, target in pairs])
    chips = [[i, i + 1] for i in range(0, band_total, 2)]
    both = lax.all_gather(near, "lat", axis=0, tiled=True, axis_index_groups=chips)

    even_part, even_own = call(even_kernel, "even_increments", [packed, own], 4, tuple(here), 0, [pad])
    chunks, own = call(
        border_fluxes_kernel,
        "border_fluxes",
        [packed, own],
        4,
        (odd_part, even_part, odd_own, even_own, top, bottom, both, from_far, metric),
    )
    chunks = lax.all_to_all(chunks, "lon", 0, 0, tiled=True)
    (chunks,) = call(
        filter_kernel,
        "filter_rows",
        [packed],
        8,
        (chunks, own, jnp.asarray(high), jnp.asarray(low)),
    )
    chunks = lax.all_to_all(chunks, "lon", 0, 0, tiled=True)
    (advanced,) = call(final_kernel, "advance", [fields], 4, (chunks, fields))
    return advanced.reshape(state.shape)


def solution(mesh):
    placed = (P(None, None, "lat", "lon"), P(None, "lat", "lon"), P(None, "lat", "lon"), P(), P())
    return jax.shard_map(
        body, mesh=mesh, in_specs=placed, out_specs=P(None, None, "lat", "lon"), check_vma=False
    )
```

```python
import math

import jax
import jax.numpy as jnp
import ml_dtypes
import numpy as np
from jax import lax
from jax.experimental import pallas as pl
from jax.experimental.pallas import tpu as pltpu
from jax.sharding import PartitionSpec as P

meridional_scale = 0.25
SLABS = 3
SLAB = 120
POINTS = 48
ROWS = 8 * SLABS
CHUNK = 6 * SLABS
GROUPS = 3


def mode_layout(circle, kmax):
    table = np.zeros((GROUPS, 256, 256), np.float64)
    reduced = np.full((GROUPS, 256), 1 << 20, np.int32)
    scale = np.zeros((GROUPS, 256), np.float64)
    b = np.arange(SLAB)
    sign = np.where(b % 2 == 0, 1.0, -1.0)
    for residue in range(POINTS // 2):
        group, place = divmod(residue, 8)
        if residue == 0:
            waves = [(48 * n, 0) for n in range(1, 8)] + [(24 + 48 * n, 128) for n in range(8)]
            factor = 2.0 / circle
        else:
            waves = [(residue + 48 * n, None) for n in range(-8, 8) if abs(residue + 48 * n) <= kmax]
            factor = 1.0 / circle
        for t, (k, row) in enumerate(waves):
            angle = 2.0 * np.pi * ((k * b) % circle) / circle
            cosine, sine = sign * np.cos(angle), sign * np.sin(angle)
            re, im = 32 * place + t, 32 * place + 16 + t
            if row is None:
                table[group, :SLAB, re], table[group, 128 : 128 + SLAB, re] = cosine, sine
                table[group, :SLAB, im], table[group, 128 : 128 + SLAB, im] = -sine, cosine
            else:
                table[group, row : row + SLAB, re] = cosine
                table[group, row : row + SLAB, im] = -sine
            reduced[group, [re, im]] = abs(k)
            scale[group, [re, im]] = factor
    high = table.astype(np.float32).astype(ml_dtypes.bfloat16)
    low = (table - high.astype(np.float64)).astype(np.float32).astype(ml_dtypes.bfloat16)
    return high, low, reduced, scale.astype(np.float32)


def row_metrics(nlat, bands):
    ids = np.arange(nlat, dtype=np.float32)
    step = np.float32(math.pi / nlat)
    center = (ids + np.float32(0.5)) * step - np.float32(math.pi / 2)
    center = np.cos(center.astype(np.float64)).astype(np.float32)
    result = np.zeros((nlat, 128), np.float32)
    result[:, 0] = np.float32(math.sin(math.pi / (2 * nlat))) / center
    result[:, 1] = np.float32(meridional_scale) / center
    result[:, 2] = np.sin(((ids + np.float32(1.0)) * step).astype(np.float64))
    result[:, 3] = np.sin((ids * step).astype(np.float64))
    result[:, 4] = np.arange(nlat) // (nlat // bands) % 2
    return result.reshape(bands, nlat // bands, 128)


def c_add(x, y):
    return (x[0] + y[0], y[1] if x[1] is None else x[1] if y[1] is None else x[1] + y[1])


def c_sub(x, y):
    if y[1] is None:
        return (x[0] - y[0], x[1])
    return (x[0] - y[0], -y[1] if x[1] is None else x[1] - y[1])


def c_conj(x):
    return (x[0], None if x[1] is None else -x[1])


def c_turn(x, numer, denom):
    numer %= denom
    eighth = 8 * numer
    if numer == 0:
        return x
    if 2 * numer == denom:
        return (-x[0], None if x[1] is None else -x[1])
    if 4 * numer == denom:
        return (jnp.zeros_like(x[0]) if x[1] is None else -x[1], x[0])
    if 4 * numer == 3 * denom:
        return (jnp.zeros_like(x[0]) if x[1] is None else x[1], -x[0])
    angle = 2.0 * math.pi * numer / denom
    c, s = math.cos(angle), math.sin(angle)
    if x[1] is None:
        return (x[0] * c, x[0] * s)
    if eighth in (denom, 3 * denom, 5 * denom, 7 * denom):
        h = math.sqrt(0.5)
        a, b = (x[0] - x[1]) * h, (x[0] + x[1]) * h
        return {1: (a, b), 3: (-b, a), 5: (-a, -b), 7: (b, -a)}[eighth // denom]
    return (x[0] * c - x[1] * s, x[0] * s + x[1] * c)


def rfft(x):
    count = len(x)
    if count == 1:
        return [(x[0], None)]
    if count == 2:
        return [(x[0] + x[1], None), (x[0] - x[1], None)]
    even, odd = rfft(x[0::2]), rfft(x[1::2])
    result = [None] * (count // 2 + 1)
    for k in range(count // 4 + 1):
        turned = c_turn(odd[k], -k, count)
        result[k] = c_add(even[k], turned)
        if k != count // 4 or count == 2:
            result[count // 2 - k] = c_conj(c_sub(even[k], turned))
    return result


def irfft(z):
    count = 2 * (len(z) - 1)
    if count == 2:
        return [z[0][0] + z[1][0], z[0][0] - z[1][0]]
    even, odd = [], []
    for k in range(count // 4 + 1):
        mirror = c_conj(z[count // 2 - k])
        even.append(c_add(z[k], mirror))
        odd.append(c_turn(c_sub(z[k], mirror), k, count))
    result = [None] * count
    result[0::2], result[1::2] = irfft(even), irfft(odd)
    return result


def circle_forward(x):
    parts = [rfft(x[a::3]) for a in range(3)]
    result = [None] * 25
    half, root = 0.5, math.sqrt(3.0) / 2.0
    for k in range(9):
        t0 = parts[0][k]
        t1, t2 = c_turn(parts[1][k], -k, 48), c_turn(parts[2][k], -2 * k, 48)
        total, gap = c_add(t1, t2), c_sub(t1, t2)
        result[k] = c_add(t0, total)
        mid = (t0[0] - half * total[0], None if t0[1] is None and total[1] is None else
               (t0[1] if total[1] is None else (0.0 if t0[1] is None else t0[1]) - half * total[1]))
        turn = (None if gap[1] is None else root * gap[1], -root * gap[0])
        plus_re = mid[0] if turn[0] is None else mid[0] + turn[0]
        plus_im = turn[1] if mid[1] is None else mid[1] + turn[1]
        minus_re = mid[0] if turn[0] is None else mid[0] - turn[0]
        minus_im = -turn[1] if mid[1] is None else mid[1] - turn[1]
        if k + 16 <= 24:
            result[k + 16] = (plus_re, plus_im)
        if k > 0 and 16 - k != k + 16 and result[16 - k] is None:
            result[16 - k] = (minus_re, -minus_im)
    return result


def circle_backward(z):
    half, root = 0.5, math.sqrt(3.0) / 2.0
    spectra = [[], [], []]
    for k in range(9):
        t0 = z[k]
        t1 = z[k + 16] if k + 16 <= 24 else c_conj(z[32 - k])
        t2 = c_conj(z[16 - k])
        total, gap = c_add(t1, t2), c_sub(t1, t2)
        if k == 0:
            total, gap = (2.0 * t1[0], None), (None, 2.0 * t1[1])
        spectra[0].append(c_add(t0, total))
        mid = (t0[0] - half * total[0],
               t0[1] if total[1] is None else (-half * total[1] if t0[1] is None else t0[1] - half * total[1]))
        turn = (-root * gap[1], None if gap[0] is None else root * gap[0])
        plus = c_add(mid, turn)
        minus = c_sub(mid, turn)
        spectra[1].append(c_turn(plus, k, 48))
        spectra[2].append(c_turn(minus, 2 * k, 48))
    result = [None] * 48
    for a in range(3):
        result[a::3] = irfft(spectra[a])
    return result


def slabs_of(part):
    lane = lax.broadcasted_iota(jnp.int32, (part.shape[0], 128), 1)
    v0, v1, v2 = part[:, :128], part[:, 128:256], part[:, 256:]
    return (
        v0,
        jnp.where(lane < 8, pltpu.roll(v0, 8, 1), pltpu.roll(v1, 8, 1)),
        jnp.where(lane < 16, pltpu.roll(v1, 16, 1), pltpu.roll(v2, 16, 1)),
    )


def border_kernel(
    state_in, zonal_in, merid_in, table, flags_in, counts_in, modes_in,
    far, near, top, bottom, state, zonal, merid, metric, flags, counts, modes, chunks, own, pad, sems,
):
    fields, rows, cells = state.shape
    band = lax.axis_index("lat")
    sources = [state_in.at[f] for f in range(fields)]
    targets = [state.at[f] for f in range(fields)]
    sources += [merid_in, zonal_in, table.at[band], flags_in, counts_in, modes_in]
    targets += [merid, zonal, metric, flags, counts, modes]
    copies = [
        pltpu.make_async_copy(source, target, sems.at[i])
        for i, (source, target) in enumerate(zip(sources, targets))
    ]
    for copy in copies:
        copy.start()
    pad[...] = jnp.zeros(pad.shape, jnp.float32)
    for copy in copies[: fields + 1]:
        copy.wait()
    for f in range(fields):
        pad[0, f : f + 1, :cells] = state[f, rows - 1 :, :]
        pad[1, f : f + 1, :cells] = state[f, :1, :]
    pad[0, fields : fields + 1, :cells] = merid[rows - 1 :, :]
    odd = band % 2 == 1
    for a, (last, first) in enumerate(zip(slabs_of(pad[0, :8, :]), slabs_of(pad[1, :8, :]))):
        here = slice(8 * a, 8 * a + 8)
        top[here, :], bottom[here, :] = last, first
        far[here, :] = jnp.where(odd, last, first)
        near[here, :] = jnp.where(odd, first, last)
    for copy in copies[fields + 1 :]:
        copy.wait()
    pl.when(works_early())(
        lambda: increments(state, zonal, merid, metric, flags, counts, modes, chunks, own, pad)
    )


def works_early():
    band = lax.axis_index("lat")
    return jnp.logical_and(band % 2 == 1, band < lax.axis_size("lat") // 2)


def late_kernel(*refs):
    pl.when(jnp.logical_not(works_early()))(lambda: increments(*refs))


def increments(state, zonal, merid, metric, flags, counts, modes, chunks_out, own, pad):
    fields, rows, cells = state.shape
    wide = 128 * SLABS
    band, sector = lax.axis_index("lat"), lax.axis_index("lon")
    chunks = chunks_out.reshape(rows * CHUNK, 128)
    for f in range(fields + 2):
        pad[f, :, wide - 128 :] = jnp.zeros((rows, 128), jnp.float32)
    for f in range(fields):
        pad[f, :, :cells] = state[f]
    pad[fields, :, :cells] = zonal[...]
    pad[fields + 1, :, :cells] = merid[...]
    lane = lax.broadcasted_iota(jnp.int32, (rows, wide), 1)
    row = lax.broadcasted_iota(jnp.int32, (rows, wide), 0)

    def spread(index):
        return jnp.broadcast_to(metric[:, index : index + 1], (rows, wide))

    zonal_factor, merid_factor, face = (spread(i) for i in range(3))
    east_wind = pad[fields]
    last_wind = pltpu.roll(east_wind, 3, 1)
    inner_wind = jnp.where(lane < cells - 1, east_wind, 0.0)
    north_wind = jnp.where(row < rows - 1, pad[fields + 1] * face, 0.0)
    for f in range(fields):
        q = pad[f]
        flux_east = inner_wind * (0.5 * (q + pltpu.roll(q, wide - 1, 1)))
        zonal_diff = flux_east - pltpu.roll(flux_east, 1, 1)
        flux_north = north_wind * (0.5 * (q + pltpu.roll(q, rows - 1, 0)))
        merid_diff = flux_north - pltpu.roll(flux_north, 1, 0)
        part = -zonal_factor * zonal_diff - merid_factor * merid_diff
        part = jnp.where(lane == cells, pltpu.roll(q, cells, 1), part)
        part = jnp.where(lane == cells + 1, pltpu.roll(q, 2, 1), part)
        part = jnp.where(lane == cells + 2, last_wind, part)
        for a, slab in enumerate(slabs_of(part)):
            chunks[pl.ds(fields * a + f, rows, stride=CHUNK), :] = slab
    place = lax.broadcasted_iota(jnp.int32, flags.shape, 0) * 128 + lax.broadcasted_iota(jnp.int32, flags.shape, 1)
    chosen = place == band * rows + sector

    def pick(values):
        picked = jnp.where(chosen, values[...].astype(jnp.float32), 0.0)
        return jnp.sum(jnp.sum(picked, axis=1, keepdims=True), axis=0, keepdims=True)

    flag, count = pick(flags), pick(counts)
    raised = jnp.maximum(count + 1.0 - modes[:8, :], 0.0)
    own[:8, :] = raised / jnp.maximum(count, 1.0) * flag * modes[8:, :]
    mine = jnp.where(row == sector, zonal_factor, 0.0)[:, :256]
    own[8:, :] = jnp.broadcast_to(jnp.sum(mine, axis=0, keepdims=True), (8, 256))


def border_fluxes_kernel(
    early_part, late_part, early_own, late_own, top_in, bottom_in, both, from_far, metric, chunks_out, own
):
    fields, rows = 6, metric.shape[0]
    inside = lax.broadcasted_iota(jnp.int32, (8, 128), 1) < SLAB

    def spread(row, index):
        return jnp.broadcast_to(metric[row : row + 1, index : index + 1], (8, 128))

    first_factor, last_factor = spread(0, 1), spread(rows - 1, 1)
    first_face, last_face = spread(0, 3), spread(rows - 1, 2)
    odd = spread(0, 4) > 0.5
    chunks = chunks_out.reshape(rows * CHUNK, 128)
    early = works_early()

    @pl.when(early)
    def _():
        chunks_out[...] = early_part[...]
        own[...] = early_own[...]

    @pl.when(jnp.logical_not(early))
    def _():
        chunks_out[...] = late_part[...]
        own[...] = late_own[...]

    for a in range(SLABS):
        here = slice(8 * a, 8 * a + 8)
        top, bottom = top_in[here, :], bottom_in[here, :]
        other = jnp.where(odd, both[here, :], both[ROWS + 8 * a : ROWS + 8 * a + 8, :])
        next_chip = from_far[here, :]
        north, south = jnp.where(odd, next_chip, other), jnp.where(odd, other, next_chip)
        flux = (south[fields : fields + 1, :] * first_face) * (0.5 * (south + bottom))
        flux = jnp.where(inside, first_factor * flux, 0.0)
        there = slice(fields * a, fields * (a + 1))
        chunks[there, :] = chunks[there, :] + flux[:fields]
        flux = (top[fields : fields + 1, :] * last_face) * (0.5 * (top + north))
        flux = jnp.where(inside, last_factor * flux, 0.0)
        there = slice((rows - 1) * CHUNK + fields * a, (rows - 1) * CHUNK + fields * (a + 1))
        chunks[there, :] = chunks[there, :] - flux[:fields]


def split(x):
    high = x.astype(jnp.bfloat16)
    return high, (x - high.astype(jnp.float32)).astype(jnp.bfloat16)


def product(x, high, low, dims):
    def dot(p, q):
        return lax.dot_general(p, q, (dims, ((), ())), preferred_element_type=jnp.float32)

    x_high, x_low = split(x)
    both = dot(jnp.concatenate([x_high, x_low], axis=0), high)
    return both[: x.shape[0]] + (both[x.shape[0] :] + dot(x_high, low))


def filter_kernel(chunks_in, own, high, low, result_out):
    sectors, fields = chunks_in.shape[0], 6
    chunks = chunks_in.reshape(sectors * CHUNK, 128)
    result = result_out.reshape(sectors * CHUNK, 128)
    lane = lax.broadcasted_iota(jnp.int32, (8, 128), 1)
    zonal_factor = own[8:, :128]
    points = [chunks[fields * p : fields * p + 8, :] for p in range(POINTS - 1)]
    points.append(pltpu.roll(chunks[sectors * CHUNK - 8 :, :], 6, 0))
    lasts = [points[3 * s + 2] for s in range(sectors)]
    for s in range(sectors):
        after = (s + 1) % sectors
        flux = pltpu.roll(lasts[s], 125, 1) * (
            0.5 * (pltpu.roll(lasts[s], 126, 1) + pltpu.roll(lasts[after], 127, 1))
        )
        edge = jnp.where(lane == SLAB - 1, zonal_factor * flux, 0.0)
        points[3 * s + 2] = points[3 * s + 2] - edge
        points[3 * after] = points[3 * after] + pltpu.roll(edge, 128 - (SLAB - 1), 1)
    for p in range(POINTS):
        result[fields * p : fields * (p + 1), :] = points[p][:fields]
    spectrum = circle_forward(points)
    spectrum[0] = (spectrum[0][0], spectrum[24][0])
    block = lax.broadcasted_iota(jnp.int32, (64, 256), 0) // 8
    column = lax.broadcasted_iota(jnp.int32, (64, 256), 1) // 32
    back = [None] * 25
    groups = range(GROUPS)
    rows = [
        jnp.concatenate([jnp.concatenate(spectrum[8 * g + i], axis=1) for i in range(8)], axis=0)
        for g in groups
    ]
    modes = [product(rows[g], high[g], low[g], ((1,), (0,))) for g in groups]
    modes = [jnp.where(block == column, modes[g] * own[g : g + 1, :], 0.0) for g in groups]
    rows = [product(modes[g], high[g], low[g], ((1,), (1,))) for g in groups]
    for g in groups:
        for i in range(8):
            part = rows[g][8 * i : 8 * i + 8, :]
            back[8 * g + i] = (part[:, :128], part[:, 128:])
    back[24] = (back[0][1], None)
    back[0] = (back[0][0], None)
    correction = circle_backward(back)
    for p in range(POINTS):
        place = slice(fields * p, fields * (p + 1))
        result[place, :] = result[place, :] - correction[p][:fields]


def final_kernel(chunks_in, state, advanced):
    fields, rows, cells = state.shape
    chunks = chunks_in.reshape(rows * CHUNK, 128)
    lane = lax.broadcasted_iota(jnp.int32, (rows, 128), 1)
    for f in range(fields):
        s0, s1, s2 = (chunks[pl.ds(fields * a + f, rows, stride=CHUNK), :] for a in range(SLABS))
        s1, s2 = pltpu.roll(s1, 120, 1), pltpu.roll(s2, 112, 1)
        advanced[f, :, :128] = state[f, :, :128] + jnp.where(lane < 120, s0, s1)
        advanced[f, :, 128:256] = state[f, :, 128:256] + jnp.where(lane < 112, s1, s2)
        advanced[f, :, 256:] = state[f, :, 256:] + s2[:, : cells - 256]


def floats(*shape):
    return jax.ShapeDtypeStruct(shape, jnp.float32)


def call(kernel, name, outs, mebibytes, args, elsewhere=0, scratch=()):
    vmem = pl.BlockSpec(memory_space=pltpu.VMEM)
    stay = pl.BlockSpec(memory_space=pltpu.HBM)
    fixed = len(args) - elsewhere
    args = args[:fixed] + tuple(
        pltpu.with_memory_space_constraint(arg, pltpu.HBM) for arg in args[fixed:]
    )
    return pl.pallas_call(
        kernel,
        out_shape=[jax.ShapeDtypeStruct(out.shape, out.dtype) for out in outs],
        in_specs=[vmem] * fixed + [stay] * elsewhere,
        out_specs=[vmem] * len(outs),
        scratch_shapes=list(scratch),
        compiler_params=pltpu.CompilerParams(vmem_limit_bytes=mebibytes << 20),
        name=name,
    )(*args)


def body(state, zonal_wind, meridional_wind, filter_flag, mode_count):
    field_count, level_count, lat_cells, lon_cells = state.shape
    item_count = field_count * level_count
    band_total, sectors = lax.axis_size("lat"), lax.axis_size("lon")
    nlat, circle = lat_cells * band_total, lon_cells * sectors
    wide = 128 * SLABS
    fields = state.reshape(item_count, lat_cells, lon_cells)
    zonal, merid = (w.reshape(lat_cells, lon_cells) for w in (zonal_wind, meridional_wind))
    high, low, reduced, scale = mode_layout(circle, circle // 16)

    modes = np.concatenate([np.pad(rows, ((0, 8 - GROUPS), (0, 0))) for rows in (reduced, scale)])
    modes = jnp.asarray(modes.astype(np.float32))
    flags, counts = filter_flag.reshape(-1, 128), mode_count.reshape(-1, 128)
    border = floats(ROWS, 128)
    metric, own = floats(lat_cells, 128), floats(16, 256)
    packed = floats(sectors, CHUNK // 2, 2, 128)
    pad = pltpu.VMEM((8, lat_cells, wide), jnp.float32)
    here = (fields, zonal, merid, jnp.asarray(row_metrics(nlat, band_total)), flags, counts, modes)
    far, near, top, bottom, *here, early_part, early_own = call(
        border_kernel,
        "borders",
        [border] * 4 + [fields, zonal, merid, metric, flags, counts, modes, packed, own],
        4,
        here,
        7,
        [pad, pltpu.SemaphoreType.DMA((item_count + 6,))],
    )
    fields, zonal, merid, metric = here[:4]
    pairs = [(i, i + 1) for i in range(1, band_total - 1, 2)]
    from_far = lax.ppermute(far, "lat", pairs + [(target, source) for source, target in pairs])
    chips = [[i, i + 1] for i in range(0, band_total, 2)]
    both = lax.all_gather(near, "lat", axis=0, tiled=True, axis_index_groups=chips)

    late_part, late_own = call(late_kernel, "increments", [packed, own], 4, tuple(here), 0, [pad])
    chunks, own = call(
        border_fluxes_kernel,
        "border_fluxes",
        [packed, own],
        4,
        (early_part, late_part, early_own, late_own, top, bottom, both, from_far, metric),
    )
    chunks = lax.all_to_all(chunks, "lon", 0, 0, tiled=True)
    (chunks,) = call(
        filter_kernel,
        "filter_rows",
        [packed],
        8,
        (chunks, own, jnp.asarray(high), jnp.asarray(low)),
    )
    chunks = lax.all_to_all(chunks, "lon", 0, 0, tiled=True)
    (advanced,) = call(final_kernel, "advance", [fields], 4, (chunks, fields))
    return advanced.reshape(state.shape)


def solution(mesh):
    placed = (P(None, None, "lat", "lon"), P(None, "lat", "lon"), P(None, "lat", "lon"), P(), P())
    return jax.shard_map(
        body, mesh=mesh, in_specs=placed, out_specs=P(None, None, "lat", "lon"), check_vma=False
    )
```

```python
import math

import jax
import jax.numpy as jnp
import ml_dtypes
import numpy as np
from jax import lax
from jax.experimental import pallas as pl
from jax.experimental.pallas import tpu as pltpu
from jax.sharding import PartitionSpec as P

meridional_scale = 0.25
SLABS = 3
SLAB = 120
POINTS = 48
ROWS = 8 * SLABS
CHUNK = 6 * SLABS
GROUPS = 3


def mode_layout(circle, kmax):
    table = np.zeros((GROUPS, 256, 256), np.float64)
    reduced = np.full((GROUPS, 256), 1 << 20, np.int32)
    scale = np.zeros((GROUPS, 256), np.float64)
    b = np.arange(SLAB)
    sign = np.where(b % 2 == 0, 1.0, -1.0)
    for residue in range(POINTS // 2):
        group, place = divmod(residue, 8)
        if residue == 0:
            waves = [(48 * n, 0) for n in range(1, 8)] + [(24 + 48 * n, 128) for n in range(8)]
            factor = 2.0 / circle
        else:
            waves = [(residue + 48 * n, None) for n in range(-8, 8) if abs(residue + 48 * n) <= kmax]
            factor = 1.0 / circle
        for t, (k, row) in enumerate(waves):
            angle = 2.0 * np.pi * ((k * b) % circle) / circle
            cosine, sine = sign * np.cos(angle), sign * np.sin(angle)
            re, im = 32 * place + t, 32 * place + 16 + t
            if row is None:
                table[group, :SLAB, re], table[group, 128 : 128 + SLAB, re] = cosine, sine
                table[group, :SLAB, im], table[group, 128 : 128 + SLAB, im] = -sine, cosine
            else:
                table[group, row : row + SLAB, re] = cosine
                table[group, row : row + SLAB, im] = -sine
            reduced[group, [re, im]] = abs(k)
            scale[group, [re, im]] = factor
    high = table.astype(np.float32).astype(ml_dtypes.bfloat16)
    low = (table - high.astype(np.float64)).astype(np.float32).astype(ml_dtypes.bfloat16)
    return high, low, reduced, scale.astype(np.float32)


def row_metrics(nlat, bands):
    ids = np.arange(nlat, dtype=np.float32)
    step = np.float32(math.pi / nlat)
    center = (ids + np.float32(0.5)) * step - np.float32(math.pi / 2)
    center = np.cos(center.astype(np.float64)).astype(np.float32)
    result = np.zeros((nlat, 128), np.float32)
    result[:, 0] = np.float32(math.sin(math.pi / (2 * nlat))) / center
    result[:, 1] = np.float32(meridional_scale) / center
    result[:, 2] = np.sin(((ids + np.float32(1.0)) * step).astype(np.float64))
    result[:, 3] = np.sin((ids * step).astype(np.float64))
    result[:, 4] = np.arange(nlat) // (nlat // bands) % 2
    result[:, 5] = np.arange(nlat) // (nlat // bands) < bands - 1
    return result.reshape(bands, nlat // bands, 128)


def c_add(x, y):
    return (x[0] + y[0], y[1] if x[1] is None else x[1] if y[1] is None else x[1] + y[1])


def c_sub(x, y):
    if y[1] is None:
        return (x[0] - y[0], x[1])
    return (x[0] - y[0], -y[1] if x[1] is None else x[1] - y[1])


def c_conj(x):
    return (x[0], None if x[1] is None else -x[1])


def c_turn(x, numer, denom):
    numer %= denom
    eighth = 8 * numer
    if numer == 0:
        return x
    if 2 * numer == denom:
        return (-x[0], None if x[1] is None else -x[1])
    if 4 * numer == denom:
        return (jnp.zeros_like(x[0]) if x[1] is None else -x[1], x[0])
    if 4 * numer == 3 * denom:
        return (jnp.zeros_like(x[0]) if x[1] is None else x[1], -x[0])
    angle = 2.0 * math.pi * numer / denom
    c, s = math.cos(angle), math.sin(angle)
    if x[1] is None:
        return (x[0] * c, x[0] * s)
    if eighth in (denom, 3 * denom, 5 * denom, 7 * denom):
        h = math.sqrt(0.5)
        a, b = (x[0] - x[1]) * h, (x[0] + x[1]) * h
        return {1: (a, b), 3: (-b, a), 5: (-a, -b), 7: (b, -a)}[eighth // denom]
    return (x[0] * c - x[1] * s, x[0] * s + x[1] * c)


def rfft(x):
    count = len(x)
    if count == 1:
        return [(x[0], None)]
    if count == 2:
        return [(x[0] + x[1], None), (x[0] - x[1], None)]
    even, odd = rfft(x[0::2]), rfft(x[1::2])
    result = [None] * (count // 2 + 1)
    for k in range(count // 4 + 1):
        turned = c_turn(odd[k], -k, count)
        result[k] = c_add(even[k], turned)
        if k != count // 4 or count == 2:
            result[count // 2 - k] = c_conj(c_sub(even[k], turned))
    return result


def irfft(z):
    count = 2 * (len(z) - 1)
    if count == 2:
        return [z[0][0] + z[1][0], z[0][0] - z[1][0]]
    even, odd = [], []
    for k in range(count // 4 + 1):
        mirror = c_conj(z[count // 2 - k])
        even.append(c_add(z[k], mirror))
        odd.append(c_turn(c_sub(z[k], mirror), k, count))
    result = [None] * count
    result[0::2], result[1::2] = irfft(even), irfft(odd)
    return result


def circle_forward(x):
    parts = [rfft(x[a::3]) for a in range(3)]
    result = [None] * 25
    half, root = 0.5, math.sqrt(3.0) / 2.0
    for k in range(9):
        t0 = parts[0][k]
        t1, t2 = c_turn(parts[1][k], -k, 48), c_turn(parts[2][k], -2 * k, 48)
        total, gap = c_add(t1, t2), c_sub(t1, t2)
        result[k] = c_add(t0, total)
        mid = (t0[0] - half * total[0], None if t0[1] is None and total[1] is None else
               (t0[1] if total[1] is None else (0.0 if t0[1] is None else t0[1]) - half * total[1]))
        turn = (None if gap[1] is None else root * gap[1], -root * gap[0])
        plus_re = mid[0] if turn[0] is None else mid[0] + turn[0]
        plus_im = turn[1] if mid[1] is None else mid[1] + turn[1]
        minus_re = mid[0] if turn[0] is None else mid[0] - turn[0]
        minus_im = -turn[1] if mid[1] is None else mid[1] - turn[1]
        if k + 16 <= 24:
            result[k + 16] = (plus_re, plus_im)
        if k > 0 and 16 - k != k + 16 and result[16 - k] is None:
            result[16 - k] = (minus_re, -minus_im)
    return result


def circle_backward(z):
    half, root = 0.5, math.sqrt(3.0) / 2.0
    spectra = [[], [], []]
    for k in range(9):
        t0 = z[k]
        t1 = z[k + 16] if k + 16 <= 24 else c_conj(z[32 - k])
        t2 = c_conj(z[16 - k])
        total, gap = c_add(t1, t2), c_sub(t1, t2)
        if k == 0:
            total, gap = (2.0 * t1[0], None), (None, 2.0 * t1[1])
        spectra[0].append(c_add(t0, total))
        mid = (t0[0] - half * total[0],
               t0[1] if total[1] is None else (-half * total[1] if t0[1] is None else t0[1] - half * total[1]))
        turn = (-root * gap[1], None if gap[0] is None else root * gap[0])
        plus = c_add(mid, turn)
        minus = c_sub(mid, turn)
        spectra[1].append(c_turn(plus, k, 48))
        spectra[2].append(c_turn(minus, 2 * k, 48))
    result = [None] * 48
    for a in range(3):
        result[a::3] = irfft(spectra[a])
    return result


def slabs_of(part):
    lane = lax.broadcasted_iota(jnp.int32, (part.shape[0], 128), 1)
    v0, v1, v2 = part[:, :128], part[:, 128:256], part[:, 256:]
    return (
        v0,
        jnp.where(lane < 8, pltpu.roll(v0, 8, 1), pltpu.roll(v1, 8, 1)),
        jnp.where(lane < 16, pltpu.roll(v1, 16, 1), pltpu.roll(v2, 16, 1)),
    )


def border_kernel(
    state_in, zonal_in, merid_in, table, flags_in, counts_in, modes_in,
    borders, state, zonal, merid, metric, flags, counts, modes, pad, sems,
):
    fields, rows, cells = state.shape
    band = lax.axis_index("lat")
    sources = [state_in.at[f] for f in range(fields)]
    targets = [state.at[f] for f in range(fields)]
    sources += [merid_in, zonal_in, table.at[band], flags_in, counts_in, modes_in]
    targets += [merid, zonal, metric, flags, counts, modes]
    copies = [
        pltpu.make_async_copy(source, target, sems.at[i])
        for i, (source, target) in enumerate(zip(sources, targets))
    ]
    for copy in copies:
        copy.start()
    pad[...] = jnp.zeros(pad.shape, jnp.float32)
    for copy in copies[: fields + 1]:
        copy.wait()
    for f in range(fields):
        pad[0, f : f + 1, :cells] = state[f, rows - 1 :, :]
        pad[1, f : f + 1, :cells] = state[f, :1, :]
    pad[0, fields : fields + 1, :cells] = merid[rows - 1 :, :]
    for place in range(2):
        for a, slab in enumerate(slabs_of(pad[place, :8, :])):
            borders[ROWS * place + 8 * a : ROWS * place + 8 * a + 8, :] = slab
    for copy in copies[fields + 1 :]:
        copy.wait()


def increment_kernel(state, zonal, merid, metric, flags, counts, modes, chunks_out, own, pad):
    fields, rows, cells = state.shape
    wide = 128 * SLABS
    band, sector = lax.axis_index("lat"), lax.axis_index("lon")
    chunks = chunks_out.reshape(rows * CHUNK, 128)
    for f in range(fields + 2):
        pad[f, :, wide - 128 :] = jnp.zeros((rows, 128), jnp.float32)
    for f in range(fields):
        pad[f, :, :cells] = state[f]
    pad[fields, :, :cells] = zonal[...]
    pad[fields + 1, :, :cells] = merid[...]
    lane = lax.broadcasted_iota(jnp.int32, (rows, wide), 1)
    row = lax.broadcasted_iota(jnp.int32, (rows, wide), 0)

    def spread(index):
        return jnp.broadcast_to(metric[:, index : index + 1], (rows, wide))

    zonal_factor, merid_factor, face = (spread(i) for i in range(3))
    east_wind = pad[fields]
    last_wind = pltpu.roll(east_wind, 3, 1)
    inner_wind = jnp.where(lane < cells - 1, east_wind, 0.0)
    north_wind = jnp.where(row < rows - 1, pad[fields + 1] * face, 0.0)
    for f in range(fields):
        q = pad[f]
        flux_east = inner_wind * (0.5 * (q + pltpu.roll(q, wide - 1, 1)))
        zonal_diff = flux_east - pltpu.roll(flux_east, 1, 1)
        flux_north = north_wind * (0.5 * (q + pltpu.roll(q, rows - 1, 0)))
        merid_diff = flux_north - pltpu.roll(flux_north, 1, 0)
        part = -zonal_factor * zonal_diff - merid_factor * merid_diff
        part = jnp.where(lane == cells, pltpu.roll(q, cells, 1), part)
        part = jnp.where(lane == cells + 1, pltpu.roll(q, 2, 1), part)
        part = jnp.where(lane == cells + 2, last_wind, part)
        for a, slab in enumerate(slabs_of(part)):
            chunks[pl.ds(fields * a + f, rows, stride=CHUNK), :] = slab
    place = lax.broadcasted_iota(jnp.int32, flags.shape, 0) * 128 + lax.broadcasted_iota(jnp.int32, flags.shape, 1)
    chosen = place == band * rows + sector

    def pick(values):
        picked = jnp.where(chosen, values[...].astype(jnp.float32), 0.0)
        return jnp.sum(jnp.sum(picked, axis=1, keepdims=True), axis=0, keepdims=True)

    flag, count = pick(flags), pick(counts)
    raised = jnp.maximum(count + 1.0 - modes[:8, :], 0.0)
    own[:8, :] = raised / jnp.maximum(count, 1.0) * flag * modes[8:, :]
    mine = jnp.where(row == sector, zonal_factor, 0.0)[:, :256]
    own[8:, :] = jnp.broadcast_to(jnp.sum(mine, axis=0, keepdims=True), (8, 256))


def passing_kernel(chip, passing):
    odd = lax.axis_index("lat") % 2 == 1
    passing[...] = jnp.where(odd, chip[ROWS : 2 * ROWS, :], chip[2 * ROWS : 3 * ROWS, :])


def border_fluxes_kernel(part, borders, chip, passed, metric, chunks_out):
    fields, rows = 6, metric.shape[0]
    inside = lax.broadcasted_iota(jnp.int32, (8, 128), 1) < SLAB

    def spread(row, index):
        return jnp.broadcast_to(metric[row : row + 1, index : index + 1], (8, 128))

    first_factor, last_factor = spread(0, 1), spread(rows - 1, 1)
    first_face, last_face = spread(0, 3), spread(rows - 1, 2)
    odd, has_north = spread(0, 4) > 0.5, spread(0, 5) > 0.5
    chunks = chunks_out.reshape(rows * CHUNK, 128)
    chunks_out[...] = part[...]
    for a in range(SLABS):
        here = slice(8 * a, 8 * a + 8)
        top, bottom = borders[here, :], borders[ROWS + 8 * a : ROWS + 8 * a + 8, :]
        south = jnp.where(odd, chip[here, :], passed[here, :])
        above = chip[3 * ROWS + 8 * a : 3 * ROWS + 8 * a + 8, :]
        north = jnp.where(has_north, jnp.where(odd, passed[here, :], above), 0.0)
        flux = (south[fields : fields + 1, :] * first_face) * (0.5 * (south + bottom))
        flux = jnp.where(inside, first_factor * flux, 0.0)
        place = slice(fields * a, fields * (a + 1))
        chunks[place, :] = chunks[place, :] + flux[:fields]
        flux = (top[fields : fields + 1, :] * last_face) * (0.5 * (top + north))
        flux = jnp.where(inside, last_factor * flux, 0.0)
        place = slice((rows - 1) * CHUNK + fields * a, (rows - 1) * CHUNK + fields * (a + 1))
        chunks[place, :] = chunks[place, :] - flux[:fields]


def split(x):
    high = x.astype(jnp.bfloat16)
    return high, (x - high.astype(jnp.float32)).astype(jnp.bfloat16)


def product(x, high, low, dims):
    def dot(p, q):
        return lax.dot_general(p, q, (dims, ((), ())), preferred_element_type=jnp.float32)

    x_high, x_low = split(x)
    both = dot(jnp.concatenate([x_high, x_low], axis=0), high)
    return both[: x.shape[0]] + (both[x.shape[0] :] + dot(x_high, low))


def filter_kernel(chunks_in, own, high, low, result_out):
    sectors, fields = chunks_in.shape[0], 6
    chunks = chunks_in.reshape(sectors * CHUNK, 128)
    result = result_out.reshape(sectors * CHUNK, 128)
    lane = lax.broadcasted_iota(jnp.int32, (8, 128), 1)
    zonal_factor = own[8:, :128]
    points = [chunks[fields * p : fields * p + 8, :] for p in range(POINTS - 1)]
    points.append(pltpu.roll(chunks[sectors * CHUNK - 8 :, :], 6, 0))
    lasts = [points[3 * s + 2] for s in range(sectors)]
    for s in range(sectors):
        after = (s + 1) % sectors
        flux = pltpu.roll(lasts[s], 125, 1) * (
            0.5 * (pltpu.roll(lasts[s], 126, 1) + pltpu.roll(lasts[after], 127, 1))
        )
        edge = jnp.where(lane == SLAB - 1, zonal_factor * flux, 0.0)
        points[3 * s + 2] = points[3 * s + 2] - edge
        points[3 * after] = points[3 * after] + pltpu.roll(edge, 128 - (SLAB - 1), 1)
    for p in range(POINTS):
        result[fields * p : fields * (p + 1), :] = points[p][:fields]
    spectrum = circle_forward(points)
    spectrum[0] = (spectrum[0][0], spectrum[24][0])
    block = lax.broadcasted_iota(jnp.int32, (64, 256), 0) // 8
    column = lax.broadcasted_iota(jnp.int32, (64, 256), 1) // 32
    back = [None] * 25
    groups = range(GROUPS)
    rows = [
        jnp.concatenate([jnp.concatenate(spectrum[8 * g + i], axis=1) for i in range(8)], axis=0)
        for g in groups
    ]
    modes = [product(rows[g], high[g], low[g], ((1,), (0,))) for g in groups]
    modes = [jnp.where(block == column, modes[g] * own[g : g + 1, :], 0.0) for g in groups]
    rows = [product(modes[g], high[g], low[g], ((1,), (1,))) for g in groups]
    for g in groups:
        for i in range(8):
            part = rows[g][8 * i : 8 * i + 8, :]
            back[8 * g + i] = (part[:, :128], part[:, 128:])
    back[24] = (back[0][1], None)
    back[0] = (back[0][0], None)
    correction = circle_backward(back)
    for p in range(POINTS):
        place = slice(fields * p, fields * (p + 1))
        result[place, :] = result[place, :] - correction[p][:fields]


def final_kernel(chunks_in, state, advanced):
    fields, rows, cells = state.shape
    chunks = chunks_in.reshape(rows * CHUNK, 128)
    lane = lax.broadcasted_iota(jnp.int32, (rows, 128), 1)
    for f in range(fields):
        s0, s1, s2 = (chunks[pl.ds(fields * a + f, rows, stride=CHUNK), :] for a in range(SLABS))
        s1, s2 = pltpu.roll(s1, 120, 1), pltpu.roll(s2, 112, 1)
        advanced[f, :, :128] = state[f, :, :128] + jnp.where(lane < 120, s0, s1)
        advanced[f, :, 128:256] = state[f, :, 128:256] + jnp.where(lane < 112, s1, s2)
        advanced[f, :, 256:] = state[f, :, 256:] + s2[:, : cells - 256]


def floats(*shape):
    return jax.ShapeDtypeStruct(shape, jnp.float32)


def call(kernel, name, outs, mebibytes, args, elsewhere=0, scratch=()):
    vmem = pl.BlockSpec(memory_space=pltpu.VMEM)
    stay = pl.BlockSpec(memory_space=pltpu.HBM)
    fixed = len(args) - elsewhere
    args = args[:fixed] + tuple(
        pltpu.with_memory_space_constraint(arg, pltpu.HBM) for arg in args[fixed:]
    )
    return pl.pallas_call(
        kernel,
        out_shape=[jax.ShapeDtypeStruct(out.shape, out.dtype) for out in outs],
        in_specs=[vmem] * fixed + [stay] * elsewhere,
        out_specs=[vmem] * len(outs),
        scratch_shapes=list(scratch),
        compiler_params=pltpu.CompilerParams(vmem_limit_bytes=mebibytes << 20),
        name=name,
    )(*args)


def body(state, zonal_wind, meridional_wind, filter_flag, mode_count):
    field_count, level_count, lat_cells, lon_cells = state.shape
    item_count = field_count * level_count
    band_total, sectors = lax.axis_size("lat"), lax.axis_size("lon")
    nlat, circle = lat_cells * band_total, lon_cells * sectors
    wide = 128 * SLABS
    fields = state.reshape(item_count, lat_cells, lon_cells)
    zonal, merid = (w.reshape(lat_cells, lon_cells) for w in (zonal_wind, meridional_wind))
    high, low, reduced, scale = mode_layout(circle, circle // 16)

    modes = np.concatenate([np.pad(rows, ((0, 8 - GROUPS), (0, 0))) for rows in (reduced, scale)])
    modes = jnp.asarray(modes.astype(np.float32))
    flags, counts = filter_flag.reshape(-1, 128), mode_count.reshape(-1, 128)
    metric, own = floats(lat_cells, 128), floats(16, 256)
    packed = floats(sectors, CHUNK // 2, 2, 128)
    pad = pltpu.VMEM((8, lat_cells, wide), jnp.float32)
    here = (fields, zonal, merid, jnp.asarray(row_metrics(nlat, band_total)), flags, counts, modes)
    borders, *here = call(
        border_kernel,
        "borders",
        [floats(2 * ROWS, 128), fields, zonal, merid, metric, flags, counts, modes],
        4,
        here,
        7,
        [pad, pltpu.SemaphoreType.DMA((item_count + 6,))],
    )
    fields, metric = here[0], here[3]
    cores = [[i, i + 1] for i in range(0, band_total, 2)]
    chip = lax.all_gather(borders, "lat", axis=0, tiled=True, axis_index_groups=cores)
    (passing,) = call(passing_kernel, "passing", [floats(ROWS, 128)], 2, (chip,))
    ring = [(i, i + 2) for i in range(0, band_total - 2, 2)] + [(band_total - 2, band_total - 1)]
    ring += [(i, i - 2) for i in range(3, band_total, 2)] + [(1, 0)]
    passed = lax.ppermute(passing, "lat", ring)
    part, own = call(increment_kernel, "increments", [packed, own], 4, tuple(here), 0, [pad])
    (chunks,) = call(
        border_fluxes_kernel, "border_fluxes", [packed], 4, (part, borders, chip, passed, metric)
    )
    chunks = lax.all_to_all(chunks, "lon", 0, 0, tiled=True)
    (chunks,) = call(
        filter_kernel,
        "filter_rows",
        [packed],
        8,
        (chunks, own, jnp.asarray(high), jnp.asarray(low)),
    )
    chunks = lax.all_to_all(chunks, "lon", 0, 0, tiled=True)
    (advanced,) = call(final_kernel, "advance", [fields], 4, (chunks, fields))
    return advanced.reshape(state.shape)


def solution(mesh):
    placed = (P(None, None, "lat", "lon"), P(None, "lat", "lon"), P(None, "lat", "lon"), P(), P())
    return jax.shard_map(
        body, mesh=mesh, in_specs=placed, out_specs=P(None, None, "lat", "lon"), check_vma=False
    )
```

```python
import math

import jax
import jax.numpy as jnp
import ml_dtypes
import numpy as np
from jax import lax
from jax.experimental import pallas as pl
from jax.experimental.pallas import tpu as pltpu
from jax.sharding import PartitionSpec as P

meridional_scale = 0.25
SLABS = 3
SLAB = 120
POINTS = 48
ROWS = 8 * SLABS
CHUNK = 6 * SLABS
GROUPS = 3


def mode_layout(circle, kmax):
    table = np.zeros((GROUPS, 256, 256), np.float64)
    reduced = np.full((GROUPS, 256), 1 << 20, np.int32)
    scale = np.zeros((GROUPS, 256), np.float64)
    b = np.arange(SLAB)
    sign = np.where(b % 2 == 0, 1.0, -1.0)
    for residue in range(POINTS // 2):
        group, place = divmod(residue, 8)
        if residue == 0:
            waves = [(48 * n, 0) for n in range(1, 8)] + [(24 + 48 * n, 128) for n in range(8)]
            factor = 2.0 / circle
        else:
            waves = [(residue + 48 * n, None) for n in range(-8, 8) if abs(residue + 48 * n) <= kmax]
            factor = 1.0 / circle
        for t, (k, row) in enumerate(waves):
            angle = 2.0 * np.pi * ((k * b) % circle) / circle
            cosine, sine = sign * np.cos(angle), sign * np.sin(angle)
            re, im = 32 * place + t, 32 * place + 16 + t
            if row is None:
                table[group, :SLAB, re], table[group, 128 : 128 + SLAB, re] = cosine, sine
                table[group, :SLAB, im], table[group, 128 : 128 + SLAB, im] = -sine, cosine
            else:
                table[group, row : row + SLAB, re] = cosine
                table[group, row : row + SLAB, im] = -sine
            reduced[group, [re, im]] = abs(k)
            scale[group, [re, im]] = factor
    high = table.astype(np.float32).astype(ml_dtypes.bfloat16)
    low = (table - high.astype(np.float64)).astype(np.float32).astype(ml_dtypes.bfloat16)
    return high, low, reduced, scale.astype(np.float32)


def row_metrics(nlat, bands):
    ids = np.arange(nlat, dtype=np.float32)
    step = np.float32(math.pi / nlat)
    center = (ids + np.float32(0.5)) * step - np.float32(math.pi / 2)
    center = np.cos(center.astype(np.float64)).astype(np.float32)
    result = np.zeros((nlat, 128), np.float32)
    result[:, 0] = np.float32(math.sin(math.pi / (2 * nlat))) / center
    result[:, 1] = np.float32(meridional_scale) / center
    result[:, 2] = np.sin(((ids + np.float32(1.0)) * step).astype(np.float64))
    result[:, 3] = np.sin((ids * step).astype(np.float64))
    result[:, 4] = np.arange(nlat) // (nlat // bands) % 2
    result[:, 5] = np.arange(nlat) // (nlat // bands) < bands - 1
    return result.reshape(bands, nlat // bands, 128)


def c_add(x, y):
    return (x[0] + y[0], y[1] if x[1] is None else x[1] if y[1] is None else x[1] + y[1])


def c_sub(x, y):
    if y[1] is None:
        return (x[0] - y[0], x[1])
    return (x[0] - y[0], -y[1] if x[1] is None else x[1] - y[1])


def c_conj(x):
    return (x[0], None if x[1] is None else -x[1])


def c_turn(x, numer, denom):
    numer %= denom
    eighth = 8 * numer
    if numer == 0:
        return x
    if 2 * numer == denom:
        return (-x[0], None if x[1] is None else -x[1])
    if 4 * numer == denom:
        return (jnp.zeros_like(x[0]) if x[1] is None else -x[1], x[0])
    if 4 * numer == 3 * denom:
        return (jnp.zeros_like(x[0]) if x[1] is None else x[1], -x[0])
    angle = 2.0 * math.pi * numer / denom
    c, s = math.cos(angle), math.sin(angle)
    if x[1] is None:
        return (x[0] * c, x[0] * s)
    if eighth in (denom, 3 * denom, 5 * denom, 7 * denom):
        h = math.sqrt(0.5)
        a, b = (x[0] - x[1]) * h, (x[0] + x[1]) * h
        return {1: (a, b), 3: (-b, a), 5: (-a, -b), 7: (b, -a)}[eighth // denom]
    return (x[0] * c - x[1] * s, x[0] * s + x[1] * c)


def rfft(x):
    count = len(x)
    if count == 1:
        return [(x[0], None)]
    if count == 2:
        return [(x[0] + x[1], None), (x[0] - x[1], None)]
    even, odd = rfft(x[0::2]), rfft(x[1::2])
    result = [None] * (count // 2 + 1)
    for k in range(count // 4 + 1):
        turned = c_turn(odd[k], -k, count)
        result[k] = c_add(even[k], turned)
        if k != count // 4 or count == 2:
            result[count // 2 - k] = c_conj(c_sub(even[k], turned))
    return result


def irfft(z):
    count = 2 * (len(z) - 1)
    if count == 2:
        return [z[0][0] + z[1][0], z[0][0] - z[1][0]]
    even, odd = [], []
    for k in range(count // 4 + 1):
        mirror = c_conj(z[count // 2 - k])
        even.append(c_add(z[k], mirror))
        odd.append(c_turn(c_sub(z[k], mirror), k, count))
    result = [None] * count
    result[0::2], result[1::2] = irfft(even), irfft(odd)
    return result


def circle_forward(x):
    parts = [rfft(x[a::3]) for a in range(3)]
    result = [None] * 25
    half, root = 0.5, math.sqrt(3.0) / 2.0
    for k in range(9):
        t0 = parts[0][k]
        t1, t2 = c_turn(parts[1][k], -k, 48), c_turn(parts[2][k], -2 * k, 48)
        total, gap = c_add(t1, t2), c_sub(t1, t2)
        result[k] = c_add(t0, total)
        mid = (t0[0] - half * total[0], None if t0[1] is None and total[1] is None else
               (t0[1] if total[1] is None else (0.0 if t0[1] is None else t0[1]) - half * total[1]))
        turn = (None if gap[1] is None else root * gap[1], -root * gap[0])
        plus_re = mid[0] if turn[0] is None else mid[0] + turn[0]
        plus_im = turn[1] if mid[1] is None else mid[1] + turn[1]
        minus_re = mid[0] if turn[0] is None else mid[0] - turn[0]
        minus_im = -turn[1] if mid[1] is None else mid[1] - turn[1]
        if k + 16 <= 24:
            result[k + 16] = (plus_re, plus_im)
        if k > 0 and 16 - k != k + 16 and result[16 - k] is None:
            result[16 - k] = (minus_re, -minus_im)
    return result


def circle_backward(z):
    half, root = 0.5, math.sqrt(3.0) / 2.0
    spectra = [[], [], []]
    for k in range(9):
        t0 = z[k]
        t1 = z[k + 16] if k + 16 <= 24 else c_conj(z[32 - k])
        t2 = c_conj(z[16 - k])
        total, gap = c_add(t1, t2), c_sub(t1, t2)
        if k == 0:
            total, gap = (2.0 * t1[0], None), (None, 2.0 * t1[1])
        spectra[0].append(c_add(t0, total))
        mid = (t0[0] - half * total[0],
               t0[1] if total[1] is None else (-half * total[1] if t0[1] is None else t0[1] - half * total[1]))
        turn = (-root * gap[1], None if gap[0] is None else root * gap[0])
        plus = c_add(mid, turn)
        minus = c_sub(mid, turn)
        spectra[1].append(c_turn(plus, k, 48))
        spectra[2].append(c_turn(minus, 2 * k, 48))
    result = [None] * 48
    for a in range(3):
        result[a::3] = irfft(spectra[a])
    return result


def slabs_of(part):
    lane = lax.broadcasted_iota(jnp.int32, (part.shape[0], 128), 1)
    v0, v1, v2 = part[:, :128], part[:, 128:256], part[:, 256:]
    return (
        v0,
        jnp.where(lane < 8, pltpu.roll(v0, 8, 1), pltpu.roll(v1, 8, 1)),
        jnp.where(lane < 16, pltpu.roll(v1, 16, 1), pltpu.roll(v2, 16, 1)),
    )


def border_kernel(state, merid, borders, last, first, wind, pad, sems):
    fields, rows, cells = state.shape
    copies = [
        pltpu.make_async_copy(state.at[:, rows - 1 :, :], last, sems.at[0]),
        pltpu.make_async_copy(state.at[:, :1, :], first, sems.at[1]),
        pltpu.make_async_copy(merid.at[rows - 1 :, :], wind, sems.at[2]),
    ]
    for copy in copies:
        copy.start()
    pad[...] = jnp.zeros(pad.shape, jnp.float32)
    for copy in copies:
        copy.wait()
    for f in range(fields):
        pad[0, f : f + 1, :cells] = last[f]
        pad[1, f : f + 1, :cells] = first[f]
    pad[0, fields : fields + 1, :cells] = wind[...]
    for place in range(2):
        for a, slab in enumerate(slabs_of(pad[place, :8, :])):
            borders[ROWS * place + 8 * a : ROWS * place + 8 * a + 8, :] = slab


def increment_kernel(
    state_in, zonal_in, merid_in, table, flags_in, counts_in, modes_in,
    chunks_out, own, state, metric, zonal, merid, flags, counts, modes, pad, sems,
):
    fields, rows, cells = state.shape
    wide = 128 * SLABS
    band, sector = lax.axis_index("lat"), lax.axis_index("lon")
    sources = [state_in.at[f] for f in range(fields)]
    targets = [state.at[f] for f in range(fields)]
    sources += [zonal_in, merid_in, table.at[band], flags_in, counts_in, modes_in]
    targets += [zonal, merid, metric, flags, counts, modes]
    copies = [
        pltpu.make_async_copy(source, target, sems.at[i])
        for i, (source, target) in enumerate(zip(sources, targets))
    ]
    for copy in copies:
        copy.start()
    chunks = chunks_out.reshape(rows * CHUNK, 128)
    for f in range(fields + 2):
        pad[f, :, wide - 128 :] = jnp.zeros((rows, 128), jnp.float32)
    for copy in copies:
        copy.wait()
    for f in range(fields):
        pad[f, :, :cells] = state[f]
    pad[fields, :, :cells] = zonal[...]
    pad[fields + 1, :, :cells] = merid[...]
    lane = lax.broadcasted_iota(jnp.int32, (rows, wide), 1)
    row = lax.broadcasted_iota(jnp.int32, (rows, wide), 0)

    def spread(index):
        return jnp.broadcast_to(metric[:, index : index + 1], (rows, wide))

    zonal_factor, merid_factor, face = (spread(i) for i in range(3))
    east_wind = pad[fields]
    last_wind = pltpu.roll(east_wind, 3, 1)
    inner_wind = jnp.where(lane < cells - 1, east_wind, 0.0)
    north_wind = jnp.where(row < rows - 1, pad[fields + 1] * face, 0.0)
    for f in range(fields):
        q = pad[f]
        flux_east = inner_wind * (0.5 * (q + pltpu.roll(q, wide - 1, 1)))
        zonal_diff = flux_east - pltpu.roll(flux_east, 1, 1)
        flux_north = north_wind * (0.5 * (q + pltpu.roll(q, rows - 1, 0)))
        merid_diff = flux_north - pltpu.roll(flux_north, 1, 0)
        part = -zonal_factor * zonal_diff - merid_factor * merid_diff
        part = jnp.where(lane == cells, pltpu.roll(q, cells, 1), part)
        part = jnp.where(lane == cells + 1, pltpu.roll(q, 2, 1), part)
        part = jnp.where(lane == cells + 2, last_wind, part)
        for a, slab in enumerate(slabs_of(part)):
            chunks[pl.ds(fields * a + f, rows, stride=CHUNK), :] = slab
    place = lax.broadcasted_iota(jnp.int32, flags.shape, 0) * 128 + lax.broadcasted_iota(jnp.int32, flags.shape, 1)
    chosen = place == band * rows + sector

    def pick(values):
        picked = jnp.where(chosen, values[...].astype(jnp.float32), 0.0)
        return jnp.sum(jnp.sum(picked, axis=1, keepdims=True), axis=0, keepdims=True)

    flag, count = pick(flags), pick(counts)
    raised = jnp.maximum(count + 1.0 - modes[:8, :], 0.0)
    own[:8, :] = raised / jnp.maximum(count, 1.0) * flag * modes[8:, :]
    mine = jnp.where(row == sector, zonal_factor, 0.0)[:, :256]
    own[8:, :] = jnp.broadcast_to(jnp.sum(mine, axis=0, keepdims=True), (8, 256))


def passing_kernel(chip, passing):
    odd = lax.axis_index("lat") % 2 == 1
    passing[...] = jnp.where(odd, chip[ROWS : 2 * ROWS, :], chip[2 * ROWS : 3 * ROWS, :])


def border_fluxes_kernel(part, borders, chip, passed, metric, chunks_out):
    fields, rows = 6, metric.shape[0]
    inside = lax.broadcasted_iota(jnp.int32, (8, 128), 1) < SLAB

    def spread(row, index):
        return jnp.broadcast_to(metric[row : row + 1, index : index + 1], (8, 128))

    first_factor, last_factor = spread(0, 1), spread(rows - 1, 1)
    first_face, last_face = spread(0, 3), spread(rows - 1, 2)
    odd, has_north = spread(0, 4) > 0.5, spread(0, 5) > 0.5
    chunks = chunks_out.reshape(rows * CHUNK, 128)
    chunks_out[...] = part[...]
    for a in range(SLABS):
        here = slice(8 * a, 8 * a + 8)
        top, bottom = borders[here, :], borders[ROWS + 8 * a : ROWS + 8 * a + 8, :]
        south = jnp.where(odd, chip[here, :], passed[here, :])
        above = chip[3 * ROWS + 8 * a : 3 * ROWS + 8 * a + 8, :]
        north = jnp.where(has_north, jnp.where(odd, passed[here, :], above), 0.0)
        flux = (south[fields : fields + 1, :] * first_face) * (0.5 * (south + bottom))
        flux = jnp.where(inside, first_factor * flux, 0.0)
        place = slice(fields * a, fields * (a + 1))
        chunks[place, :] = chunks[place, :] + flux[:fields]
        flux = (top[fields : fields + 1, :] * last_face) * (0.5 * (top + north))
        flux = jnp.where(inside, last_factor * flux, 0.0)
        place = slice((rows - 1) * CHUNK + fields * a, (rows - 1) * CHUNK + fields * (a + 1))
        chunks[place, :] = chunks[place, :] - flux[:fields]


def split(x):
    high = x.astype(jnp.bfloat16)
    return high, (x - high.astype(jnp.float32)).astype(jnp.bfloat16)


def product(x, high, low, dims):
    def dot(p, q):
        return lax.dot_general(p, q, (dims, ((), ())), preferred_element_type=jnp.float32)

    x_high, x_low = split(x)
    both = dot(jnp.concatenate([x_high, x_low], axis=0), high)
    return both[: x.shape[0]] + (both[x.shape[0] :] + dot(x_high, low))


def filter_kernel(chunks_in, own, high, low, result_out):
    sectors, fields = chunks_in.shape[0], 6
    chunks = chunks_in.reshape(sectors * CHUNK, 128)
    result = result_out.reshape(sectors * CHUNK, 128)
    lane = lax.broadcasted_iota(jnp.int32, (8, 128), 1)
    zonal_factor = own[8:, :128]
    points = [chunks[fields * p : fields * p + 8, :] for p in range(POINTS - 1)]
    points.append(pltpu.roll(chunks[sectors * CHUNK - 8 :, :], 6, 0))
    lasts = [points[3 * s + 2] for s in range(sectors)]
    for s in range(sectors):
        after = (s + 1) % sectors
        flux = pltpu.roll(lasts[s], 125, 1) * (
            0.5 * (pltpu.roll(lasts[s], 126, 1) + pltpu.roll(lasts[after], 127, 1))
        )
        edge = jnp.where(lane == SLAB - 1, zonal_factor * flux, 0.0)
        points[3 * s + 2] = points[3 * s + 2] - edge
        points[3 * after] = points[3 * after] + pltpu.roll(edge, 128 - (SLAB - 1), 1)
    for p in range(POINTS):
        result[fields * p : fields * (p + 1), :] = points[p][:fields]
    spectrum = circle_forward(points)
    spectrum[0] = (spectrum[0][0], spectrum[24][0])
    block = lax.broadcasted_iota(jnp.int32, (64, 256), 0) // 8
    column = lax.broadcasted_iota(jnp.int32, (64, 256), 1) // 32
    back = [None] * 25
    groups = range(GROUPS)
    rows = [
        jnp.concatenate([jnp.concatenate(spectrum[8 * g + i], axis=1) for i in range(8)], axis=0)
        for g in groups
    ]
    modes = [product(rows[g], high[g], low[g], ((1,), (0,))) for g in groups]
    modes = [jnp.where(block == column, modes[g] * own[g : g + 1, :], 0.0) for g in groups]
    rows = [product(modes[g], high[g], low[g], ((1,), (1,))) for g in groups]
    for g in groups:
        for i in range(8):
            part = rows[g][8 * i : 8 * i + 8, :]
            back[8 * g + i] = (part[:, :128], part[:, 128:])
    back[24] = (back[0][1], None)
    back[0] = (back[0][0], None)
    correction = circle_backward(back)
    for p in range(POINTS):
        place = slice(fields * p, fields * (p + 1))
        result[place, :] = result[place, :] - correction[p][:fields]


def final_kernel(chunks_in, state, advanced):
    fields, rows, cells = state.shape
    chunks = chunks_in.reshape(rows * CHUNK, 128)
    lane = lax.broadcasted_iota(jnp.int32, (rows, 128), 1)
    for f in range(fields):
        s0, s1, s2 = (chunks[pl.ds(fields * a + f, rows, stride=CHUNK), :] for a in range(SLABS))
        s1, s2 = pltpu.roll(s1, 120, 1), pltpu.roll(s2, 112, 1)
        advanced[f, :, :128] = state[f, :, :128] + jnp.where(lane < 120, s0, s1)
        advanced[f, :, 128:256] = state[f, :, 128:256] + jnp.where(lane < 112, s1, s2)
        advanced[f, :, 256:] = state[f, :, 256:] + s2[:, : cells - 256]


def floats(*shape):
    return jax.ShapeDtypeStruct(shape, jnp.float32)


def call(kernel, name, outs, mebibytes, args, elsewhere=0, scratch=()):
    vmem = pl.BlockSpec(memory_space=pltpu.VMEM)
    stay = pl.BlockSpec(memory_space=pltpu.HBM)
    fixed = len(args) - elsewhere
    args = args[:fixed] + tuple(
        pltpu.with_memory_space_constraint(arg, pltpu.HBM) for arg in args[fixed:]
    )
    return pl.pallas_call(
        kernel,
        out_shape=[jax.ShapeDtypeStruct(out.shape, out.dtype) for out in outs],
        in_specs=[vmem] * fixed + [stay] * elsewhere,
        out_specs=[vmem] * len(outs),
        scratch_shapes=list(scratch),
        compiler_params=pltpu.CompilerParams(vmem_limit_bytes=mebibytes << 20),
        name=name,
    )(*args)


def body(state, zonal_wind, meridional_wind, filter_flag, mode_count):
    field_count, level_count, lat_cells, lon_cells = state.shape
    item_count = field_count * level_count
    band_total, sectors = lax.axis_size("lat"), lax.axis_size("lon")
    nlat, circle = lat_cells * band_total, lon_cells * sectors
    wide = 128 * SLABS
    fields = state.reshape(item_count, lat_cells, lon_cells)
    zonal, merid = (w.reshape(lat_cells, lon_cells) for w in (zonal_wind, meridional_wind))
    high, low, reduced, scale = mode_layout(circle, circle // 16)

    modes = np.concatenate([np.pad(rows, ((0, 8 - GROUPS), (0, 0))) for rows in (reduced, scale)])
    modes = jnp.asarray(modes.astype(np.float32))
    flags, counts = filter_flag.reshape(-1, 128), mode_count.reshape(-1, 128)
    metric, own = floats(lat_cells, 128), floats(16, 256)
    packed = floats(sectors, CHUNK // 2, 2, 128)
    pad = pltpu.VMEM((8, lat_cells, wide), jnp.float32)
    here = (fields, zonal, merid, jnp.asarray(row_metrics(nlat, band_total)), flags, counts, modes)
    line = pltpu.VMEM((item_count, 1, lon_cells), jnp.float32)
    (borders,) = call(
        border_kernel,
        "borders",
        [floats(2 * ROWS, 128)],
        2,
        (fields, merid),
        2,
        [line, line, pltpu.VMEM((1, lon_cells), jnp.float32), pltpu.VMEM((3, 8, wide), jnp.float32)]
        + [pltpu.SemaphoreType.DMA((3,))],
    )
    cores = [[i, i + 1] for i in range(0, band_total, 2)]
    chip = lax.all_gather(borders, "lat", axis=0, tiled=True, axis_index_groups=cores)
    (passing,) = call(passing_kernel, "passing", [floats(ROWS, 128)], 2, (chip,))
    ring = [(i, i + 2) for i in range(0, band_total - 2, 2)] + [(band_total - 2, band_total - 1)]
    ring += [(i, i - 2) for i in range(3, band_total, 2)] + [(1, 0)]
    passed = lax.ppermute(passing, "lat", ring)
    part, own, fields, metric = call(
        increment_kernel,
        "increments",
        [packed, own, fields, metric],
        4,
        here,
        7,
        [pltpu.VMEM(x.shape, x.dtype) for x in (zonal, merid, flags, counts, modes)]
        + [pad, pltpu.SemaphoreType.DMA((item_count + 6,))],
    )
    (chunks,) = call(
        border_fluxes_kernel, "border_fluxes", [packed], 4, (part, borders, chip, passed, metric)
    )
    chunks = lax.all_to_all(chunks, "lon", 0, 0, tiled=True)
    (chunks,) = call(
        filter_kernel,
        "filter_rows",
        [packed],
        8,
        (chunks, own, jnp.asarray(high), jnp.asarray(low)),
    )
    chunks = lax.all_to_all(chunks, "lon", 0, 0, tiled=True)
    (advanced,) = call(final_kernel, "advance", [fields], 4, (chunks, fields))
    return advanced.reshape(state.shape)


def solution(mesh):
    placed = (P(None, None, "lat", "lon"), P(None, "lat", "lon"), P(None, "lat", "lon"), P(), P())
    return jax.shard_map(
        body, mesh=mesh, in_specs=placed, out_specs=P(None, None, "lat", "lon"), check_vma=False
    )
```

```python
import math

import jax
import jax.numpy as jnp
import ml_dtypes
import numpy as np
from jax import lax
from jax.experimental import pallas as pl
from jax.experimental.pallas import tpu as pltpu
from jax.sharding import PartitionSpec as P

meridional_scale = 0.25
SLABS = 3
SLAB = 120
POINTS = 48
ROWS = 8 * SLABS
CHUNK = 6 * SLABS
GROUPS = 3


def mode_layout(circle, kmax):
    table = np.zeros((GROUPS, 256, 256), np.float64)
    reduced = np.full((GROUPS, 256), 1 << 20, np.int32)
    scale = np.zeros((GROUPS, 256), np.float64)
    b = np.arange(SLAB)
    sign = np.where(b % 2 == 0, 1.0, -1.0)
    for residue in range(POINTS // 2):
        group, place = divmod(residue, 8)
        if residue == 0:
            waves = [(48 * n, 0) for n in range(1, 8)] + [(24 + 48 * n, 128) for n in range(8)]
            factor = 2.0 / circle
        else:
            waves = [(residue + 48 * n, None) for n in range(-8, 8) if abs(residue + 48 * n) <= kmax]
            factor = 1.0 / circle
        for t, (k, row) in enumerate(waves):
            angle = 2.0 * np.pi * ((k * b) % circle) / circle
            cosine, sine = sign * np.cos(angle), sign * np.sin(angle)
            re, im = 32 * place + t, 32 * place + 16 + t
            if row is None:
                table[group, :SLAB, re], table[group, 128 : 128 + SLAB, re] = cosine, sine
                table[group, :SLAB, im], table[group, 128 : 128 + SLAB, im] = -sine, cosine
            else:
                table[group, row : row + SLAB, re] = cosine
                table[group, row : row + SLAB, im] = -sine
            reduced[group, [re, im]] = abs(k)
            scale[group, [re, im]] = factor
    high = table.astype(np.float32).astype(ml_dtypes.bfloat16)
    low = (table - high.astype(np.float64)).astype(np.float32).astype(ml_dtypes.bfloat16)
    return high, low, reduced, scale.astype(np.float32)


def row_metrics(nlat, bands):
    ids = np.arange(nlat, dtype=np.float32)
    step = np.float32(math.pi / nlat)
    center = (ids + np.float32(0.5)) * step - np.float32(math.pi / 2)
    center = np.cos(center.astype(np.float64)).astype(np.float32)
    result = np.zeros((nlat, 128), np.float32)
    result[:, 0] = np.float32(math.sin(math.pi / (2 * nlat))) / center
    result[:, 1] = np.float32(meridional_scale) / center
    result[:, 2] = np.sin(((ids + np.float32(1.0)) * step).astype(np.float64))
    result[:, 3] = np.sin((ids * step).astype(np.float64))
    result[:, 4] = np.arange(nlat) // (nlat // bands) % 2
    result[:, 5] = np.arange(nlat) // (nlat // bands) < bands - 1
    return result.reshape(bands, nlat // bands, 128)


def c_add(x, y):
    return (x[0] + y[0], y[1] if x[1] is None else x[1] if y[1] is None else x[1] + y[1])


def c_sub(x, y):
    if y[1] is None:
        return (x[0] - y[0], x[1])
    return (x[0] - y[0], -y[1] if x[1] is None else x[1] - y[1])


def c_conj(x):
    return (x[0], None if x[1] is None else -x[1])


def c_turn(x, numer, denom):
    numer %= denom
    eighth = 8 * numer
    if numer == 0:
        return x
    if 2 * numer == denom:
        return (-x[0], None if x[1] is None else -x[1])
    if 4 * numer == denom:
        return (jnp.zeros_like(x[0]) if x[1] is None else -x[1], x[0])
    if 4 * numer == 3 * denom:
        return (jnp.zeros_like(x[0]) if x[1] is None else x[1], -x[0])
    angle = 2.0 * math.pi * numer / denom
    c, s = math.cos(angle), math.sin(angle)
    if x[1] is None:
        return (x[0] * c, x[0] * s)
    if eighth in (denom, 3 * denom, 5 * denom, 7 * denom):
        h = math.sqrt(0.5)
        a, b = (x[0] - x[1]) * h, (x[0] + x[1]) * h
        return {1: (a, b), 3: (-b, a), 5: (-a, -b), 7: (b, -a)}[eighth // denom]
    return (x[0] * c - x[1] * s, x[0] * s + x[1] * c)


def rfft(x):
    count = len(x)
    if count == 1:
        return [(x[0], None)]
    if count == 2:
        return [(x[0] + x[1], None), (x[0] - x[1], None)]
    even, odd = rfft(x[0::2]), rfft(x[1::2])
    result = [None] * (count // 2 + 1)
    for k in range(count // 4 + 1):
        turned = c_turn(odd[k], -k, count)
        result[k] = c_add(even[k], turned)
        if k != count // 4 or count == 2:
            result[count // 2 - k] = c_conj(c_sub(even[k], turned))
    return result


def irfft(z):
    count = 2 * (len(z) - 1)
    if count == 2:
        return [z[0][0] + z[1][0], z[0][0] - z[1][0]]
    even, odd = [], []
    for k in range(count // 4 + 1):
        mirror = c_conj(z[count // 2 - k])
        even.append(c_add(z[k], mirror))
        odd.append(c_turn(c_sub(z[k], mirror), k, count))
    result = [None] * count
    result[0::2], result[1::2] = irfft(even), irfft(odd)
    return result


def circle_forward(x):
    parts = [rfft(x[a::3]) for a in range(3)]
    result = [None] * 25
    half, root = 0.5, math.sqrt(3.0) / 2.0
    for k in range(9):
        t0 = parts[0][k]
        t1, t2 = c_turn(parts[1][k], -k, 48), c_turn(parts[2][k], -2 * k, 48)
        total, gap = c_add(t1, t2), c_sub(t1, t2)
        result[k] = c_add(t0, total)
        mid = (t0[0] - half * total[0], None if t0[1] is None and total[1] is None else
               (t0[1] if total[1] is None else (0.0 if t0[1] is None else t0[1]) - half * total[1]))
        turn = (None if gap[1] is None else root * gap[1], -root * gap[0])
        plus_re = mid[0] if turn[0] is None else mid[0] + turn[0]
        plus_im = turn[1] if mid[1] is None else mid[1] + turn[1]
        minus_re = mid[0] if turn[0] is None else mid[0] - turn[0]
        minus_im = -turn[1] if mid[1] is None else mid[1] - turn[1]
        if k + 16 <= 24:
            result[k + 16] = (plus_re, plus_im)
        if k > 0 and 16 - k != k + 16 and result[16 - k] is None:
            result[16 - k] = (minus_re, -minus_im)
    return result


def circle_backward(z):
    half, root = 0.5, math.sqrt(3.0) / 2.0
    spectra = [[], [], []]
    for k in range(9):
        t0 = z[k]
        t1 = z[k + 16] if k + 16 <= 24 else c_conj(z[32 - k])
        t2 = c_conj(z[16 - k])
        total, gap = c_add(t1, t2), c_sub(t1, t2)
        if k == 0:
            total, gap = (2.0 * t1[0], None), (None, 2.0 * t1[1])
        spectra[0].append(c_add(t0, total))
        mid = (t0[0] - half * total[0],
               t0[1] if total[1] is None else (-half * total[1] if t0[1] is None else t0[1] - half * total[1]))
        turn = (-root * gap[1], None if gap[0] is None else root * gap[0])
        plus = c_add(mid, turn)
        minus = c_sub(mid, turn)
        spectra[1].append(c_turn(plus, k, 48))
        spectra[2].append(c_turn(minus, 2 * k, 48))
    result = [None] * 48
    for a in range(3):
        result[a::3] = irfft(spectra[a])
    return result


def slabs_of(part):
    lane = lax.broadcasted_iota(jnp.int32, (part.shape[0], 128), 1)
    v0, v1, v2 = part[:, :128], part[:, 128:256], part[:, 256:]
    return (
        v0,
        jnp.where(lane < 8, pltpu.roll(v0, 8, 1), pltpu.roll(v1, 8, 1)),
        jnp.where(lane < 16, pltpu.roll(v1, 16, 1), pltpu.roll(v2, 16, 1)),
    )


def border_kernel(state, merid, borders, last, first, wind, pad, sems):
    fields, rows, cells = state.shape
    copies = [
        pltpu.make_async_copy(state.at[:, rows - 1 :, :], last, sems.at[0]),
        pltpu.make_async_copy(state.at[:, :1, :], first, sems.at[1]),
        pltpu.make_async_copy(merid.at[rows - 1 :, :], wind, sems.at[2]),
    ]
    for copy in copies:
        copy.start()
    pad[...] = jnp.zeros(pad.shape, jnp.float32)
    for copy in copies:
        copy.wait()
    for f in range(fields):
        pad[0, f : f + 1, :cells] = last[f]
        pad[1, f : f + 1, :cells] = first[f]
    pad[0, fields : fields + 1, :cells] = wind[...]
    for place in range(2):
        for a, slab in enumerate(slabs_of(pad[place, :8, :])):
            borders[ROWS * place + 8 * a : ROWS * place + 8 * a + 8, :] = slab


def increment_kernel(
    state_in, zonal_in, merid_in, table, flags_in, counts_in, modes_in, waves_in,
    chunks_out, own, state, metric, waves, zonal, merid, flags, counts, modes, pad, sems,
):
    fields, rows, cells = state.shape
    wide = 128 * SLABS
    band, sector = lax.axis_index("lat"), lax.axis_index("lon")
    sources = [state_in.at[f] for f in range(fields)]
    targets = [state.at[f] for f in range(fields)]
    sources += [zonal_in, merid_in, table.at[band], flags_in, counts_in, modes_in, waves_in]
    targets += [zonal, merid, metric, flags, counts, modes, waves]
    copies = [
        pltpu.make_async_copy(source, target, sems.at[i])
        for i, (source, target) in enumerate(zip(sources, targets))
    ]
    for copy in copies:
        copy.start()
    chunks = chunks_out.reshape(rows * CHUNK, 128)
    for f in range(fields + 2):
        pad[f, :, wide - 128 :] = jnp.zeros((rows, 128), jnp.float32)
    for copy in copies[:-1]:
        copy.wait()
    for f in range(fields):
        pad[f, :, :cells] = state[f]
    pad[fields, :, :cells] = zonal[...]
    pad[fields + 1, :, :cells] = merid[...]
    lane = lax.broadcasted_iota(jnp.int32, (rows, wide), 1)
    row = lax.broadcasted_iota(jnp.int32, (rows, wide), 0)

    def spread(index):
        return jnp.broadcast_to(metric[:, index : index + 1], (rows, wide))

    zonal_factor, merid_factor, face = (spread(i) for i in range(3))
    east_wind = pad[fields]
    last_wind = pltpu.roll(east_wind, 3, 1)
    inner_wind = jnp.where(lane < cells - 1, east_wind, 0.0)
    north_wind = jnp.where(row < rows - 1, pad[fields + 1] * face, 0.0)
    for f in range(fields):
        q = pad[f]
        flux_east = inner_wind * (0.5 * (q + pltpu.roll(q, wide - 1, 1)))
        zonal_diff = flux_east - pltpu.roll(flux_east, 1, 1)
        flux_north = north_wind * (0.5 * (q + pltpu.roll(q, rows - 1, 0)))
        merid_diff = flux_north - pltpu.roll(flux_north, 1, 0)
        part = -zonal_factor * zonal_diff - merid_factor * merid_diff
        part = jnp.where(lane == cells, pltpu.roll(q, cells, 1), part)
        part = jnp.where(lane == cells + 1, pltpu.roll(q, 2, 1), part)
        part = jnp.where(lane == cells + 2, last_wind, part)
        for a, slab in enumerate(slabs_of(part)):
            chunks[pl.ds(fields * a + f, rows, stride=CHUNK), :] = slab
    place = lax.broadcasted_iota(jnp.int32, flags.shape, 0) * 128 + lax.broadcasted_iota(jnp.int32, flags.shape, 1)
    chosen = place == band * rows + sector

    def pick(values):
        picked = jnp.where(chosen, values[...].astype(jnp.float32), 0.0)
        return jnp.sum(jnp.sum(picked, axis=1, keepdims=True), axis=0, keepdims=True)

    flag, count = pick(flags), pick(counts)
    raised = jnp.maximum(count + 1.0 - modes[:8, :], 0.0)
    own[:8, :] = raised / jnp.maximum(count, 1.0) * flag * modes[8:, :]
    mine = jnp.where(row == sector, zonal_factor, 0.0)[:, :256]
    own[8:, :] = jnp.broadcast_to(jnp.sum(mine, axis=0, keepdims=True), (8, 256))
    copies[-1].wait()


def passing_kernel(chip, passing):
    odd = lax.axis_index("lat") % 2 == 1
    passing[...] = jnp.where(odd, chip[ROWS : 2 * ROWS, :], chip[2 * ROWS : 3 * ROWS, :])


def border_fluxes_kernel(part, borders, chip, passed, metric, chunks_out):
    fields, rows = 6, metric.shape[0]
    inside = lax.broadcasted_iota(jnp.int32, (8, 128), 1) < SLAB

    def spread(row, index):
        return jnp.broadcast_to(metric[row : row + 1, index : index + 1], (8, 128))

    first_factor, last_factor = spread(0, 1), spread(rows - 1, 1)
    first_face, last_face = spread(0, 3), spread(rows - 1, 2)
    odd, has_north = spread(0, 4) > 0.5, spread(0, 5) > 0.5
    chunks = chunks_out.reshape(rows * CHUNK, 128)
    chunks_out[...] = part[...]
    for a in range(SLABS):
        here = slice(8 * a, 8 * a + 8)
        top, bottom = borders[here, :], borders[ROWS + 8 * a : ROWS + 8 * a + 8, :]
        south = jnp.where(odd, chip[here, :], passed[here, :])
        above = chip[3 * ROWS + 8 * a : 3 * ROWS + 8 * a + 8, :]
        north = jnp.where(has_north, jnp.where(odd, passed[here, :], above), 0.0)
        flux = (south[fields : fields + 1, :] * first_face) * (0.5 * (south + bottom))
        flux = jnp.where(inside, first_factor * flux, 0.0)
        place = slice(fields * a, fields * (a + 1))
        chunks[place, :] = chunks[place, :] + flux[:fields]
        flux = (top[fields : fields + 1, :] * last_face) * (0.5 * (top + north))
        flux = jnp.where(inside, last_factor * flux, 0.0)
        place = slice((rows - 1) * CHUNK + fields * a, (rows - 1) * CHUNK + fields * (a + 1))
        chunks[place, :] = chunks[place, :] - flux[:fields]


def split(x):
    high = x.astype(jnp.bfloat16)
    return high, (x - high.astype(jnp.float32)).astype(jnp.bfloat16)


def product(x, high, low):
    x_high, x_low = split(x)
    both = jnp.dot(jnp.concatenate([x_high, x_low], axis=0), high, preferred_element_type=jnp.float32)
    rest = jnp.dot(x_high, low, preferred_element_type=jnp.float32)
    return both[: x.shape[0]] + (both[x.shape[0] :] + rest)


def filter_kernel(chunks_in, own, waves, result_out):
    sectors, fields = chunks_in.shape[0], 6
    chunks = chunks_in.reshape(sectors * CHUNK, 128)
    result = result_out.reshape(sectors * CHUNK, 128)
    lane = lax.broadcasted_iota(jnp.int32, (8, 128), 1)
    zonal_factor = own[8:, :128]
    points = [chunks[fields * p : fields * p + 8, :] for p in range(POINTS - 1)]
    points.append(pltpu.roll(chunks[sectors * CHUNK - 8 :, :], 6, 0))
    lasts = [points[3 * s + 2] for s in range(sectors)]
    for s in range(sectors):
        after = (s + 1) % sectors
        flux = pltpu.roll(lasts[s], 125, 1) * (
            0.5 * (pltpu.roll(lasts[s], 126, 1) + pltpu.roll(lasts[after], 127, 1))
        )
        edge = jnp.where(lane == SLAB - 1, zonal_factor * flux, 0.0)
        points[3 * s + 2] = points[3 * s + 2] - edge
        points[3 * after] = points[3 * after] + pltpu.roll(edge, 128 - (SLAB - 1), 1)
    for p in range(POINTS):
        result[fields * p : fields * (p + 1), :] = points[p][:fields]
    spectrum = circle_forward(points)
    spectrum[0] = (spectrum[0][0], spectrum[24][0])
    block = lax.broadcasted_iota(jnp.int32, (64, 256), 0) // 8
    column = lax.broadcasted_iota(jnp.int32, (64, 256), 1) // 32
    back = [None] * 25
    groups = range(GROUPS)
    rows = [
        jnp.concatenate([jnp.concatenate(spectrum[8 * g + i], axis=1) for i in range(8)], axis=0)
        for g in groups
    ]
    modes = [product(rows[g], waves[g], waves[3 + g]) for g in groups]
    modes = [jnp.where(block == column, modes[g] * own[g : g + 1, :], 0.0) for g in groups]
    rows = [product(modes[g], waves[6 + g], waves[9 + g]) for g in groups]
    for g in groups:
        for i in range(8):
            part = rows[g][8 * i : 8 * i + 8, :]
            back[8 * g + i] = (part[:, :128], part[:, 128:])
    back[24] = (back[0][1], None)
    back[0] = (back[0][0], None)
    correction = circle_backward(back)
    for p in range(POINTS):
        place = slice(fields * p, fields * (p + 1))
        result[place, :] = result[place, :] - correction[p][:fields]


def final_kernel(chunks_in, state, advanced):
    fields, rows, cells = state.shape
    chunks = chunks_in.reshape(rows * CHUNK, 128)
    lane = lax.broadcasted_iota(jnp.int32, (rows, 128), 1)
    for f in range(fields):
        s0, s1, s2 = (chunks[pl.ds(fields * a + f, rows, stride=CHUNK), :] for a in range(SLABS))
        s1, s2 = pltpu.roll(s1, 120, 1), pltpu.roll(s2, 112, 1)
        advanced[f, :, :128] = state[f, :, :128] + jnp.where(lane < 120, s0, s1)
        advanced[f, :, 128:256] = state[f, :, 128:256] + jnp.where(lane < 112, s1, s2)
        advanced[f, :, 256:] = state[f, :, 256:] + s2[:, : cells - 256]


def floats(*shape):
    return jax.ShapeDtypeStruct(shape, jnp.float32)


def call(kernel, name, outs, mebibytes, args, elsewhere=0, scratch=()):
    vmem = pl.BlockSpec(memory_space=pltpu.VMEM)
    stay = pl.BlockSpec(memory_space=pltpu.HBM)
    fixed = len(args) - elsewhere
    args = args[:fixed] + tuple(
        pltpu.with_memory_space_constraint(arg, pltpu.HBM) for arg in args[fixed:]
    )
    return pl.pallas_call(
        kernel,
        out_shape=[jax.ShapeDtypeStruct(out.shape, out.dtype) for out in outs],
        in_specs=[vmem] * fixed + [stay] * elsewhere,
        out_specs=[vmem] * len(outs),
        scratch_shapes=list(scratch),
        compiler_params=pltpu.CompilerParams(vmem_limit_bytes=mebibytes << 20),
        name=name,
    )(*args)


def body(state, zonal_wind, meridional_wind, filter_flag, mode_count):
    field_count, level_count, lat_cells, lon_cells = state.shape
    item_count = field_count * level_count
    band_total, sectors = lax.axis_size("lat"), lax.axis_size("lon")
    nlat, circle = lat_cells * band_total, lon_cells * sectors
    wide = 128 * SLABS
    fields = state.reshape(item_count, lat_cells, lon_cells)
    zonal, merid = (w.reshape(lat_cells, lon_cells) for w in (zonal_wind, meridional_wind))
    high, low, reduced, scale = mode_layout(circle, circle // 16)
    waves = [high, low, high.transpose(0, 2, 1), low.transpose(0, 2, 1)]
    waves = jnp.asarray(np.concatenate(waves))

    modes = np.concatenate([np.pad(rows, ((0, 8 - GROUPS), (0, 0))) for rows in (reduced, scale)])
    modes = jnp.asarray(modes.astype(np.float32))
    flags, counts = filter_flag.reshape(-1, 128), mode_count.reshape(-1, 128)
    metric, own = floats(lat_cells, 128), floats(16, 256)
    packed = floats(sectors, CHUNK // 2, 2, 128)
    pad = pltpu.VMEM((8, lat_cells, wide), jnp.float32)
    here = (fields, zonal, merid, jnp.asarray(row_metrics(nlat, band_total)), flags, counts, modes)
    line = pltpu.VMEM((item_count, 1, lon_cells), jnp.float32)
    (borders,) = call(
        border_kernel,
        "borders",
        [floats(2 * ROWS, 128)],
        2,
        (fields, merid),
        2,
        [line, line, pltpu.VMEM((1, lon_cells), jnp.float32), pltpu.VMEM((3, 8, wide), jnp.float32)]
        + [pltpu.SemaphoreType.DMA((3,))],
    )
    cores = [[i, i + 1] for i in range(0, band_total, 2)]
    chip = lax.all_gather(borders, "lat", axis=0, tiled=True, axis_index_groups=cores)
    (passing,) = call(passing_kernel, "passing", [floats(ROWS, 128)], 2, (chip,))
    ring = [(i, i + 2) for i in range(0, band_total - 2, 2)] + [(band_total - 2, band_total - 1)]
    ring += [(i, i - 2) for i in range(3, band_total, 2)] + [(1, 0)]
    passed = lax.ppermute(passing, "lat", ring)
    part, own, fields, metric, waves = call(
        increment_kernel,
        "increments",
        [packed, own, fields, metric, waves],
        6,
        (*here, waves),
        8,
        [pltpu.VMEM(x.shape, x.dtype) for x in (zonal, merid, flags, counts, modes)]
        + [pad, pltpu.SemaphoreType.DMA((item_count + 7,))],
    )
    (chunks,) = call(
        border_fluxes_kernel, "border_fluxes", [packed], 4, (part, borders, chip, passed, metric)
    )
    chunks = lax.all_to_all(chunks, "lon", 0, 0, tiled=True)
    (chunks,) = call(
        filter_kernel,
        "filter_rows",
        [packed],
        8,
        (chunks, own, waves),
    )
    chunks = lax.all_to_all(chunks, "lon", 0, 0, tiled=True)
    (advanced,) = call(final_kernel, "advance", [fields], 4, (chunks, fields))
    return advanced.reshape(state.shape)


def solution(mesh):
    placed = (P(None, None, "lat", "lon"), P(None, "lat", "lon"), P(None, "lat", "lon"), P(), P())
    return jax.shard_map(
        body, mesh=mesh, in_specs=placed, out_specs=P(None, None, "lat", "lon"), check_vma=False
    )
```

```python
import math

import jax
import jax.numpy as jnp
import ml_dtypes
import numpy as np
from jax import lax
from jax.experimental import pallas as pl
from jax.experimental.pallas import tpu as pltpu
from jax.sharding import PartitionSpec as P

meridional_scale = 0.25
SLABS = 3
SLAB = 120
POINTS = 48
ROWS = 8 * SLABS
CHUNK = 6 * SLABS
GROUPS = 3


def mode_layout(circle, kmax):
    table = np.zeros((GROUPS, 256, 256), np.float64)
    reduced = np.full((GROUPS, 256), 1 << 20, np.int32)
    scale = np.zeros((GROUPS, 256), np.float64)
    b = np.arange(SLAB)
    sign = np.where(b % 2 == 0, 1.0, -1.0)
    for residue in range(POINTS // 2):
        group, place = divmod(residue, 8)
        if residue == 0:
            waves = [(48 * n, 0) for n in range(1, 8)] + [(24 + 48 * n, 128) for n in range(8)]
            factor = 2.0 / circle
        else:
            waves = [(residue + 48 * n, None) for n in range(-8, 8) if abs(residue + 48 * n) <= kmax]
            factor = 1.0 / circle
        for t, (k, row) in enumerate(waves):
            angle = 2.0 * np.pi * ((k * b) % circle) / circle
            cosine, sine = sign * np.cos(angle), sign * np.sin(angle)
            re, im = 32 * place + t, 32 * place + 16 + t
            if row is None:
                table[group, :SLAB, re], table[group, 128 : 128 + SLAB, re] = cosine, sine
                table[group, :SLAB, im], table[group, 128 : 128 + SLAB, im] = -sine, cosine
            else:
                table[group, row : row + SLAB, re] = cosine
                table[group, row : row + SLAB, im] = -sine
            reduced[group, [re, im]] = abs(k)
            scale[group, [re, im]] = factor
    high = table.astype(np.float32).astype(ml_dtypes.bfloat16)
    low = (table - high.astype(np.float64)).astype(np.float32).astype(ml_dtypes.bfloat16)
    return high, low, reduced, scale.astype(np.float32)


def row_metrics(nlat, bands):
    ids = np.arange(nlat, dtype=np.float32)
    step = np.float32(math.pi / nlat)
    center = (ids + np.float32(0.5)) * step - np.float32(math.pi / 2)
    center = np.cos(center.astype(np.float64)).astype(np.float32)
    result = np.zeros((nlat, 128), np.float32)
    result[:, 0] = np.float32(math.sin(math.pi / (2 * nlat))) / center
    result[:, 1] = np.float32(meridional_scale) / center
    result[:, 2] = np.sin(((ids + np.float32(1.0)) * step).astype(np.float64))
    result[:, 3] = np.sin((ids * step).astype(np.float64))
    result[:, 4] = np.arange(nlat) // (nlat // bands) % 2
    result[:, 5] = np.arange(nlat) // (nlat // bands) < bands - 1
    return result.reshape(bands, nlat // bands, 128)


def c_add(x, y):
    return (x[0] + y[0], y[1] if x[1] is None else x[1] if y[1] is None else x[1] + y[1])


def c_sub(x, y):
    if y[1] is None:
        return (x[0] - y[0], x[1])
    return (x[0] - y[0], -y[1] if x[1] is None else x[1] - y[1])


def c_conj(x):
    return (x[0], None if x[1] is None else -x[1])


def c_turn(x, numer, denom):
    numer %= denom
    eighth = 8 * numer
    if numer == 0:
        return x
    if 2 * numer == denom:
        return (-x[0], None if x[1] is None else -x[1])
    if 4 * numer == denom:
        return (jnp.zeros_like(x[0]) if x[1] is None else -x[1], x[0])
    if 4 * numer == 3 * denom:
        return (jnp.zeros_like(x[0]) if x[1] is None else x[1], -x[0])
    angle = 2.0 * math.pi * numer / denom
    c, s = math.cos(angle), math.sin(angle)
    if x[1] is None:
        return (x[0] * c, x[0] * s)
    if eighth in (denom, 3 * denom, 5 * denom, 7 * denom):
        h = math.sqrt(0.5)
        a, b = (x[0] - x[1]) * h, (x[0] + x[1]) * h
        return {1: (a, b), 3: (-b, a), 5: (-a, -b), 7: (b, -a)}[eighth // denom]
    return (x[0] * c - x[1] * s, x[0] * s + x[1] * c)


def rfft(x):
    count = len(x)
    if count == 1:
        return [(x[0], None)]
    if count == 2:
        return [(x[0] + x[1], None), (x[0] - x[1], None)]
    even, odd = rfft(x[0::2]), rfft(x[1::2])
    result = [None] * (count // 2 + 1)
    for k in range(count // 4 + 1):
        turned = c_turn(odd[k], -k, count)
        result[k] = c_add(even[k], turned)
        if k != count // 4 or count == 2:
            result[count // 2 - k] = c_conj(c_sub(even[k], turned))
    return result


def irfft(z):
    count = 2 * (len(z) - 1)
    if count == 2:
        return [z[0][0] + z[1][0], z[0][0] - z[1][0]]
    even, odd = [], []
    for k in range(count // 4 + 1):
        mirror = c_conj(z[count // 2 - k])
        even.append(c_add(z[k], mirror))
        odd.append(c_turn(c_sub(z[k], mirror), k, count))
    result = [None] * count
    result[0::2], result[1::2] = irfft(even), irfft(odd)
    return result


def circle_forward(x):
    parts = [rfft(x[a::3]) for a in range(3)]
    result = [None] * 25
    half, root = 0.5, math.sqrt(3.0) / 2.0
    for k in range(9):
        t0 = parts[0][k]
        t1, t2 = c_turn(parts[1][k], -k, 48), c_turn(parts[2][k], -2 * k, 48)
        total, gap = c_add(t1, t2), c_sub(t1, t2)
        result[k] = c_add(t0, total)
        mid = (t0[0] - half * total[0], None if t0[1] is None and total[1] is None else
               (t0[1] if total[1] is None else (0.0 if t0[1] is None else t0[1]) - half * total[1]))
        turn = (None if gap[1] is None else root * gap[1], -root * gap[0])
        plus_re = mid[0] if turn[0] is None else mid[0] + turn[0]
        plus_im = turn[1] if mid[1] is None else mid[1] + turn[1]
        minus_re = mid[0] if turn[0] is None else mid[0] - turn[0]
        minus_im = -turn[1] if mid[1] is None else mid[1] - turn[1]
        if k + 16 <= 24:
            result[k + 16] = (plus_re, plus_im)
        if k > 0 and 16 - k != k + 16 and result[16 - k] is None:
            result[16 - k] = (minus_re, -minus_im)
    return result


def circle_backward(z):
    half, root = 0.5, math.sqrt(3.0) / 2.0
    spectra = [[], [], []]
    for k in range(9):
        t0 = z[k]
        t1 = z[k + 16] if k + 16 <= 24 else c_conj(z[32 - k])
        t2 = c_conj(z[16 - k])
        total, gap = c_add(t1, t2), c_sub(t1, t2)
        if k == 0:
            total, gap = (2.0 * t1[0], None), (None, 2.0 * t1[1])
        spectra[0].append(c_add(t0, total))
        mid = (t0[0] - half * total[0],
               t0[1] if total[1] is None else (-half * total[1] if t0[1] is None else t0[1] - half * total[1]))
        turn = (-root * gap[1], None if gap[0] is None else root * gap[0])
        plus = c_add(mid, turn)
        minus = c_sub(mid, turn)
        spectra[1].append(c_turn(plus, k, 48))
        spectra[2].append(c_turn(minus, 2 * k, 48))
    result = [None] * 48
    for a in range(3):
        result[a::3] = irfft(spectra[a])
    return result


def slabs_of(part):
    lane = lax.broadcasted_iota(jnp.int32, (part.shape[0], 128), 1)
    v0, v1, v2 = part[:, :128], part[:, 128:256], part[:, 256:]
    return (
        v0,
        jnp.where(lane < 8, pltpu.roll(v0, 8, 1), pltpu.roll(v1, 8, 1)),
        jnp.where(lane < 16, pltpu.roll(v1, 16, 1), pltpu.roll(v2, 16, 1)),
    )


def border_kernel(state, merid, borders, last, first, wind, pad, sems):
    fields, rows, cells = state.shape
    copies = [
        pltpu.make_async_copy(state.at[:, rows - 1 :, :], last, sems.at[0]),
        pltpu.make_async_copy(state.at[:, :1, :], first, sems.at[1]),
        pltpu.make_async_copy(merid.at[rows - 1 :, :], wind, sems.at[2]),
    ]
    for copy in copies:
        copy.start()
    pad[...] = jnp.zeros(pad.shape, jnp.float32)
    for copy in copies:
        copy.wait()
    for f in range(fields):
        pad[0, f : f + 1, :cells] = last[f]
        pad[1, f : f + 1, :cells] = first[f]
    pad[0, fields : fields + 1, :cells] = wind[...]
    for place in range(2):
        for a, slab in enumerate(slabs_of(pad[place, :8, :])):
            borders[ROWS * place + 8 * a : ROWS * place + 8 * a + 8, :] = slab


def increment_kernel(
    state_in, zonal_in, merid_in, table, flags_in, counts_in, modes_in, waves_in,
    chunks_out, own, state, metric, waves, zonal, merid, flags, counts, modes, pad, sems,
):
    fields, rows, cells = state.shape
    wide = 128 * SLABS
    band, sector = lax.axis_index("lat"), lax.axis_index("lon")
    sources = [state_in.at[f] for f in range(fields)]
    targets = [state.at[f] for f in range(fields)]
    sources += [zonal_in, merid_in, table.at[band], flags_in, counts_in, modes_in, waves_in]
    targets += [zonal, merid, metric, flags, counts, modes, waves]
    copies = [
        pltpu.make_async_copy(source, target, sems.at[i])
        for i, (source, target) in enumerate(zip(sources, targets))
    ]
    for copy in copies:
        copy.start()
    chunks = chunks_out.reshape(rows * CHUNK, 128)
    for f in range(fields + 2):
        pad[f, :, wide - 128 :] = jnp.zeros((rows, 128), jnp.float32)
    for copy in copies[:-1]:
        copy.wait()
    for f in range(fields):
        pad[f, :, :cells] = state[f]
    pad[fields, :, :cells] = zonal[...]
    pad[fields + 1, :, :cells] = merid[...]
    lane = lax.broadcasted_iota(jnp.int32, (rows, wide), 1)
    row = lax.broadcasted_iota(jnp.int32, (rows, wide), 0)

    def spread(index):
        return jnp.broadcast_to(metric[:, index : index + 1], (rows, wide))

    zonal_factor, merid_factor, face = (spread(i) for i in range(3))
    east_wind = pad[fields]
    last_shift = SLAB - (cells - 1 - (wide - 128))
    last_wind = 0.5 * pltpu.roll(east_wind[:, wide - 128 :], last_shift, 1)
    inner_wind = jnp.where(lane < cells - 1, east_wind, 0.0)
    north_wind = jnp.where(row < rows - 1, pad[fields + 1] * face, 0.0)
    for f in range(fields):
        q = pad[f]
        flux_east = inner_wind * (0.5 * (q + pltpu.roll(q, wide - 1, 1)))
        zonal_diff = flux_east - pltpu.roll(flux_east, 1, 1)
        flux_north = north_wind * (0.5 * (q + pltpu.roll(q, rows - 1, 0)))
        merid_diff = flux_north - pltpu.roll(flux_north, 1, 0)
        part = -zonal_factor * zonal_diff - merid_factor * merid_diff
        edges = (last_wind, pltpu.roll(q[:, wide - 128 :], last_shift, 1), pltpu.roll(q[:, :128], SLAB, 1))
        for a, slab in enumerate(slabs_of(part)):
            slab = jnp.where(lane[:, :128] == SLAB, edges[a], slab)
            chunks[pl.ds(fields * a + f, rows, stride=CHUNK), :] = slab
    place = lax.broadcasted_iota(jnp.int32, flags.shape, 0) * 128 + lax.broadcasted_iota(jnp.int32, flags.shape, 1)
    chosen = place == band * rows + sector

    def pick(values):
        picked = jnp.where(chosen, values[...].astype(jnp.float32), 0.0)
        return jnp.sum(jnp.sum(picked, axis=1, keepdims=True), axis=0, keepdims=True)

    flag, count = pick(flags), pick(counts)
    raised = jnp.maximum(count + 1.0 - modes[:8, :], 0.0)
    own[:8, :] = raised / jnp.maximum(count, 1.0) * flag * modes[8:, :]
    mine = jnp.where(row == sector, zonal_factor, 0.0)[:, :256]
    own[8:, :] = jnp.broadcast_to(jnp.sum(mine, axis=0, keepdims=True), (8, 256))
    copies[-1].wait()


def passing_kernel(chip, passing):
    odd = lax.axis_index("lat") % 2 == 1
    passing[...] = jnp.where(odd, chip[ROWS : 2 * ROWS, :], chip[2 * ROWS : 3 * ROWS, :])


def border_fluxes_kernel(part, borders, chip, passed, metric, chunks_out):
    fields, rows = 6, metric.shape[0]
    inside = lax.broadcasted_iota(jnp.int32, (8, 128), 1) < SLAB

    def spread(row, index):
        return jnp.broadcast_to(metric[row : row + 1, index : index + 1], (8, 128))

    first_factor, last_factor = spread(0, 1), spread(rows - 1, 1)
    first_face, last_face = spread(0, 3), spread(rows - 1, 2)
    odd, has_north = spread(0, 4) > 0.5, spread(0, 5) > 0.5
    chunks = chunks_out.reshape(rows * CHUNK, 128)
    chunks_out[...] = part[...]
    for a in range(SLABS):
        here = slice(8 * a, 8 * a + 8)
        top, bottom = borders[here, :], borders[ROWS + 8 * a : ROWS + 8 * a + 8, :]
        south = jnp.where(odd, chip[here, :], passed[here, :])
        above = chip[3 * ROWS + 8 * a : 3 * ROWS + 8 * a + 8, :]
        north = jnp.where(has_north, jnp.where(odd, passed[here, :], above), 0.0)
        flux = (south[fields : fields + 1, :] * first_face) * (0.5 * (south + bottom))
        flux = jnp.where(inside, first_factor * flux, 0.0)
        place = slice(fields * a, fields * (a + 1))
        chunks[place, :] = chunks[place, :] + flux[:fields]
        flux = (top[fields : fields + 1, :] * last_face) * (0.5 * (top + north))
        flux = jnp.where(inside, last_factor * flux, 0.0)
        place = slice((rows - 1) * CHUNK + fields * a, (rows - 1) * CHUNK + fields * (a + 1))
        chunks[place, :] = chunks[place, :] - flux[:fields]


def split(x):
    high = x.astype(jnp.bfloat16)
    return high, (x - high.astype(jnp.float32)).astype(jnp.bfloat16)


def product(x, high, low):
    x_high, x_low = split(x)
    both = jnp.dot(jnp.concatenate([x_high, x_low], axis=0), high, preferred_element_type=jnp.float32)
    rest = jnp.dot(x_high, low, preferred_element_type=jnp.float32)
    return both[: x.shape[0]] + (both[x.shape[0] :] + rest)


def filter_kernel(chunks_in, own, waves, result_out):
    sectors, fields = chunks_in.shape[0], 6
    chunks = chunks_in.reshape(sectors * CHUNK, 128)
    result = result_out.reshape(sectors * CHUNK, 128)
    lane = lax.broadcasted_iota(jnp.int32, (8, 128), 1)
    zonal_factor = own[8:, :128]
    points = [chunks[fields * p : fields * p + 8, :] for p in range(POINTS - 1)]
    points.append(pltpu.roll(chunks[sectors * CHUNK - 8 :, :], 6, 0))
    came = list(points)
    for s in range(sectors):
        after = (s + 1) % sectors
        flux = came[3 * s] * (came[3 * s + 1] + came[3 * after + 2])
        edge = jnp.where(lane == SLAB, zonal_factor * flux, 0.0)
        points[3 * s + 2] = points[3 * s + 2] - pltpu.roll(edge, 127, 1)
        points[3 * after] = points[3 * after] + pltpu.roll(edge, 128 - SLAB, 1)
    for p in range(POINTS):
        result[fields * p : fields * (p + 1), :] = points[p][:fields]
    spectrum = circle_forward(points)
    spectrum[0] = (spectrum[0][0], spectrum[24][0])
    block = lax.broadcasted_iota(jnp.int32, (64, 256), 0) // 8
    column = lax.broadcasted_iota(jnp.int32, (64, 256), 1) // 32
    back = [None] * 25
    groups = range(GROUPS)
    rows = [
        jnp.concatenate([jnp.concatenate(spectrum[8 * g + i], axis=1) for i in range(8)], axis=0)
        for g in groups
    ]
    modes = [product(rows[g], waves[g], waves[3 + g]) for g in groups]
    modes = [jnp.where(block == column, modes[g] * own[g : g + 1, :], 0.0) for g in groups]
    rows = [product(modes[g], waves[6 + g], waves[9 + g]) for g in groups]
    for g in groups:
        for i in range(8):
            part = rows[g][8 * i : 8 * i + 8, :]
            back[8 * g + i] = (part[:, :128], part[:, 128:])
    back[24] = (back[0][1], None)
    back[0] = (back[0][0], None)
    correction = circle_backward(back)
    for p in range(POINTS):
        place = slice(fields * p, fields * (p + 1))
        result[place, :] = result[place, :] - correction[p][:fields]


def final_kernel(chunks_in, state, advanced):
    fields, rows, cells = state.shape
    chunks = chunks_in.reshape(rows * CHUNK, 128)
    lane = lax.broadcasted_iota(jnp.int32, (rows, 128), 1)
    for f in range(fields):
        s0, s1, s2 = (chunks[pl.ds(fields * a + f, rows, stride=CHUNK), :] for a in range(SLABS))
        s1, s2 = pltpu.roll(s1, 120, 1), pltpu.roll(s2, 112, 1)
        advanced[f, :, :128] = state[f, :, :128] + jnp.where(lane < 120, s0, s1)
        advanced[f, :, 128:256] = state[f, :, 128:256] + jnp.where(lane < 112, s1, s2)
        advanced[f, :, 256:] = state[f, :, 256:] + s2[:, : cells - 256]


def floats(*shape):
    return jax.ShapeDtypeStruct(shape, jnp.float32)


def call(kernel, name, outs, mebibytes, args, elsewhere=0, scratch=()):
    vmem = pl.BlockSpec(memory_space=pltpu.VMEM)
    stay = pl.BlockSpec(memory_space=pltpu.HBM)
    fixed = len(args) - elsewhere
    args = args[:fixed] + tuple(
        pltpu.with_memory_space_constraint(arg, pltpu.HBM) for arg in args[fixed:]
    )
    return pl.pallas_call(
        kernel,
        out_shape=[jax.ShapeDtypeStruct(out.shape, out.dtype) for out in outs],
        in_specs=[vmem] * fixed + [stay] * elsewhere,
        out_specs=[vmem] * len(outs),
        scratch_shapes=list(scratch),
        compiler_params=pltpu.CompilerParams(vmem_limit_bytes=mebibytes << 20),
        name=name,
    )(*args)


def body(state, zonal_wind, meridional_wind, filter_flag, mode_count):
    field_count, level_count, lat_cells, lon_cells = state.shape
    item_count = field_count * level_count
    band_total, sectors = lax.axis_size("lat"), lax.axis_size("lon")
    nlat, circle = lat_cells * band_total, lon_cells * sectors
    wide = 128 * SLABS
    fields = state.reshape(item_count, lat_cells, lon_cells)
    zonal, merid = (w.reshape(lat_cells, lon_cells) for w in (zonal_wind, meridional_wind))
    high, low, reduced, scale = mode_layout(circle, circle // 16)
    waves = [high, low, high.transpose(0, 2, 1), low.transpose(0, 2, 1)]
    waves = jnp.asarray(np.concatenate(waves))

    modes = np.concatenate([np.pad(rows, ((0, 8 - GROUPS), (0, 0))) for rows in (reduced, scale)])
    modes = jnp.asarray(modes.astype(np.float32))
    flags, counts = filter_flag.reshape(-1, 128), mode_count.reshape(-1, 128)
    metric, own = floats(lat_cells, 128), floats(16, 256)
    packed = floats(sectors, CHUNK // 2, 2, 128)
    pad = pltpu.VMEM((8, lat_cells, wide), jnp.float32)
    here = (fields, zonal, merid, jnp.asarray(row_metrics(nlat, band_total)), flags, counts, modes)
    line = pltpu.VMEM((item_count, 1, lon_cells), jnp.float32)
    (borders,) = call(
        border_kernel,
        "borders",
        [floats(2 * ROWS, 128)],
        2,
        (fields, merid),
        2,
        [line, line, pltpu.VMEM((1, lon_cells), jnp.float32), pltpu.VMEM((3, 8, wide), jnp.float32)]
        + [pltpu.SemaphoreType.DMA((3,))],
    )
    cores = [[i, i + 1] for i in range(0, band_total, 2)]
    chip = lax.all_gather(borders, "lat", axis=0, tiled=True, axis_index_groups=cores)
    (passing,) = call(passing_kernel, "passing", [floats(ROWS, 128)], 2, (chip,))
    ring = [(i, i + 2) for i in range(0, band_total - 2, 2)] + [(band_total - 2, band_total - 1)]
    ring += [(i, i - 2) for i in range(3, band_total, 2)] + [(1, 0)]
    passed = lax.ppermute(passing, "lat", ring)
    part, own, fields, metric, waves = call(
        increment_kernel,
        "increments",
        [packed, own, fields, metric, waves],
        6,
        (*here, waves),
        8,
        [pltpu.VMEM(x.shape, x.dtype) for x in (zonal, merid, flags, counts, modes)]
        + [pad, pltpu.SemaphoreType.DMA((item_count + 7,))],
    )
    (chunks,) = call(
        border_fluxes_kernel, "border_fluxes", [packed], 4, (part, borders, chip, passed, metric)
    )
    chunks = lax.all_to_all(chunks, "lon", 0, 0, tiled=True)
    (chunks,) = call(
        filter_kernel,
        "filter_rows",
        [packed],
        8,
        (chunks, own, waves),
    )
    chunks = lax.all_to_all(chunks, "lon", 0, 0, tiled=True)
    (advanced,) = call(final_kernel, "advance", [fields], 4, (chunks, fields))
    return advanced.reshape(state.shape)


def solution(mesh):
    placed = (P(None, None, "lat", "lon"), P(None, "lat", "lon"), P(None, "lat", "lon"), P(), P())
    return jax.shard_map(
        body, mesh=mesh, in_specs=placed, out_specs=P(None, None, "lat", "lon"), check_vma=False
    )
```

```python
import math

import jax
import jax.numpy as jnp
import ml_dtypes
import numpy as np
from jax import lax
from jax.experimental import pallas as pl
from jax.experimental.pallas import tpu as pltpu
from jax.sharding import PartitionSpec as P

meridional_scale = 0.25
SLABS = 3
SLAB = 120
POINTS = 48
ROWS = 8 * SLABS
CHUNK = 6 * SLABS
GROUPS = 3


def mode_layout(circle, kmax):
    table = np.zeros((GROUPS, 256, 256), np.float64)
    reduced = np.full((GROUPS, 256), 1 << 20, np.int32)
    scale = np.zeros((GROUPS, 256), np.float64)
    b = np.arange(SLAB)
    sign = np.where(b % 2 == 0, 1.0, -1.0)
    for residue in range(POINTS // 2):
        group, place = divmod(residue, 8)
        if residue == 0:
            waves = [(48 * n, 0) for n in range(1, 8)] + [(24 + 48 * n, 128) for n in range(8)]
            factor = 2.0 / circle
        else:
            waves = [(residue + 48 * n, None) for n in range(-8, 8) if abs(residue + 48 * n) <= kmax]
            factor = 1.0 / circle
        for t, (k, row) in enumerate(waves):
            angle = 2.0 * np.pi * ((k * b) % circle) / circle
            cosine, sine = sign * np.cos(angle), sign * np.sin(angle)
            re, im = 32 * place + t, 32 * place + 16 + t
            if row is None:
                table[group, :SLAB, re], table[group, 128 : 128 + SLAB, re] = cosine, sine
                table[group, :SLAB, im], table[group, 128 : 128 + SLAB, im] = -sine, cosine
            else:
                table[group, row : row + SLAB, re] = cosine
                table[group, row : row + SLAB, im] = -sine
            reduced[group, [re, im]] = abs(k)
            scale[group, [re, im]] = factor
    high = table.astype(np.float32).astype(ml_dtypes.bfloat16)
    low = (table - high.astype(np.float64)).astype(np.float32).astype(ml_dtypes.bfloat16)
    return high, low, reduced, scale.astype(np.float32)


def row_metrics(nlat, bands):
    ids = np.arange(nlat, dtype=np.float32)
    step = np.float32(math.pi / nlat)
    center = (ids + np.float32(0.5)) * step - np.float32(math.pi / 2)
    center = np.cos(center.astype(np.float64)).astype(np.float32)
    result = np.zeros((nlat, 128), np.float32)
    result[:, 0] = np.float32(math.sin(math.pi / (2 * nlat))) / center
    result[:, 1] = np.float32(meridional_scale) / center
    result[:, 2] = np.sin(((ids + np.float32(1.0)) * step).astype(np.float64))
    result[:, 3] = np.sin((ids * step).astype(np.float64))
    result[:, 4] = np.arange(nlat) // (nlat // bands) % 2
    result[:, 5] = np.arange(nlat) // (nlat // bands) < bands - 1
    return result.reshape(bands, nlat // bands, 128)


def c_add(x, y):
    return (x[0] + y[0], y[1] if x[1] is None else x[1] if y[1] is None else x[1] + y[1])


def c_sub(x, y):
    if y[1] is None:
        return (x[0] - y[0], x[1])
    return (x[0] - y[0], -y[1] if x[1] is None else x[1] - y[1])


def c_conj(x):
    return (x[0], None if x[1] is None else -x[1])


def c_turn(x, numer, denom):
    numer %= denom
    eighth = 8 * numer
    if numer == 0:
        return x
    if 2 * numer == denom:
        return (-x[0], None if x[1] is None else -x[1])
    if 4 * numer == denom:
        return (jnp.zeros_like(x[0]) if x[1] is None else -x[1], x[0])
    if 4 * numer == 3 * denom:
        return (jnp.zeros_like(x[0]) if x[1] is None else x[1], -x[0])
    angle = 2.0 * math.pi * numer / denom
    c, s = math.cos(angle), math.sin(angle)
    if x[1] is None:
        return (x[0] * c, x[0] * s)
    if eighth in (denom, 3 * denom, 5 * denom, 7 * denom):
        h = math.sqrt(0.5)
        a, b = (x[0] - x[1]) * h, (x[0] + x[1]) * h
        return {1: (a, b), 3: (-b, a), 5: (-a, -b), 7: (b, -a)}[eighth // denom]
    return (x[0] * c - x[1] * s, x[0] * s + x[1] * c)


def rfft(x):
    count = len(x)
    if count == 1:
        return [(x[0], None)]
    if count == 2:
        return [(x[0] + x[1], None), (x[0] - x[1], None)]
    even, odd = rfft(x[0::2]), rfft(x[1::2])
    result = [None] * (count // 2 + 1)
    for k in range(count // 4 + 1):
        turned = c_turn(odd[k], -k, count)
        result[k] = c_add(even[k], turned)
        if k != count // 4 or count == 2:
            result[count // 2 - k] = c_conj(c_sub(even[k], turned))
    return result


def irfft(z):
    count = 2 * (len(z) - 1)
    if count == 2:
        return [z[0][0] + z[1][0], z[0][0] - z[1][0]]
    even, odd = [], []
    for k in range(count // 4 + 1):
        mirror = c_conj(z[count // 2 - k])
        even.append(c_add(z[k], mirror))
        odd.append(c_turn(c_sub(z[k], mirror), k, count))
    result = [None] * count
    result[0::2], result[1::2] = irfft(even), irfft(odd)
    return result


def circle_forward(x):
    parts = [rfft(x[a::3]) for a in range(3)]
    result = [None] * 25
    half, root = 0.5, math.sqrt(3.0) / 2.0
    for k in range(9):
        t0 = parts[0][k]
        t1, t2 = c_turn(parts[1][k], -k, 48), c_turn(parts[2][k], -2 * k, 48)
        total, gap = c_add(t1, t2), c_sub(t1, t2)
        result[k] = c_add(t0, total)
        mid = (t0[0] - half * total[0], None if t0[1] is None and total[1] is None else
               (t0[1] if total[1] is None else (0.0 if t0[1] is None else t0[1]) - half * total[1]))
        turn = (None if gap[1] is None else root * gap[1], -root * gap[0])
        plus_re = mid[0] if turn[0] is None else mid[0] + turn[0]
        plus_im = turn[1] if mid[1] is None else mid[1] + turn[1]
        minus_re = mid[0] if turn[0] is None else mid[0] - turn[0]
        minus_im = -turn[1] if mid[1] is None else mid[1] - turn[1]
        if k + 16 <= 24:
            result[k + 16] = (plus_re, plus_im)
        if k > 0 and 16 - k != k + 16 and result[16 - k] is None:
            result[16 - k] = (minus_re, -minus_im)
    return result


def circle_backward(z):
    half, root = 0.5, math.sqrt(3.0) / 2.0
    spectra = [[], [], []]
    for k in range(9):
        t0 = z[k]
        t1 = z[k + 16] if k + 16 <= 24 else c_conj(z[32 - k])
        t2 = c_conj(z[16 - k])
        total, gap = c_add(t1, t2), c_sub(t1, t2)
        if k == 0:
            total, gap = (2.0 * t1[0], None), (None, 2.0 * t1[1])
        spectra[0].append(c_add(t0, total))
        mid = (t0[0] - half * total[0],
               t0[1] if total[1] is None else (-half * total[1] if t0[1] is None else t0[1] - half * total[1]))
        turn = (-root * gap[1], None if gap[0] is None else root * gap[0])
        plus = c_add(mid, turn)
        minus = c_sub(mid, turn)
        spectra[1].append(c_turn(plus, k, 48))
        spectra[2].append(c_turn(minus, 2 * k, 48))
    result = [None] * 48
    for a in range(3):
        result[a::3] = irfft(spectra[a])
    return result


def slabs_of(part):
    lane = lax.broadcasted_iota(jnp.int32, (part.shape[0], 128), 1)
    v0, v1, v2 = part[:, :128], part[:, 128:256], part[:, 256:]
    return (
        v0,
        jnp.where(lane < 8, pltpu.roll(v0, 8, 1), pltpu.roll(v1, 8, 1)),
        jnp.where(lane < 16, pltpu.roll(v1, 16, 1), pltpu.roll(v2, 16, 1)),
    )


def border_kernel(state, merid, borders, last, first, wind, pad, sems):
    fields, rows, cells = state.shape
    copies = [
        pltpu.make_async_copy(state.at[:, rows - 1 :, :], last, sems.at[0]),
        pltpu.make_async_copy(state.at[:, :1, :], first, sems.at[1]),
        pltpu.make_async_copy(merid.at[rows - 1 :, :], wind, sems.at[2]),
    ]
    for copy in copies:
        copy.start()
    pad[...] = jnp.zeros(pad.shape, jnp.float32)
    for copy in copies:
        copy.wait()
    for f in range(fields):
        pad[0, f : f + 1, :cells] = last[f]
        pad[1, f : f + 1, :cells] = first[f]
    pad[0, fields : fields + 1, :cells] = wind[...]
    for place in range(2):
        for a, slab in enumerate(slabs_of(pad[place, :8, :])):
            borders[ROWS * place + 8 * a : ROWS * place + 8 * a + 8, :] = slab


def increment_kernel(
    state_in, zonal_in, merid_in, table, flags_in, counts_in, modes_in, waves_in,
    chunks_out, own, state, metric, waves, zonal, merid, flags, counts, modes, pad, sems,
):
    fields, rows, cells = state.shape
    wide = 128 * SLABS
    band, sector = lax.axis_index("lat"), lax.axis_index("lon")
    sources = [state_in.at[f] for f in range(fields)]
    targets = [state.at[f] for f in range(fields)]
    sources += [zonal_in, merid_in, table.at[band], flags_in, counts_in, modes_in, waves_in]
    targets += [zonal, merid, metric, flags, counts, modes, waves]
    copies = [
        pltpu.make_async_copy(source, target, sems.at[i])
        for i, (source, target) in enumerate(zip(sources, targets))
    ]
    for copy in copies:
        copy.start()
    chunks = chunks_out.reshape(rows * CHUNK, 128)
    for f in range(fields + 2):
        pad[f, :, wide - 128 :] = jnp.zeros((rows, 128), jnp.float32)
    for copy in copies[:-1]:
        copy.wait()
    for f in range(fields):
        pad[f, :, :cells] = state[f]
    pad[fields, :, :cells] = zonal[...]
    pad[fields + 1, :, :cells] = merid[...]
    lane = lax.broadcasted_iota(jnp.int32, (rows, wide), 1)
    row = lax.broadcasted_iota(jnp.int32, (rows, wide), 0)

    def spread(index):
        return jnp.broadcast_to(metric[:, index : index + 1], (rows, wide))

    zonal_factor, merid_factor, face = (spread(i) for i in range(3))
    east_wind = pad[fields]
    last_shift = SLAB - (cells - 1 - (wide - 128))
    last_wind = 0.5 * pltpu.roll(east_wind[:, wide - 128 :], last_shift, 1)
    inner_wind = jnp.where(lane < cells - 1, east_wind, 0.0)
    north_wind = jnp.where(row < rows - 1, pad[fields + 1] * face, 0.0)
    for f in range(fields):
        q = pad[f]
        flux_east = inner_wind * (0.5 * (q + pltpu.roll(q, wide - 1, 1)))
        zonal_diff = flux_east - pltpu.roll(flux_east, 1, 1)
        flux_north = north_wind * (0.5 * (q + pltpu.roll(q, rows - 1, 0)))
        merid_diff = flux_north - pltpu.roll(flux_north, 1, 0)
        part = -zonal_factor * zonal_diff - merid_factor * merid_diff
        edges = (last_wind, pltpu.roll(q[:, wide - 128 :], last_shift, 1), pltpu.roll(q[:, :128], SLAB, 1))
        for a, slab in enumerate(slabs_of(part)):
            slab = jnp.where(lane[:, :128] == SLAB, edges[a], slab)
            chunks[pl.ds(fields * a + f, rows, stride=CHUNK), :] = slab
    place = lax.broadcasted_iota(jnp.int32, flags.shape, 0) * 128 + lax.broadcasted_iota(jnp.int32, flags.shape, 1)
    chosen = place == band * rows + sector

    def pick(values):
        picked = jnp.where(chosen, values[...].astype(jnp.float32), 0.0)
        return jnp.sum(jnp.sum(picked, axis=1, keepdims=True), axis=0, keepdims=True)

    flag, count = pick(flags), pick(counts)
    raised = jnp.maximum(count + 1.0 - modes[:8, :], 0.0)
    own[:8, :] = raised / jnp.maximum(count, 1.0) * flag * modes[8:, :]
    mine = jnp.where(row == sector, zonal_factor, 0.0)[:, :256]
    own[8:, :] = jnp.broadcast_to(jnp.sum(mine, axis=0, keepdims=True), (8, 256))
    copies[-1].wait()


def passing_kernel(chip, passing):
    odd = lax.axis_index("lat") % 2 == 1
    passing[...] = jnp.where(odd, chip[ROWS : 2 * ROWS, :], chip[2 * ROWS : 3 * ROWS, :])


def border_fluxes_kernel(part, borders, chip, passed, metric, chunks_out):
    fields, rows = 6, metric.shape[0]
    inside = lax.broadcasted_iota(jnp.int32, (8, 128), 1) < SLAB

    def spread(row, index):
        return jnp.broadcast_to(metric[row : row + 1, index : index + 1], (8, 128))

    first_factor, last_factor = spread(0, 1), spread(rows - 1, 1)
    first_face, last_face = spread(0, 3), spread(rows - 1, 2)
    odd, has_north = spread(0, 4) > 0.5, spread(0, 5) > 0.5
    chunks = chunks_out.reshape(rows * CHUNK, 128)
    chunks_out[...] = part[...]
    for a in range(SLABS):
        here = slice(8 * a, 8 * a + 8)
        top, bottom = borders[here, :], borders[ROWS + 8 * a : ROWS + 8 * a + 8, :]
        south = jnp.where(odd, chip[here, :], passed[here, :])
        above = chip[3 * ROWS + 8 * a : 3 * ROWS + 8 * a + 8, :]
        north = jnp.where(has_north, jnp.where(odd, passed[here, :], above), 0.0)
        flux = (south[fields : fields + 1, :] * first_face) * (0.5 * (south + bottom))
        flux = jnp.where(inside, first_factor * flux, 0.0)
        place = slice(fields * a, fields * (a + 1))
        chunks[place, :] = chunks[place, :] + flux[:fields]
        flux = (top[fields : fields + 1, :] * last_face) * (0.5 * (top + north))
        flux = jnp.where(inside, last_factor * flux, 0.0)
        place = slice((rows - 1) * CHUNK + fields * a, (rows - 1) * CHUNK + fields * (a + 1))
        chunks[place, :] = chunks[place, :] - flux[:fields]


def split(x):
    high = x.astype(jnp.bfloat16)
    return high, (x - high.astype(jnp.float32)).astype(jnp.bfloat16)


def product(x, high, low):
    x_high, x_low = split(x)
    both = jnp.dot(jnp.concatenate([x_high, x_low], axis=0), high, preferred_element_type=jnp.float32)
    rest = jnp.dot(x_high, low, preferred_element_type=jnp.float32)
    return both[: x.shape[0]] + (both[x.shape[0] :] + rest)


def filter_kernel(chunks_in, own, waves, high, low, result_out):
    sectors, fields = chunks_in.shape[0], 6
    chunks = chunks_in.reshape(sectors * CHUNK, 128)
    result = result_out.reshape(sectors * CHUNK, 128)
    lane = lax.broadcasted_iota(jnp.int32, (8, 128), 1)
    zonal_factor = own[8:, :128]
    points = [chunks[fields * p : fields * p + 8, :] for p in range(POINTS - 1)]
    points.append(pltpu.roll(chunks[sectors * CHUNK - 8 :, :], 6, 0))
    came = list(points)
    for s in range(sectors):
        after = (s + 1) % sectors
        flux = came[3 * s] * (came[3 * s + 1] + came[3 * after + 2])
        edge = jnp.where(lane == SLAB, zonal_factor * flux, 0.0)
        points[3 * s + 2] = points[3 * s + 2] - pltpu.roll(edge, 127, 1)
        points[3 * after] = points[3 * after] + pltpu.roll(edge, 128 - SLAB, 1)
    for p in range(POINTS):
        result[fields * p : fields * (p + 1), :] = points[p][:fields]
    spectrum = circle_forward(points)
    spectrum[0] = (spectrum[0][0], spectrum[24][0])
    block = lax.broadcasted_iota(jnp.int32, (64, 256), 0) // 8
    column = lax.broadcasted_iota(jnp.int32, (64, 256), 1) // 32
    back = [None] * 25
    groups = range(GROUPS)
    rows = [
        jnp.concatenate([jnp.concatenate(spectrum[8 * g + i], axis=1) for i in range(8)], axis=0)
        for g in groups
    ]
    modes = [product(rows[g], high[g], low[g]) for g in groups]
    modes = [jnp.where(block == column, modes[g] * own[g : g + 1, :], 0.0) for g in groups]
    rows = [product(modes[g], waves[g], waves[3 + g]) for g in groups]
    for g in groups:
        for i in range(8):
            part = rows[g][8 * i : 8 * i + 8, :]
            back[8 * g + i] = (part[:, :128], part[:, 128:])
    back[24] = (back[0][1], None)
    back[0] = (back[0][0], None)
    correction = circle_backward(back)
    for p in range(POINTS):
        place = slice(fields * p, fields * (p + 1))
        result[place, :] = result[place, :] - correction[p][:fields]


def final_kernel(chunks_in, state, advanced):
    fields, rows, cells = state.shape
    chunks = chunks_in.reshape(rows * CHUNK, 128)
    lane = lax.broadcasted_iota(jnp.int32, (rows, 128), 1)
    for f in range(fields):
        s0, s1, s2 = (chunks[pl.ds(fields * a + f, rows, stride=CHUNK), :] for a in range(SLABS))
        s1, s2 = pltpu.roll(s1, 120, 1), pltpu.roll(s2, 112, 1)
        advanced[f, :, :128] = state[f, :, :128] + jnp.where(lane < 120, s0, s1)
        advanced[f, :, 128:256] = state[f, :, 128:256] + jnp.where(lane < 112, s1, s2)
        advanced[f, :, 256:] = state[f, :, 256:] + s2[:, : cells - 256]


def floats(*shape):
    return jax.ShapeDtypeStruct(shape, jnp.float32)


def call(kernel, name, outs, mebibytes, args, elsewhere=0, scratch=()):
    vmem = pl.BlockSpec(memory_space=pltpu.VMEM)
    stay = pl.BlockSpec(memory_space=pltpu.HBM)
    fixed = len(args) - elsewhere
    args = args[:fixed] + tuple(
        pltpu.with_memory_space_constraint(arg, pltpu.HBM) for arg in args[fixed:]
    )
    return pl.pallas_call(
        kernel,
        out_shape=[jax.ShapeDtypeStruct(out.shape, out.dtype) for out in outs],
        in_specs=[vmem] * fixed + [stay] * elsewhere,
        out_specs=[vmem] * len(outs),
        scratch_shapes=list(scratch),
        compiler_params=pltpu.CompilerParams(vmem_limit_bytes=mebibytes << 20),
        name=name,
    )(*args)


def body(state, zonal_wind, meridional_wind, filter_flag, mode_count):
    field_count, level_count, lat_cells, lon_cells = state.shape
    item_count = field_count * level_count
    band_total, sectors = lax.axis_size("lat"), lax.axis_size("lon")
    nlat, circle = lat_cells * band_total, lon_cells * sectors
    wide = 128 * SLABS
    fields = state.reshape(item_count, lat_cells, lon_cells)
    zonal, merid = (w.reshape(lat_cells, lon_cells) for w in (zonal_wind, meridional_wind))
    high, low, reduced, scale = mode_layout(circle, circle // 16)
    waves = [high.transpose(0, 2, 1), low.transpose(0, 2, 1)]
    waves = jnp.asarray(np.concatenate(waves))

    modes = np.concatenate([np.pad(rows, ((0, 8 - GROUPS), (0, 0))) for rows in (reduced, scale)])
    modes = jnp.asarray(modes.astype(np.float32))
    flags, counts = filter_flag.reshape(-1, 128), mode_count.reshape(-1, 128)
    metric, own = floats(lat_cells, 128), floats(16, 256)
    packed = floats(sectors, CHUNK // 2, 2, 128)
    pad = pltpu.VMEM((8, lat_cells, wide), jnp.float32)
    here = (fields, zonal, merid, jnp.asarray(row_metrics(nlat, band_total)), flags, counts, modes)
    line = pltpu.VMEM((item_count, 1, lon_cells), jnp.float32)
    (borders,) = call(
        border_kernel,
        "borders",
        [floats(2 * ROWS, 128)],
        2,
        (fields, merid),
        2,
        [line, line, pltpu.VMEM((1, lon_cells), jnp.float32), pltpu.VMEM((3, 8, wide), jnp.float32)]
        + [pltpu.SemaphoreType.DMA((3,))],
    )
    cores = [[i, i + 1] for i in range(0, band_total, 2)]
    chip = lax.all_gather(borders, "lat", axis=0, tiled=True, axis_index_groups=cores)
    (passing,) = call(passing_kernel, "passing", [floats(ROWS, 128)], 2, (chip,))
    ring = [(i, i + 2) for i in range(0, band_total - 2, 2)] + [(band_total - 2, band_total - 1)]
    ring += [(i, i - 2) for i in range(3, band_total, 2)] + [(1, 0)]
    passed = lax.ppermute(passing, "lat", ring)
    part, own, fields, metric, waves = call(
        increment_kernel,
        "increments",
        [packed, own, fields, metric, waves],
        6,
        (*here, waves),
        8,
        [pltpu.VMEM(x.shape, x.dtype) for x in (zonal, merid, flags, counts, modes)]
        + [pad, pltpu.SemaphoreType.DMA((item_count + 7,))],
    )
    (chunks,) = call(
        border_fluxes_kernel, "border_fluxes", [packed], 4, (part, borders, chip, passed, metric)
    )
    chunks = lax.all_to_all(chunks, "lon", 0, 0, tiled=True)
    (chunks,) = call(
        filter_kernel,
        "filter_rows",
        [packed],
        8,
        (chunks, own, waves, jnp.asarray(high), jnp.asarray(low)),
    )
    chunks = lax.all_to_all(chunks, "lon", 0, 0, tiled=True)
    (advanced,) = call(final_kernel, "advance", [fields], 4, (chunks, fields))
    return advanced.reshape(state.shape)


def solution(mesh):
    placed = (P(None, None, "lat", "lon"), P(None, "lat", "lon"), P(None, "lat", "lon"), P(), P())
    return jax.shard_map(
        body, mesh=mesh, in_specs=placed, out_specs=P(None, None, "lat", "lon"), check_vma=False
    )
```

```python
import math

import jax
import jax.numpy as jnp
import ml_dtypes
import numpy as np
from jax import lax
from jax.experimental import pallas as pl
from jax.experimental.pallas import tpu as pltpu
from jax.sharding import PartitionSpec as P

meridional_scale = 0.25
SLABS = 3
SLAB = 120
POINTS = 48
ROWS = 8 * SLABS
CHUNK = 6 * SLABS
GROUPS = 3


def mode_layout(circle, kmax):
    table = np.zeros((GROUPS, 256, 256), np.float64)
    reduced = np.full((GROUPS, 256), 1 << 20, np.int32)
    scale = np.zeros((GROUPS, 256), np.float64)
    b = np.arange(SLAB)
    sign = np.where(b % 2 == 0, 1.0, -1.0)
    for residue in range(POINTS // 2):
        group, place = divmod(residue, 8)
        if residue == 0:
            waves = [(48 * n, 0) for n in range(1, 8)] + [(24 + 48 * n, 128) for n in range(8)]
            factor = 2.0 / circle
        else:
            waves = [(residue + 48 * n, None) for n in range(-8, 8) if abs(residue + 48 * n) <= kmax]
            factor = 1.0 / circle
        for t, (k, row) in enumerate(waves):
            angle = 2.0 * np.pi * ((k * b) % circle) / circle
            cosine, sine = sign * np.cos(angle), sign * np.sin(angle)
            re, im = 32 * place + t, 32 * place + 16 + t
            if row is None:
                table[group, :SLAB, re], table[group, 128 : 128 + SLAB, re] = cosine, sine
                table[group, :SLAB, im], table[group, 128 : 128 + SLAB, im] = -sine, cosine
            else:
                table[group, row : row + SLAB, re] = cosine
                table[group, row : row + SLAB, im] = -sine
            reduced[group, [re, im]] = abs(k)
            scale[group, [re, im]] = factor
    high = table.astype(np.float32).astype(ml_dtypes.bfloat16)
    low = (table - high.astype(np.float64)).astype(np.float32).astype(ml_dtypes.bfloat16)
    return high, low, reduced, scale.astype(np.float32)


def row_metrics(nlat, bands):
    ids = np.arange(nlat, dtype=np.float32)
    step = np.float32(math.pi / nlat)
    center = (ids + np.float32(0.5)) * step - np.float32(math.pi / 2)
    center = np.cos(center.astype(np.float64)).astype(np.float32)
    result = np.zeros((nlat, 128), np.float32)
    result[:, 0] = np.float32(math.sin(math.pi / (2 * nlat))) / center
    result[:, 1] = np.float32(meridional_scale) / center
    result[:, 2] = np.sin(((ids + np.float32(1.0)) * step).astype(np.float64))
    result[:, 3] = np.sin((ids * step).astype(np.float64))
    result[:, 4] = np.arange(nlat) // (nlat // bands) % 2
    result[:, 5] = np.arange(nlat) // (nlat // bands) < bands - 1
    return result.reshape(bands, nlat // bands, 128)


def c_add(x, y):
    return (x[0] + y[0], y[1] if x[1] is None else x[1] if y[1] is None else x[1] + y[1])


def c_sub(x, y):
    if y[1] is None:
        return (x[0] - y[0], x[1])
    return (x[0] - y[0], -y[1] if x[1] is None else x[1] - y[1])


def c_conj(x):
    return (x[0], None if x[1] is None else -x[1])


def c_sub_conj(x, y):
    if x[1] is None or y[1] is None:
        return c_conj(c_sub(x, y)) if y[1] is None else (x[0] - y[0], y[1])
    return (x[0] - y[0], y[1] - x[1])


def c_mirror(x, y):
    if x[1] is None or y[1] is None:
        return c_add(x, c_conj(y)), c_sub(x, c_conj(y))
    return (x[0] + y[0], x[1] - y[1]), (x[0] - y[0], x[1] + y[1])


def c_turn(x, numer, denom):
    numer %= denom
    eighth = 8 * numer
    if numer == 0:
        return x
    if 2 * numer == denom:
        return (-x[0], None if x[1] is None else -x[1])
    if 4 * numer == denom:
        return (jnp.zeros_like(x[0]) if x[1] is None else -x[1], x[0])
    if 4 * numer == 3 * denom:
        return (jnp.zeros_like(x[0]) if x[1] is None else x[1], -x[0])
    angle = 2.0 * math.pi * numer / denom
    c, s = math.cos(angle), math.sin(angle)
    if x[1] is None:
        return (x[0] * c, x[0] * s)
    if eighth in (denom, 3 * denom, 5 * denom, 7 * denom):
        h = math.sqrt(0.5)
        a, b = (x[0] - x[1]) * h, (x[0] + x[1]) * h
        return {1: (a, b), 3: (-b, a), 5: (-a, -b), 7: (b, -a)}[eighth // denom]
    return (x[0] * c - x[1] * s, x[0] * s + x[1] * c)


def rfft(x):
    count = len(x)
    if count == 1:
        return [(x[0], None)]
    if count == 2:
        return [(x[0] + x[1], None), (x[0] - x[1], None)]
    even, odd = rfft(x[0::2]), rfft(x[1::2])
    result = [None] * (count // 2 + 1)
    for k in range(count // 4 + 1):
        turned = c_turn(odd[k], -k, count)
        result[k] = c_add(even[k], turned)
        if k != count // 4 or count == 2:
            result[count // 2 - k] = c_sub_conj(even[k], turned)
    return result


def irfft(z):
    count = 2 * (len(z) - 1)
    if count == 2:
        return [z[0][0] + z[1][0], z[0][0] - z[1][0]]
    even, odd = [], []
    for k in range(count // 4 + 1):
        total, gap = c_mirror(z[k], z[count // 2 - k])
        even.append(total)
        odd.append(c_turn(gap, k, count))
    result = [None] * count
    result[0::2], result[1::2] = irfft(even), irfft(odd)
    return result


def circle_forward(x):
    parts = [rfft(x[a::3]) for a in range(3)]
    result = [None] * 25
    half, root = 0.5, math.sqrt(3.0) / 2.0
    for k in range(9):
        t0 = parts[0][k]
        t1, t2 = c_turn(parts[1][k], -k, 48), c_turn(parts[2][k], -2 * k, 48)
        total, gap = c_add(t1, t2), c_sub(t1, t2)
        result[k] = c_add(t0, total)
        mid = (t0[0] - half * total[0], None if t0[1] is None and total[1] is None else
               (t0[1] if total[1] is None else (0.0 if t0[1] is None else t0[1]) - half * total[1]))
        turn = (None if gap[1] is None else root * gap[1], -root * gap[0])
        plus_re = mid[0] if turn[0] is None else mid[0] + turn[0]
        plus_im = turn[1] if mid[1] is None else mid[1] + turn[1]
        minus_re = mid[0] if turn[0] is None else mid[0] - turn[0]
        minus_im = -turn[1] if mid[1] is None else mid[1] - turn[1]
        if k + 16 <= 24:
            result[k + 16] = (plus_re, plus_im)
        if k > 0 and 16 - k != k + 16 and result[16 - k] is None:
            result[16 - k] = (minus_re, -minus_im)
    return result


def circle_backward(z):
    half, root = 0.5, math.sqrt(3.0) / 2.0
    spectra = [[], [], []]
    for k in range(9):
        t0 = z[k]
        t1 = z[k + 16] if k + 16 <= 24 else c_conj(z[32 - k])
        t2 = c_conj(z[16 - k])
        total, gap = c_add(t1, t2), c_sub(t1, t2)
        if k == 0:
            total, gap = (2.0 * t1[0], None), (None, 2.0 * t1[1])
        spectra[0].append(c_add(t0, total))
        mid = (t0[0] - half * total[0],
               t0[1] if total[1] is None else (-half * total[1] if t0[1] is None else t0[1] - half * total[1]))
        turn = (-root * gap[1], None if gap[0] is None else root * gap[0])
        plus = c_add(mid, turn)
        minus = c_sub(mid, turn)
        spectra[1].append(c_turn(plus, k, 48))
        spectra[2].append(c_turn(minus, 2 * k, 48))
    result = [None] * 48
    for a in range(3):
        result[a::3] = irfft(spectra[a])
    return result


def slabs_of(part):
    lane = lax.broadcasted_iota(jnp.int32, (part.shape[0], 128), 1)
    v0, v1, v2 = part[:, :128], part[:, 128:256], part[:, 256:]
    return (
        v0,
        jnp.where(lane < 8, pltpu.roll(v0, 8, 1), pltpu.roll(v1, 8, 1)),
        jnp.where(lane < 16, pltpu.roll(v1, 16, 1), pltpu.roll(v2, 16, 1)),
    )


def border_kernel(state, merid, borders, last, first, wind, pad, sems):
    fields, rows, cells = state.shape
    copies = [
        pltpu.make_async_copy(state.at[:, rows - 1 :, :], last, sems.at[0]),
        pltpu.make_async_copy(state.at[:, :1, :], first, sems.at[1]),
        pltpu.make_async_copy(merid.at[rows - 1 :, :], wind, sems.at[2]),
    ]
    for copy in copies:
        copy.start()
    pad[...] = jnp.zeros(pad.shape, jnp.float32)
    for copy in copies:
        copy.wait()
    for f in range(fields):
        pad[0, f : f + 1, :cells] = last[f]
        pad[1, f : f + 1, :cells] = first[f]
    pad[0, fields : fields + 1, :cells] = wind[...]
    for place in range(2):
        for a, slab in enumerate(slabs_of(pad[place, :8, :])):
            borders[ROWS * place + 8 * a : ROWS * place + 8 * a + 8, :] = slab


def increment_kernel(
    state_in, zonal_in, merid_in, table, flags_in, counts_in, modes_in, waves_in,
    chunks_out, own, state, metric, waves, zonal, merid, flags, counts, modes, pad, sems,
):
    fields, rows, cells = state.shape
    wide = 128 * SLABS
    band, sector = lax.axis_index("lat"), lax.axis_index("lon")
    sources = [state_in.at[f] for f in range(fields)]
    targets = [state.at[f] for f in range(fields)]
    sources += [zonal_in, merid_in, table.at[band], flags_in, counts_in, modes_in, waves_in]
    targets += [zonal, merid, metric, flags, counts, modes, waves]
    copies = [
        pltpu.make_async_copy(source, target, sems.at[i])
        for i, (source, target) in enumerate(zip(sources, targets))
    ]
    for copy in copies:
        copy.start()
    chunks = chunks_out.reshape(rows * CHUNK, 128)
    for f in range(fields + 2):
        pad[f, :, wide - 128 :] = jnp.zeros((rows, 128), jnp.float32)
    for copy in copies[:-1]:
        copy.wait()
    for f in range(fields):
        pad[f, :, :cells] = state[f]
    pad[fields, :, :cells] = zonal[...]
    pad[fields + 1, :, :cells] = merid[...]
    lane = lax.broadcasted_iota(jnp.int32, (rows, wide), 1)
    row = lax.broadcasted_iota(jnp.int32, (rows, wide), 0)

    def spread(index):
        return jnp.broadcast_to(metric[:, index : index + 1], (rows, wide))

    zonal_factor, merid_factor, face = (spread(i) for i in range(3))
    east_wind = pad[fields]
    last_shift = SLAB - (cells - 1 - (wide - 128))
    last_wind = 0.5 * pltpu.roll(east_wind[:, wide - 128 :], last_shift, 1)
    inner_wind = jnp.where(lane < cells - 1, east_wind, 0.0)
    north_wind = jnp.where(row < rows - 1, pad[fields + 1] * face, 0.0)
    for f in range(fields):
        q = pad[f]
        flux_east = inner_wind * (0.5 * (q + pltpu.roll(q, wide - 1, 1)))
        zonal_diff = flux_east - pltpu.roll(flux_east, 1, 1)
        flux_north = north_wind * (0.5 * (q + pltpu.roll(q, rows - 1, 0)))
        merid_diff = flux_north - pltpu.roll(flux_north, 1, 0)
        part = -zonal_factor * zonal_diff - merid_factor * merid_diff
        edges = (last_wind, pltpu.roll(q[:, wide - 128 :], last_shift, 1), pltpu.roll(q[:, :128], SLAB, 1))
        for a, slab in enumerate(slabs_of(part)):
            slab = jnp.where(lane[:, :128] == SLAB, edges[a], slab)
            chunks[pl.ds(fields * a + f, rows, stride=CHUNK), :] = slab
    place = lax.broadcasted_iota(jnp.int32, flags.shape, 0) * 128 + lax.broadcasted_iota(jnp.int32, flags.shape, 1)
    chosen = place == band * rows + sector

    def pick(values):
        picked = jnp.where(chosen, values[...].astype(jnp.float32), 0.0)
        return jnp.sum(jnp.sum(picked, axis=1, keepdims=True), axis=0, keepdims=True)

    flag, count = pick(flags), pick(counts)
    raised = jnp.maximum(count + 1.0 - modes[:8, :], 0.0)
    own[:8, :] = raised / jnp.maximum(count, 1.0) * flag * modes[8:, :]
    mine = jnp.where(row == sector, zonal_factor, 0.0)[:, :256]
    own[8:, :] = jnp.broadcast_to(jnp.sum(mine, axis=0, keepdims=True), (8, 256))
    copies[-1].wait()


def passing_kernel(chip, passing):
    odd = lax.axis_index("lat") % 2 == 1
    passing[...] = jnp.where(odd, chip[ROWS : 2 * ROWS, :], chip[2 * ROWS : 3 * ROWS, :])


def border_fluxes_kernel(part, borders, chip, passed, metric, chunks_out):
    fields, rows = 6, metric.shape[0]
    inside = lax.broadcasted_iota(jnp.int32, (8, 128), 1) < SLAB

    def spread(row, index):
        return jnp.broadcast_to(metric[row : row + 1, index : index + 1], (8, 128))

    first_factor, last_factor = spread(0, 1), spread(rows - 1, 1)
    first_face, last_face = spread(0, 3), spread(rows - 1, 2)
    odd, has_north = spread(0, 4) > 0.5, spread(0, 5) > 0.5
    chunks = chunks_out.reshape(rows * CHUNK, 128)
    chunks_out[...] = part[...]
    for a in range(SLABS):
        here = slice(8 * a, 8 * a + 8)
        top, bottom = borders[here, :], borders[ROWS + 8 * a : ROWS + 8 * a + 8, :]
        south = jnp.where(odd, chip[here, :], passed[here, :])
        above = chip[3 * ROWS + 8 * a : 3 * ROWS + 8 * a + 8, :]
        north = jnp.where(has_north, jnp.where(odd, passed[here, :], above), 0.0)
        flux = (south[fields : fields + 1, :] * first_face) * (0.5 * (south + bottom))
        flux = jnp.where(inside, first_factor * flux, 0.0)
        place = slice(fields * a, fields * (a + 1))
        chunks[place, :] = chunks[place, :] + flux[:fields]
        flux = (top[fields : fields + 1, :] * last_face) * (0.5 * (top + north))
        flux = jnp.where(inside, last_factor * flux, 0.0)
        place = slice((rows - 1) * CHUNK + fields * a, (rows - 1) * CHUNK + fields * (a + 1))
        chunks[place, :] = chunks[place, :] - flux[:fields]


def split(x):
    high = x.astype(jnp.bfloat16)
    return high, (x - high.astype(jnp.float32)).astype(jnp.bfloat16)


def product(x, high, low):
    x_high, x_low = split(x)
    both = jnp.dot(jnp.concatenate([x_high, x_low], axis=0), high, preferred_element_type=jnp.float32)
    rest = jnp.dot(x_high, low, preferred_element_type=jnp.float32)
    return both[: x.shape[0]] + (both[x.shape[0] :] + rest)


def filter_kernel(chunks_in, own, waves, result_out):
    sectors, fields = chunks_in.shape[0], 6
    chunks = chunks_in.reshape(sectors * CHUNK, 128)
    result = result_out.reshape(sectors * CHUNK, 128)
    lane = lax.broadcasted_iota(jnp.int32, (8, 128), 1)
    zonal_factor = own[8:, :128]
    points = [chunks[fields * p : fields * p + 8, :] for p in range(POINTS - 1)]
    points.append(pltpu.roll(chunks[sectors * CHUNK - 8 :, :], 6, 0))
    came = list(points)
    for s in range(sectors):
        after = (s + 1) % sectors
        flux = came[3 * s] * (came[3 * s + 1] + came[3 * after + 2])
        edge = jnp.where(lane == SLAB, zonal_factor * flux, 0.0)
        points[3 * s + 2] = points[3 * s + 2] - pltpu.roll(edge, 127, 1)
        points[3 * after] = points[3 * after] + pltpu.roll(edge, 128 - SLAB, 1)
    for p in range(POINTS):
        result[fields * p : fields * (p + 1), :] = points[p][:fields]
    spectrum = circle_forward(points)
    spectrum[0] = (spectrum[0][0], spectrum[24][0])
    block = lax.broadcasted_iota(jnp.int32, (64, 256), 0) // 8
    column = lax.broadcasted_iota(jnp.int32, (64, 256), 1) // 32
    back = [None] * 25
    groups = range(GROUPS)
    rows = [
        jnp.concatenate([jnp.concatenate(spectrum[8 * g + i], axis=1) for i in range(8)], axis=0)
        for g in groups
    ]
    modes = [product(rows[g], waves[g], waves[3 + g]) for g in groups]
    modes = [jnp.where(block == column, modes[g] * own[g : g + 1, :], 0.0) for g in groups]
    rows = [product(modes[g], waves[6 + g], waves[9 + g]) for g in groups]
    for g in groups:
        for i in range(8):
            part = rows[g][8 * i : 8 * i + 8, :]
            back[8 * g + i] = (part[:, :128], part[:, 128:])
    back[24] = (back[0][1], None)
    back[0] = (back[0][0], None)
    correction = circle_backward(back)
    for p in range(POINTS):
        place = slice(fields * p, fields * (p + 1))
        result[place, :] = result[place, :] - correction[p][:fields]


def final_kernel(chunks_in, state, advanced):
    fields, rows, cells = state.shape
    chunks = chunks_in.reshape(rows * CHUNK, 128)
    lane = lax.broadcasted_iota(jnp.int32, (rows, 128), 1)
    for f in range(fields):
        s0, s1, s2 = (chunks[pl.ds(fields * a + f, rows, stride=CHUNK), :] for a in range(SLABS))
        s1, s2 = pltpu.roll(s1, 120, 1), pltpu.roll(s2, 112, 1)
        advanced[f, :, :128] = state[f, :, :128] + jnp.where(lane < 120, s0, s1)
        advanced[f, :, 128:256] = state[f, :, 128:256] + jnp.where(lane < 112, s1, s2)
        advanced[f, :, 256:] = state[f, :, 256:] + s2[:, : cells - 256]


def floats(*shape):
    return jax.ShapeDtypeStruct(shape, jnp.float32)


def call(kernel, name, outs, mebibytes, args, elsewhere=0, scratch=()):
    vmem = pl.BlockSpec(memory_space=pltpu.VMEM)
    stay = pl.BlockSpec(memory_space=pltpu.HBM)
    fixed = len(args) - elsewhere
    args = args[:fixed] + tuple(
        pltpu.with_memory_space_constraint(arg, pltpu.HBM) for arg in args[fixed:]
    )
    return pl.pallas_call(
        kernel,
        out_shape=[jax.ShapeDtypeStruct(out.shape, out.dtype) for out in outs],
        in_specs=[vmem] * fixed + [stay] * elsewhere,
        out_specs=[vmem] * len(outs),
        scratch_shapes=list(scratch),
        compiler_params=pltpu.CompilerParams(vmem_limit_bytes=mebibytes << 20),
        name=name,
    )(*args)


def body(state, zonal_wind, meridional_wind, filter_flag, mode_count):
    field_count, level_count, lat_cells, lon_cells = state.shape
    item_count = field_count * level_count
    band_total, sectors = lax.axis_size("lat"), lax.axis_size("lon")
    nlat, circle = lat_cells * band_total, lon_cells * sectors
    wide = 128 * SLABS
    fields = state.reshape(item_count, lat_cells, lon_cells)
    zonal, merid = (w.reshape(lat_cells, lon_cells) for w in (zonal_wind, meridional_wind))
    high, low, reduced, scale = mode_layout(circle, circle // 16)
    waves = [high, low, high.transpose(0, 2, 1), low.transpose(0, 2, 1)]
    waves = jnp.asarray(np.concatenate(waves))

    modes = np.concatenate([np.pad(rows, ((0, 8 - GROUPS), (0, 0))) for rows in (reduced, scale)])
    modes = jnp.asarray(modes.astype(np.float32))
    flags, counts = filter_flag.reshape(-1, 128), mode_count.reshape(-1, 128)
    metric, own = floats(lat_cells, 128), floats(16, 256)
    packed = floats(sectors, CHUNK // 2, 2, 128)
    pad = pltpu.VMEM((8, lat_cells, wide), jnp.float32)
    here = (fields, zonal, merid, jnp.asarray(row_metrics(nlat, band_total)), flags, counts, modes)
    line = pltpu.VMEM((item_count, 1, lon_cells), jnp.float32)
    (borders,) = call(
        border_kernel,
        "borders",
        [floats(2 * ROWS, 128)],
        2,
        (fields, merid),
        2,
        [line, line, pltpu.VMEM((1, lon_cells), jnp.float32), pltpu.VMEM((3, 8, wide), jnp.float32)]
        + [pltpu.SemaphoreType.DMA((3,))],
    )
    cores = [[i, i + 1] for i in range(0, band_total, 2)]
    chip = lax.all_gather(borders, "lat", axis=0, tiled=True, axis_index_groups=cores)
    (passing,) = call(passing_kernel, "passing", [floats(ROWS, 128)], 2, (chip,))
    ring = [(i, i + 2) for i in range(0, band_total - 2, 2)] + [(band_total - 2, band_total - 1)]
    ring += [(i, i - 2) for i in range(3, band_total, 2)] + [(1, 0)]
    passed = lax.ppermute(passing, "lat", ring)
    part, own, fields, metric, waves = call(
        increment_kernel,
        "increments",
        [packed, own, fields, metric, waves],
        6,
        (*here, waves),
        8,
        [pltpu.VMEM(x.shape, x.dtype) for x in (zonal, merid, flags, counts, modes)]
        + [pad, pltpu.SemaphoreType.DMA((item_count + 7,))],
    )
    (chunks,) = call(
        border_fluxes_kernel, "border_fluxes", [packed], 4, (part, borders, chip, passed, metric)
    )
    chunks = lax.all_to_all(chunks, "lon", 0, 0, tiled=True)
    (chunks,) = call(
        filter_kernel,
        "filter_rows",
        [packed],
        8,
        (chunks, own, waves),
    )
    chunks = lax.all_to_all(chunks, "lon", 0, 0, tiled=True)
    (advanced,) = call(final_kernel, "advance", [fields], 4, (chunks, fields))
    return advanced.reshape(state.shape)


def solution(mesh):
    placed = (P(None, None, "lat", "lon"), P(None, "lat", "lon"), P(None, "lat", "lon"), P(), P())
    return jax.shard_map(
        body, mesh=mesh, in_specs=placed, out_specs=P(None, None, "lat", "lon"), check_vma=False
    )
```
